32 devices in a mesh: section: 2 (over core), dp: 16 (over z, y, x).
Axes of the slice: x: 2, y: 2, z: 4, core: 2. Of those that a mesh axis runs over, the one named last changes fastest.
Arguments:
- patches: bfloat16 [64, 529, 768], P('dp'), may hold values from -6 to 6
- visible: int32 [64], P('dp'), may hold values from 40 to 529, as said below
- source: int32 [64, 529], P('dp'), may hold values from -1 to 528, as said below
- enc_gains: bfloat16 [3, 768], replicated, may hold values from 0.5 to 1.5
- enc_shifts: bfloat16 [3, 768], replicated, may hold values from -1.25 to 1.25
- enc_qkv: bfloat16 [768, 2304], replicated, may hold values from -0.21875 to 0.21875
- enc_out: bfloat16 [768, 768], replicated, may hold values from -2.5 to 2.5
- enc_bias_out: bfloat16 [2, 768], replicated, may hold values from -1.25 to 1.25
- enc_up: bfloat16 [768, 3072], replicated, may hold values from -0.21875 to 0.21875
- enc_bias_up: bfloat16 [3072], replicated, may hold values from -1.25 to 1.25
- enc_down: bfloat16 [3072, 768], replicated, may hold values from -0.109375 to 0.109375
- enc_proj: bfloat16 [768, 512], replicated, may hold values from -0.21875 to 0.21875
- proj_bias: bfloat16 [512], replicated, may hold values from -1.25 to 1.25
- mask_token: bfloat16 [512], replicated, may hold values from -6 to 6
- dec_gains: bfloat16 [2, 512], replicated, may hold values from 0.5 to 1.5
- dec_shifts: bfloat16 [2, 512], replicated, may hold values from -1.25 to 1.25
- dec_qkv: bfloat16 [512, 1536], replicated, may hold values from -0.25 to 0.25
- dec_out: bfloat16 [512, 512], replicated, may hold values from -3 to 3
- dec_bias_out: bfloat16 [2, 512], replicated, may hold values from -1.25 to 1.25
- dec_up: bfloat16 [512, 2048], replicated, may hold values from -0.25 to 0.25
- dec_bias_up: bfloat16 [2048], replicated, may hold values from -1.25 to 1.25
- dec_down: bfloat16 [2048, 512], replicated, may hold values from -0.125 to 0.125
- cotangent: bfloat16 [64, 529, 512], P('dp'), may hold values from -6 to 6
Outputs:
- decoded: bfloat16 [64, 529, 512], P('dp', None, 'section')
- patch_grad: bfloat16 [64, 529, 768], P('dp', None, 'section')
- grad_enc_gains: float32 [3, 768], P(None, ('section', 'dp'))
- grad_enc_shifts: float32 [3, 768], P(None, ('section', 'dp'))
- grad_enc_qkv: float32 [768, 2304], P(('section', 'dp'))
- grad_enc_out: float32 [768, 768], P(('section', 'dp'))
- grad_enc_bias_out: float32 [2, 768], P(None, ('section', 'dp'))
- grad_enc_up: float32 [768, 3072], P(('section', 'dp'))
- grad_enc_bias_up: float32 [3072], P(('section', 'dp'))
- grad_enc_down: float32 [3072, 768], P(('section', 'dp'))
- grad_enc_proj: float32 [768, 512], P(('section', 'dp'))
- grad_proj_bias: float32 [512], P(('section', 'dp'))
- grad_mask_token: float32 [512], P(('section', 'dp'))
- grad_dec_gains: float32 [2, 512], P(None, ('section', 'dp'))
- grad_dec_shifts: float32 [2, 512], P(None, ('section', 'dp'))
- grad_dec_qkv: float32 [512, 1536], P(('section', 'dp'))
- grad_dec_out: float32 [512, 512], P(('section', 'dp'))
- grad_dec_bias_out: float32 [2, 512], P(None, ('section', 'dp'))
- grad_dec_up: float32 [512, 2048], P(('section', 'dp'))
- grad_dec_bias_up: float32 [2048], P(('section', 'dp'))
- grad_dec_down: float32 [2048, 512], P(('section', 'dp'))
The draws below stay inside these ranges and needn't reach their ends.
Inputs may be any that keep to these rules, and one draw needn't show every extreme that they name: Rows of a strip at and after its count are padding. Some strip has 529 visible patches and some has 40. `source`: the non-negative entries of row i are 0 to visible[i] - 1, each once; all other entries are -1.
All inputs are finite; a program needn't handle non-finite values.
Results may differ from the reference program's by a relative error of at most 0.018.
Values may be sent and summed in bfloat16 or wider, within the bound.
No kernel may reach another device: no remote copies, remote signals or barrier semaphores. Data moves between devices by JAX's collectives and lax.ppermute only.
A program may use at most 576 MiB of HBM per device.

```python
import math
import jax
import jax.numpy as jnp
from jax import lax

D_ENC = 768
HEADS_ENC = 12
FF_ENC = 3072
D_DEC = 512
HEADS_DEC = 16
FF_DEC = 2048
LENGTH = 529
LEAST = 40
STRIPS = 64


def shared_counts(key):
    key_one, key_two, key_three = jax.random.split(key, 3)
    counts = jax.random.randint(key_one, (STRIPS,), LEAST, LENGTH + 1, dtype=jnp.int32)
    fullest = jax.random.randint(key_two, (), 0, STRIPS, dtype=jnp.int32)
    offset = jax.random.randint(key_three, (), 1, STRIPS, dtype=jnp.int32)
    fewest = (fullest + offset) % STRIPS
    places = jnp.arange(STRIPS, dtype=jnp.int32)
    counts = jnp.where(places == fullest, LENGTH, counts)
    return jnp.where(places == fewest, LEAST, counts).astype(jnp.int32)


def shuffled(strip_key):
    return jax.random.permutation(strip_key, LENGTH).astype(jnp.int32)


def draw_visible(key, part):
    counts = shared_counts(key)
    return counts


def draw_source(key, part):
    counts = shared_counts(key)
    key = jax.random.fold_in(key, 5)
    strip_keys = jax.random.split(key, STRIPS)
    orders = jax.vmap(shuffled)(strip_keys)
    return jnp.where(orders < counts[:, None], orders, -1).astype(jnp.int32)


def level_of(stream_key, shape, cuts, smallest, top_value):
    gain, own = 1.0, jax.random.fold_in(stream_key, 6)
    for dim, shards_of in cuts:
        heights = jnp.exp(jax.random.uniform(jax.random.fold_in(own, dim), (shards_of,), jnp.float32, smallest / len(cuts), top_value / len(cuts)))
        gain = gain * jnp.repeat(heights, shape[dim] // shards_of).reshape([-1 if axis == dim else 1 for axis in range(len(shape))])
    return gain


def scatter_about(key, dims, scale, most, cuts=(), kind=jnp.bfloat16):
    array = scale * jax.random.normal(key, dims, jnp.float32)
    if cuts:
        array = array * level_of(key, dims, cuts, -0.22, 0.18)
    return jnp.clip(array, -most, most).astype(kind)


def setup_inputs(seed: int = 0) -> dict:
    splits = jax.random.split(jax.random.key(seed), 24)
    return {
        "patches": scatter_about(splits[0], (STRIPS, LENGTH, D_ENC), 1.0, 6.0, ((0, 16),)),
        "visible": draw_visible(jax.random.fold_in(splits[23], 71), 0),
        "source": draw_source(jax.random.fold_in(splits[23], 71), 0),
        "enc_gains": jnp.clip(1.0 + 0.1 * jax.random.normal(splits[3], (3, D_ENC), jnp.float32), 0.5, 1.5).astype(jnp.bfloat16),
        "enc_shifts": scatter_about(splits[4], (3, D_ENC), 0.2, 1.25),
        "enc_qkv": scatter_about(splits[5], (D_ENC, 3 * D_ENC), D_ENC ** -0.5, 0.21875),
        "enc_out": scatter_about(splits[6], (D_ENC, D_ENC), (max(D_ENC // 128, 1)) ** -0.5, 2.5),
        "enc_bias_out": scatter_about(splits[7], (2, D_ENC), 0.2, 1.25),
        "enc_up": scatter_about(splits[8], (D_ENC, FF_ENC), D_ENC ** -0.5, 0.21875),
        "enc_bias_up": scatter_about(splits[9], (FF_ENC,), 0.2, 1.25),
        "enc_down": scatter_about(splits[10], (FF_ENC, D_ENC), FF_ENC ** -0.5, 0.109375),
        "enc_proj": scatter_about(splits[11], (D_ENC, D_DEC), D_ENC ** -0.5, 0.21875),
        "proj_bias": scatter_about(splits[12], (D_DEC,), 0.2, 1.25),
        "mask_token": scatter_about(splits[13], (D_DEC,), 1.0, 6.0),
        "dec_gains": jnp.clip(1.0 + 0.1 * jax.random.normal(splits[14], (2, D_DEC), jnp.float32), 0.5, 1.5).astype(jnp.bfloat16),
        "dec_shifts": scatter_about(splits[15], (2, D_DEC), 0.2, 1.25),
        "dec_qkv": scatter_about(splits[16], (D_DEC, 3 * D_DEC), D_DEC ** -0.5, 0.25),
        "dec_out": scatter_about(splits[17], (D_DEC, D_DEC), (max(D_DEC // 128, 1)) ** -0.5, 3.0),
        "dec_bias_out": scatter_about(splits[18], (2, D_DEC), 0.2, 1.25),
        "dec_up": scatter_about(splits[19], (D_DEC, FF_DEC), D_DEC ** -0.5, 0.25),
        "dec_bias_up": scatter_about(splits[20], (FF_DEC,), 0.2, 1.25),
        "dec_down": scatter_about(splits[21], (FF_DEC, D_DEC), FF_DEC ** -0.5, 0.125),
        "cotangent": scatter_about(splits[22], (STRIPS, LENGTH, D_DEC), 1.0, 6.0, ((0, 16),)),
    }


highest_precision = lax.Precision.HIGHEST
epsilon = 1e-06

@jax.custom_vjp
def low(v):
    return lax.optimization_barrier(v.astype(jnp.bfloat16)).astype(jnp.float32)

@jax.custom_vjp
def low_back(v):
    return v

def low_keep(v):
    return (low(v), None)

def low_pass(kept, grad):
    return (grad,)

def back_keep(v):
    return (v, None)

def back_low(kept, grad):
    return (low(grad),)
low.defvjp(low_keep, low_pass)
low_back.defvjp(back_keep, back_low)

def matmul(left_side, right_side):
    return jnp.dot(left_side, right_side, precision=highest_precision)

def layer_norm(values, gain_row, shift_row):
    center = values - lax.optimization_barrier(jnp.mean(values, axis=-1, keepdims=True))
    variance = lax.optimization_barrier(jnp.mean(center * center, axis=-1, keepdims=True))
    return center * lax.rsqrt(variance + epsilon) * gain_row + shift_row

def place_table(length_rows, model_width):
    halfway = model_width // 2
    places = jnp.arange(length_rows, dtype=jnp.float32)[:, None]
    rates = jnp.exp(jnp.arange(halfway, dtype=jnp.float32) * (-math.log(10000.0) / halfway))[None, :]
    return jnp.concatenate([jnp.sin(places * rates), jnp.cos(places * rates)], axis=1)

def block(inputs, live_count, gain_rows, shifts, w_qkv, w_out, bias_out, w_up, bias_up, w_down, head_count):
    length, model_width = inputs.shape
    head_size = model_width // head_count
    normed_one = low(layer_norm(inputs, gain_rows[0], shifts[0]))
    packed = low(low_back(matmul(normed_one, w_qkv)))
    queries = packed[:, :model_width].reshape(length, head_count, head_size)
    key_rows = packed[:, model_width:2 * model_width].reshape(length, head_count, head_size)
    value_rows = packed[:, 2 * model_width:].reshape(length, head_count, head_size)
    scores = low_back(jnp.einsum('qhd,khd->hqk', queries, key_rows, precision=highest_precision) * head_size ** (-0.5))
    key_valid = jnp.arange(length, dtype=jnp.int32) < live_count
    scores = jnp.where(key_valid[None, None, :], scores, -1e+30)
    top_score = lax.optimization_barrier(jnp.max(scores, axis=-1, keepdims=True))
    exp_terms = jnp.exp(scores - top_score)
    weights_low = low(exp_terms / lax.optimization_barrier(jnp.sum(exp_terms, axis=-1, keepdims=True)))
    mixed_rows = jnp.einsum('hqk,khd->qhd', weights_low, value_rows, precision=highest_precision)
    mixed_rows = low(low_back(mixed_rows.reshape(length, model_width)))
    middle = inputs + low_back(matmul(mixed_rows, w_out) + bias_out[0])
    normed_two = low(layer_norm(middle, gain_rows[1], shifts[1]))
    hidden = low_back(matmul(normed_two, w_up) + bias_up)
    active = low(jax.nn.gelu(hidden, approximate=False))
    return middle + low_back(matmul(active, w_down) + bias_out[1])

def reference(patches, visible, source, enc_gains, enc_shifts, enc_qkv, enc_out, enc_bias_out, enc_up, enc_bias_up, enc_down, enc_proj, proj_bias, mask_token, dec_gains, dec_shifts, dec_qkv, dec_out, dec_bias_out, dec_up, dec_bias_up, dec_down, cotangent):
    params = tuple((weight.astype(jnp.float32) for weight in (enc_gains, enc_shifts, enc_qkv, enc_out, enc_bias_out, enc_up, enc_bias_up, enc_down, enc_proj, proj_bias, mask_token, dec_gains, dec_shifts, dec_qkv, dec_out, dec_bias_out, dec_up, dec_bias_up, dec_down)))

    def forward(inputs, weight_set):
        e_gains, e_shifts, e_qkv, e_out, e_bias_out, e_up, e_bias_up, e_down, w_proj, bias_proj, mask_row, d_gains, d_shifts, d_qkv, d_out, d_bias_out, d_up, d_bias_up, d_down = weight_set

        def encode_one(element):
            strip_rows, live_count = element
            result = block(strip_rows, live_count, e_gains, e_shifts, e_qkv, e_out, e_bias_out, e_up, e_bias_up, e_down, HEADS_ENC)
            encoded = low(low_back(layer_norm(result, e_gains[2], e_shifts[2])))
            return low(low_back(matmul(encoded, w_proj) + bias_proj))
        projected = lax.map(jax.checkpoint(encode_one), (inputs, visible))
        places = place_table(LENGTH, D_DEC)

        def decode_one(element):
            rows_in, sources = element
            picker = (sources[:, None] == jnp.arange(LENGTH, dtype=jnp.int32)[None, :]).astype(jnp.float32)
            missing = (sources < 0).astype(jnp.float32)[:, None]
            started = matmul(picker, rows_in) + missing * mask_row + places
            return block(started, LENGTH, d_gains, d_shifts, d_qkv, d_out, d_bias_out, d_up, d_bias_up, d_down, HEADS_DEC)
        return lax.map(jax.checkpoint(decode_one), (projected, source))
    decoded, pullback = jax.vjp(forward, patches.astype(jnp.float32), params)
    grad_in, gradients = pullback(cotangent.astype(jnp.float32))
    return (decoded.astype(jnp.bfloat16), grad_in.astype(jnp.bfloat16), gradients[0], gradients[1], gradients[2], gradients[3], gradients[4], gradients[5], gradients[6], gradients[7], gradients[8], gradients[9], gradients[10], gradients[11], gradients[12], gradients[13], gradients[14], gradients[15], gradients[16], gradients[17], gradients[18])
```

```python
import math

import jax
import jax.numpy as jnp
from jax import lax
from jax.sharding import PartitionSpec as P

HEADS_ENC = 12
HEADS_DEC = 16


epsilon = 1e-06


def apply_norm(values, gain_row, shift_row):
    center = values - jnp.mean(values, axis=-1, keepdims=True)
    inverse = lax.rsqrt(jnp.mean(center * center, axis=-1, keepdims=True) + epsilon)
    normed = center * inverse
    return (normed * gain_row + shift_row, normed, inverse)


def norm_grad(grad_out, normed, inverse, gain_row):
    scaled = grad_out * gain_row
    grad_in = inverse * (
        scaled
        - jnp.mean(scaled, axis=-1, keepdims=True)
        - normed * jnp.mean(scaled * normed, axis=-1, keepdims=True)
    )
    return (grad_in, jnp.sum(grad_out * normed, axis=(0, 1)), jnp.sum(grad_out, axis=(0, 1)))


def gelu_exact(values):
    return jax.nn.gelu(values, approximate=False)


def place_table(length_rows, model_width):
    halfway = model_width // 2
    places = jnp.arange(length_rows, dtype=jnp.float32)[:, None]
    rates = jnp.exp(jnp.arange(halfway, dtype=jnp.float32) * (-math.log(10000.0) / halfway))[
        None, :
    ]
    return jnp.concatenate([jnp.sin(places * rates), jnp.cos(places * rates)], axis=1)


def forward_product(left_side, right_side):
    return jnp.einsum("bld,df->blf", left_side, right_side, preferred_element_type=jnp.float32)


def backward_product(left_side, right_side):
    return jnp.einsum("blf,df->bld", left_side, right_side, preferred_element_type=jnp.float32)


def weight_product(left_side, right_side):
    return jnp.einsum("bld,blf->df", left_side, right_side, preferred_element_type=jnp.float32)


def split_heads(packed, head_count):
    batch_size, length, triple = packed.shape
    model_width = triple // 3
    head_size = model_width // head_count
    head_shape = (batch_size, length, head_count, head_size)
    queries = packed[..., :model_width].reshape(head_shape)
    key_rows = packed[..., model_width : 2 * model_width].reshape(head_shape)
    value_rows = packed[..., 2 * model_width :].reshape(head_shape)
    return (queries, key_rows, value_rows, head_size ** (-0.5))


def masked_scores(queries, key_rows, key_valid, factor):
    scores = (
        jnp.einsum("bqhd,bkhd->bhqk", queries, key_rows, preferred_element_type=jnp.float32)
        * factor
    )
    return jnp.where(key_valid[:, None, None, :], scores, -1e30)


def attend(packed, key_valid, head_count):
    queries, key_rows, value_rows, factor = split_heads(packed, head_count)
    scores = masked_scores(queries, key_rows, key_valid, factor)
    highest = jnp.max(scores, axis=-1, keepdims=True)
    exp_terms = jnp.exp(scores - highest)
    totals = jnp.sum(exp_terms, axis=-1, keepdims=True)
    weights_low = (exp_terms / totals).astype(jnp.bfloat16)
    mixed_rows = jnp.einsum(
        "bhqk,bkhd->bqhd", weights_low, value_rows, preferred_element_type=jnp.float32
    )
    mixed_rows = mixed_rows.reshape(packed.shape[0], packed.shape[1], -1).astype(jnp.bfloat16)
    return (mixed_rows, (highest, totals))


def attend_grad(packed, key_valid, head_count, softmax_kept, grad_mixed):
    queries, key_rows, value_rows, factor = split_heads(packed, head_count)
    highest, totals = softmax_kept
    weights_full = jnp.exp(masked_scores(queries, key_rows, key_valid, factor) - highest) / totals
    grad_heads = grad_mixed.reshape(queries.shape)
    grad_weights = jnp.einsum(
        "bqhd,bkhd->bhqk", grad_heads, value_rows, preferred_element_type=jnp.float32
    )
    grad_scores = (
        weights_full * (grad_weights - jnp.sum(weights_full * grad_weights, axis=-1, keepdims=True))
    ).astype(jnp.bfloat16)
    grad_queries = (
        jnp.einsum("bhqk,bkhd->bqhd", grad_scores, key_rows, preferred_element_type=jnp.float32)
        * factor
    )
    grad_keys = (
        jnp.einsum("bhqk,bqhd->bkhd", grad_scores, queries, preferred_element_type=jnp.float32)
        * factor
    )
    grad_values = jnp.einsum(
        "bhqk,bqhd->bkhd",
        weights_full.astype(jnp.bfloat16),
        grad_heads,
        preferred_element_type=jnp.float32,
    )
    flat_shape = (packed.shape[0], packed.shape[1], -1)
    return jnp.concatenate(
        [
            grad_queries.reshape(flat_shape),
            grad_keys.reshape(flat_shape),
            grad_values.reshape(flat_shape),
        ],
        axis=-1,
    ).astype(jnp.bfloat16)


def block_forward(inputs, key_valid, weights, head_count):
    gain_rows, shifts, w_qkv, w_out, bias_out, w_up, bias_up, w_down = weights
    normed_one, unit_one, inverse_one = apply_norm(inputs, gain_rows[0], shifts[0])
    low_one = normed_one.astype(jnp.bfloat16)
    packed = forward_product(low_one, w_qkv).astype(jnp.bfloat16)
    mixed_rows, softmax_kept = attend(packed, key_valid, head_count)
    middle = inputs + forward_product(mixed_rows, w_out) + bias_out[0]
    normed_two, unit_two, inverse_two = apply_norm(middle, gain_rows[1], shifts[1])
    low_two = normed_two.astype(jnp.bfloat16)
    hidden = forward_product(low_two, w_up) + bias_up
    active = gelu_exact(hidden).astype(jnp.bfloat16)
    result = middle + forward_product(active, w_down) + bias_out[1]
    return (
        result,
        (
            unit_one,
            inverse_one,
            low_one,
            packed,
            mixed_rows,
            softmax_kept,
            unit_two,
            inverse_two,
            low_two,
            hidden,
            active,
        ),
    )


def block_backward(grad_result, kept_values, weights, key_valid, head_count):
    gain_rows, shifts, w_qkv, w_out, bias_out, w_up, bias_up, w_down = weights
    (
        unit_one,
        inverse_one,
        low_one,
        packed,
        mixed_rows,
        softmax_kept,
        unit_two,
        inverse_two,
        low_two,
        hidden,
        active,
    ) = kept_values
    grad_low = grad_result.astype(jnp.bfloat16)
    grad_down = weight_product(active, grad_low)
    grad_bias_two = jnp.sum(grad_low.astype(jnp.float32), axis=(0, 1))
    grad_active = backward_product(grad_low, w_down)
    gelu_value, gelu_pull = jax.vjp(gelu_exact, hidden)
    grad_hidden = gelu_pull(grad_active)[0].astype(jnp.bfloat16)
    grad_up = weight_product(low_two, grad_hidden)
    grad_bias_up = jnp.sum(grad_hidden.astype(jnp.float32), axis=(0, 1))
    grad_norm_two = backward_product(grad_hidden, w_up)
    grad_from_two, grad_gain_two, grad_shift_two = norm_grad(
        grad_norm_two, unit_two, inverse_two, gain_rows[1]
    )
    grad_middle = grad_result + grad_from_two
    grad_middle_low = grad_middle.astype(jnp.bfloat16)
    grad_out = weight_product(mixed_rows, grad_middle_low)
    grad_bias_one = jnp.sum(grad_middle_low.astype(jnp.float32), axis=(0, 1))
    grad_mixed = backward_product(grad_middle_low, w_out).astype(jnp.bfloat16)
    grad_packed = attend_grad(packed, key_valid, head_count, softmax_kept, grad_mixed)
    grad_qkv = weight_product(low_one, grad_packed)
    grad_norm_one = backward_product(grad_packed, w_qkv)
    grad_from_one, grad_gain_one, grad_shift_one = norm_grad(
        grad_norm_one, unit_one, inverse_one, gain_rows[0]
    )
    grad_inputs = grad_middle + grad_from_one
    block_grads = (
        jnp.stack([grad_gain_one, grad_gain_two]),
        jnp.stack([grad_shift_one, grad_shift_two]),
        grad_qkv,
        grad_out,
        jnp.stack([grad_bias_one, grad_bias_two]),
        grad_up,
        grad_bias_up,
        grad_down,
    )
    return (grad_inputs, block_grads)


def row_scatter(grad_value):
    rows, width = grad_value.shape
    count = lax.axis_size("section") * lax.axis_size("dp")
    blocks = grad_value.astype(jnp.bfloat16).reshape(count, rows // count, width)
    out = lax.psum_scatter(blocks, ("section", "dp"), scatter_dimension=0, tiled=True)
    return out.reshape(rows // count, width).astype(jnp.float32)


def small_scatter(grad_values, axis_values):
    count = lax.axis_size("section") * lax.axis_size("dp")
    flat = jnp.concatenate(
        [
            jnp.moveaxis(grad_value, axis_dim, 0).reshape(count, -1)
            for grad_value, axis_dim in zip(grad_values, axis_values)
        ],
        axis=1,
    )
    summed = lax.psum_scatter(flat, ("section", "dp"), scatter_dimension=0, tiled=True)[0]
    portions = []
    offset = 0
    for grad_value, axis_dim in zip(grad_values, axis_values):
        shape = jnp.moveaxis(grad_value, axis_dim, 0).shape
        local_shape = (shape[0] // count,) + shape[1:]
        length = math.prod(local_shape)
        portions.append(jnp.moveaxis(summed[offset : offset + length].reshape(local_shape), 0, axis_dim))
        offset += length
    return portions


def local(
    patches,
    visible,
    source,
    enc_gains,
    enc_shifts,
    enc_qkv,
    enc_out,
    enc_bias_out,
    enc_up,
    enc_bias_up,
    enc_down,
    enc_proj,
    proj_bias,
    mask_token,
    dec_gains,
    dec_shifts,
    dec_qkv,
    dec_out,
    dec_bias_out,
    dec_up,
    dec_bias_up,
    dec_down,
    cotangent,
):
    section_index = lax.axis_index("section")
    strip_len = patches.shape[1]
    enc_width = patches.shape[2]
    dec_width = dec_qkv.shape[0]
    mine = patches.shape[0] // 2
    take = lambda array: lax.dynamic_slice_in_dim(array, section_index * mine, mine, 0)
    patches, visible, source, cotangent = map(take, (patches, visible, source, cotangent))
    enc_gain_f = enc_gains.astype(jnp.float32)
    enc_shift_f = enc_shifts.astype(jnp.float32)
    enc_weights = (
        enc_gain_f,
        enc_shift_f,
        enc_qkv,
        enc_out,
        enc_bias_out.astype(jnp.float32),
        enc_up,
        enc_bias_up.astype(jnp.float32),
        enc_down,
    )
    dec_weights = (
        dec_gains.astype(jnp.float32),
        dec_shifts.astype(jnp.float32),
        dec_qkv,
        dec_out,
        dec_bias_out.astype(jnp.float32),
        dec_up,
        dec_bias_up.astype(jnp.float32),
        dec_down,
    )
    bias_proj = proj_bias.astype(jnp.float32)
    mask_row = mask_token.astype(jnp.float32)
    positions = jnp.arange(strip_len, dtype=jnp.int32)
    places = place_table(strip_len, dec_width)
    enc_valid = positions[None, :] < visible[:, None]
    dec_valid = jnp.ones(source.shape, dtype=jnp.bool_)
    enc_in = patches.astype(jnp.float32)
    enc_result, enc_kept = block_forward(enc_in, enc_valid, enc_weights, HEADS_ENC)
    final_normed, final_unit, final_inverse = apply_norm(enc_result, enc_gain_f[2], enc_shift_f[2])
    encoded = final_normed.astype(jnp.bfloat16)
    rows_in = (forward_product(encoded, enc_proj) + bias_proj).astype(jnp.bfloat16)
    picker = (source[:, :, None] == positions[None, None, :]).astype(jnp.bfloat16)
    missing = (source < 0).astype(jnp.float32)[:, :, None]
    dec_in = (
        jnp.einsum("bjr,brc->bjc", picker, rows_in, preferred_element_type=jnp.float32)
        + missing * mask_row
        + places
    )
    dec_result, dec_kept = block_forward(dec_in, dec_valid, dec_weights, HEADS_DEC)
    grad_dec_in, dec_grads = block_backward(
        cotangent.astype(jnp.float32), dec_kept, dec_weights, dec_valid, HEADS_DEC
    )
    grad_mask = jnp.sum(grad_dec_in * missing, axis=(0, 1))
    grad_rows = jnp.einsum(
        "bjr,bjc->brc",
        picker,
        grad_dec_in.astype(jnp.bfloat16),
        preferred_element_type=jnp.float32,
    ).astype(jnp.bfloat16)
    grad_proj = weight_product(encoded, grad_rows)
    grad_bias_proj = jnp.sum(grad_rows.astype(jnp.float32), axis=(0, 1))
    back_rows = backward_product(grad_rows, enc_proj).astype(jnp.bfloat16)
    grad_enc_result, grad_gain_final, grad_shift_final = norm_grad(
        back_rows.astype(jnp.float32), final_unit, final_inverse, enc_gain_f[2]
    )
    grad_inputs, enc_grads = block_backward(
        grad_enc_result, enc_kept, enc_weights, enc_valid, HEADS_ENC
    )
    enc_small = (
        jnp.concatenate([enc_grads[0], grad_gain_final[None]], axis=0),
        jnp.concatenate([enc_grads[1], grad_shift_final[None]], axis=0),
    )
    half_enc = enc_width // 2
    half_dec = dec_width // 2
    decoded_full = dec_result.astype(jnp.bfloat16)
    patch_full = grad_inputs.astype(jnp.bfloat16)

    def swap_halves(full):
        half = full.shape[-1] // 2
        low_half, high_half = full[..., :half], full[..., half:]
        first = section_index == 0
        kept = jnp.where(first, low_half, high_half)
        arrived = lax.ppermute(jnp.where(first, high_half, low_half), "section", [(0, 1), (1, 0)])
        return jnp.concatenate(
            [jnp.where(first, kept, arrived), jnp.where(first, arrived, kept)], axis=0
        )

    decoded = swap_halves(decoded_full)
    patch_grad = swap_halves(patch_full)
    dec_gain_grad, dec_shift_grad, g_dqkv, g_dout, g_dbias, g_dup, g_dbup, g_ddown = dec_grads
    _, _, g_eqkv, g_eout, g_ebias, g_eup, g_ebup, g_edown = enc_grads
    small = small_scatter(
        (
            enc_small[0],
            enc_small[1],
            g_ebias,
            g_ebup,
            grad_bias_proj,
            grad_mask,
            dec_gain_grad,
            dec_shift_grad,
            g_dbias,
            g_dbup,
        ),
        (1, 1, 1, 0, 0, 0, 1, 1, 1, 0),
    )
    return (
        decoded,
        patch_grad,
        small[0],
        small[1],
        row_scatter(g_eqkv),
        row_scatter(g_eout),
        small[2],
        row_scatter(g_eup),
        small[3],
        row_scatter(g_edown),
        row_scatter(grad_proj),
        small[4],
        small[5],
        small[6],
        small[7],
        row_scatter(g_dqkv),
        row_scatter(g_dout),
        small[8],
        row_scatter(g_dup),
        small[9],
        row_scatter(g_ddown),
    )


def solution(mesh):
    return jax.shard_map(
        local,
        mesh=mesh,
        in_specs=(
            P("dp", None, None),
            P("dp"),
            P("dp", None),
            P(),
            P(),
            P(),
            P(),
            P(),
            P(),
            P(),
            P(),
            P(),
            P(),
            P(),
            P(),
            P(),
            P(),
            P(),
            P(),
            P(),
            P(),
            P(),
            P("dp", None, None),
        ),
        out_specs=(
            P("dp", None, "section"),
            P("dp", None, "section"),
            P(None, ("section", "dp")),
            P(None, ("section", "dp")),
            P(("section", "dp"), None),
            P(("section", "dp"), None),
            P(None, ("section", "dp")),
            P(("section", "dp"), None),
            P(("section", "dp")),
            P(("section", "dp"), None),
            P(("section", "dp"), None),
            P(("section", "dp")),
            P(("section", "dp")),
            P(None, ("section", "dp")),
            P(None, ("section", "dp")),
            P(("section", "dp"), None),
            P(("section", "dp"), None),
            P(None, ("section", "dp")),
            P(("section", "dp"), None),
            P(("section", "dp")),
            P(("section", "dp"), None),
        ),
        check_vma=False,
    )
```

```python
import functools
import math

import jax
import jax.numpy as jnp
import numpy as np
from jax import lax
from jax.experimental import pallas as pl
from jax.experimental.pallas import tpu as pltpu
from jax.sharding import PartitionSpec as P

HEADS_ENC = 12
HEADS_DEC = 16
ROW_STEP = 32
GROUP = 128
VMEM_BYTES = 56 * 1024 * 1024
MASKED = -1e30
LOG2E = math.log2(math.e)

epsilon = 1e-06

NN = (((1,), (0,)), ((), ()))
NT = (((1,), (1,)), ((), ()))
TN = (((0,), (0,)), ((), ()))


def dot(left_side, right_side, dims):
    return lax.dot_general(left_side, right_side, dims, preferred_element_type=jnp.float32)


def low(values):
    return values.astype(jnp.bfloat16)


def call(
    kernel, out_shape, grid, in_specs, out_specs, flops, moved, scalars=1, exps=0, after=(), name=None, scratch=()
):
    count = scalars + len(in_specs)
    ordered = [pl.BlockSpec(memory_space=pl.ANY)] * len(after)

    def body(*refs):
        kernel(*refs[:count], *refs[count + len(after) :])

    made = pl.pallas_call(
        body,
        out_shape=out_shape,
        grid_spec=pltpu.PrefetchScalarGridSpec(
            num_scalar_prefetch=scalars,
            grid=grid,
            in_specs=list(in_specs) + ordered,
            out_specs=out_specs,
            scratch_shapes=list(scratch),
        ),
        compiler_params=pltpu.CompilerParams(vmem_limit_bytes=VMEM_BYTES),
        cost_estimate=pl.CostEstimate(flops=flops // 256, bytes_accessed=moved // 256, transcendentals=0),
        name=name,
    )
    return lambda *operands: made(*operands, *after)


def whole(array):
    rank = array.ndim
    return pl.BlockSpec(array.shape, lambda *unused: (0,) * rank)


def row_of(ref, place):
    return ref[place : place + 1, :].astype(jnp.float32)


def vector_of(ref):
    return ref[...].astype(jnp.float32).reshape(1, -1)


def live_rows(values, start, count):
    row = lax.broadcasted_iota(jnp.int32, (values.shape[0], 1), 0) + start
    return jnp.where(row < count, values.astype(jnp.float32), 0.0)


def sds(shape, kind=jnp.bfloat16):
    return jax.ShapeDtypeStruct(shape, kind)


def norm(values, gain_row, shift_row):
    center = values - jnp.mean(values, axis=-1, keepdims=True)
    inverse = lax.rsqrt(jnp.mean(center * center, axis=-1, keepdims=True) + epsilon)
    unit = center * inverse
    return unit * gain_row + shift_row, unit, inverse


def norm_back(grad_out, unit, inverse, gain_row):
    scaled = grad_out * gain_row
    return inverse * (
        scaled
        - jnp.mean(scaled, axis=-1, keepdims=True)
        - unit * jnp.mean(scaled * unit, axis=-1, keepdims=True)
    )


def col_sum(values):
    return jnp.sum(values, axis=0, keepdims=True)


def gelu_parts(values):
    size = jnp.abs(values)
    t = 1.0 / (1.0 + (0.3275911 / math.sqrt(2.0)) * size)
    bell = jnp.exp2(values * values * (-0.5 * LOG2E))
    poly = t * (
        0.5 * 0.254829592
        + t
        * (
            0.5 * -0.284496736
            + t * (0.5 * 1.421413741 + t * (0.5 * -1.453152027 + t * (0.5 * 1.061405429)))
        )
    )
    tail = poly * bell
    share = jnp.where(values >= 0.0, 1.0 - tail, tail)
    return values * share, share + values * bell * (1.0 / math.sqrt(2.0 * math.pi))


def add_rows(ref, rows):
    @pl.when((pl.program_id(0) == 0) & (pl.program_id(1) == 0))
    def start():
        ref[...] = jnp.zeros_like(ref)

    for place, row in enumerate(rows):
        ref[place : place + 1, :] += row


BLOCK = 1
STRIP = 2


def place_info(visible, strips):
    section_index = lax.axis_index("section")
    block = section_index * lax.axis_size("dp") + lax.axis_index("dp")
    mine = section_index * strips + jnp.arange(strips, dtype=jnp.int32)
    every = jnp.arange(2 * strips, dtype=jnp.int32)
    return jnp.concatenate(
        [
            jnp.stack([section_index, block]),
            mine,
            lax.dynamic_slice_in_dim(visible, section_index * strips, strips, 0),
            every // strips,
            every % strips,
        ]
    ).astype(jnp.int32)


class Sizes:
    def __init__(self, strips, length, padded):
        self.strips, self.length, self.padded = strips, length, padded
        self.rows = strips * padded
        self.pieces = 2
        self.step = padded // self.pieces
        self.grid = (strips, self.pieces)

    def flat(self, width):
        return pl.BlockSpec((self.step, width), lambda s, i, info: (s * self.pieces + i, 0))

    def flat_three(self, width):
        return pl.BlockSpec((3, self.step, width), lambda s, i, info: (0, s * self.pieces + i, 0))

    def raw(self, width):
        return pl.BlockSpec((None, self.step, width), lambda s, i, info: (info[STRIP + s], i, 0))

    def half(self, width):
        return pl.BlockSpec((None, self.step, width), lambda s, i, info: (s, i, 0))

    def sums(self, width):
        return pl.BlockSpec((8, width), lambda s, i, info: (0, 0))

    def strip(self, width):
        return pl.BlockSpec((None, self.padded, width), lambda s, i, info: (s, 0, 0))


class OneStrip(Sizes):
    def __init__(self, sizes, strip):
        super().__init__(sizes.strips, sizes.length, sizes.padded)
        self.at = strip
        self.grid = (1, self.pieces)

    def flat(self, width):
        return pl.BlockSpec((self.step, width), lambda s, i, info: (self.at * self.pieces + i, 0))

    def flat_three(self, width):
        return pl.BlockSpec(
            (3, self.step, width), lambda s, i, info: (0, self.at * self.pieces + i, 0)
        )

    def raw(self, width):
        return pl.BlockSpec((None, self.step, width), lambda s, i, info: (info[STRIP + self.at], i, 0))

    def half(self, width):
        return pl.BlockSpec((None, self.step, width), lambda s, i, info: (0, i, 0))


def store_halves(info_ref, kept_ref, sent_ref, values):
    half = kept_ref.shape[-1]
    first = info_ref[0] == 0
    kept_ref[...] = low(jnp.where(first, values[:, :half], values[:, half:]))
    sent_ref[...] = low(jnp.where(first, values[:, half:], values[:, :half]))


def packed_kernel(info_ref, x_ref, gain_ref, shift_ref, w_ref, n_ref, packed_ref, *, length):
    x = live_rows(x_ref[...], pl.program_id(1) * x_ref.shape[0], length)
    normed, _, _ = norm(x, row_of(gain_ref, 0), row_of(shift_ref, 0))
    normed = low(normed)
    n_ref[...] = normed
    packed_ref[...] = low(dot(normed, w_ref[...], NN))


def packed_call(sizes, info, x, gains, shifts, w_qkv):
    rows, width = sizes.rows, x.shape[2]
    return call(
        functools.partial(packed_kernel, length=sizes.length),
        (sds((rows, width)), sds((rows, 3 * width))),
        sizes.grid,
        [sizes.raw(width), whole(gains), whole(shifts), whole(w_qkv)],
        (sizes.flat(width), sizes.flat(3 * width)),
        6 * rows * width * width,
        rows * width * 10 + 6 * width * width,
        name="encoder_packed",
    )(info, x, gains, shifts, w_qkv)


def picker_of(source_ref, strip):
    taken = source_ref[pl.ds(strip, 1), :]
    length = taken.shape[1]
    return low(jnp.where(taken == lax.broadcasted_iota(jnp.int32, (length, length), 0), 1.0, 0.0))


def last_row(length):
    return lax.broadcasted_iota(jnp.int32, (length, 1), 0) == length - 1


def decoder_in_kernel(
    info_ref,
    rows_ref,
    source_ref,
    mask_ref,
    places_ref,
    gain_ref,
    shift_ref,
    w_ref,
    x_ref,
    n_ref,
    packed_ref,
):
    picker = picker_of(source_ref, info_ref[STRIP + pl.program_id(0)])
    rows = jnp.where(
        last_row(rows_ref.shape[0]), vector_of(mask_ref), rows_ref[...].astype(jnp.float32)
    )
    x = dot(picker, low(rows), TN) + places_ref[...]
    x_ref[...] = x
    normed, _, _ = norm(x, row_of(gain_ref, 0), row_of(shift_ref, 0))
    normed = low(normed)
    n_ref[...] = normed
    packed_ref[...] = low(dot(normed, w_ref[...], NN))


def decoder_in_call(sizes, info, projected, source, mask_row, places, gains, shifts, w_qkv):
    width = projected.shape[1]
    rows, strips, padded = sizes.rows, sizes.strips, sizes.padded
    weights = (gains, shifts, w_qkv)
    return call(
        decoder_in_kernel,
        (
            sds((strips, padded, width), jnp.float32),
            sds((strips, padded, width)),
            sds((strips, padded, 3 * width)),
        ),
        (strips, 1),
        [sizes.strip(width), whole(source), whole(mask_row), whole(places)]
        + [whole(w) for w in weights],
        (sizes.strip(width), sizes.strip(width), sizes.strip(3 * width)),
        6 * rows * width * width + 2 * rows * padded * width,
        rows * width * 18 + 6 * width * width,
        name="decoder_packed",
    )(info, projected.reshape(strips, padded, width), source, mask_row, places, *weights)


def head_parts(head, heads_here):
    lane = lax.broadcasted_iota(jnp.int32, (1, GROUP), 1)
    size = GROUP // heads_here
    mine = (lane >= head * size) & (lane < (head + 1) * size)
    spare = ((head + 1) % heads_here) * size
    return mine, lane == spare, spare


def key_bias(live, length):
    row = lax.broadcasted_iota(jnp.int32, (length, 1), 0)
    return low(jnp.where(row < live, 0.0, MASKED))


def attend_kernel(info_ref, q_ref, k_ref, v_ref, out_ref, *, heads_here, live):
    length = q_ref.shape[1]
    rate = (GROUP // heads_here) ** -0.5 * LOG2E
    q, k, v = q_ref[0], k_ref[0], v_ref[0]
    bias = key_bias(live(info_ref, pl.program_id(0)), length)
    one = jnp.bfloat16(1.0)
    mixed = jnp.zeros((length, GROUP), jnp.float32)
    for head in range(heads_here):
        mine, at_spare, spare = head_parts(head, heads_here)
        head_q = jnp.where(mine, q, low(jnp.where(at_spare, 1.0, 0.0)))
        scores = dot(head_q, jnp.where(at_spare, bias, k), NT)
        highest = jnp.max(scores, axis=1, keepdims=True)
        terms = low(jnp.exp2((scores - highest) * rate))
        product = dot(terms, jnp.where(at_spare, one, v), NN)
        total = product[:, spare : spare + 1]
        mixed = jnp.where(mine, product * (1.0 / total), mixed)
    out_ref[0] = low(mixed)


def all_live(length):
    return lambda info_ref, strip: length


def visible_live(strips):
    return lambda info_ref, strip: info_ref[STRIP + strips + strip]


def attend_call(packed, info, heads, live, name):
    strips, length, triple = packed.shape
    width = triple // 3
    heads_here = GROUP // (width // heads)
    groups = width // GROUP
    third = lambda j: pl.BlockSpec((1, length, GROUP), lambda s, g, _: (s, 0, g + j * groups))
    return call(
        functools.partial(attend_kernel, heads_here=heads_here, live=live),
        sds((strips, length, width)),
        (strips, groups),
        [third(0), third(1), third(2)],
        third(0),
        strips * heads * length * length * GROUP * 6,
        strips * length * width * 8,
        exps=strips * heads * length * length,
        name=name,
    )(info, packed, packed, packed)


def attend_back_kernel(
    info_ref,
    q_ref,
    k_ref,
    v_ref,
    dout_ref,
    n_ref,
    grad_ref,
    kept_ref,
    sent_ref,
    total_ref,
    *,
    heads_here,
    live
):
    length = q_ref.shape[1]
    factor = (GROUP // heads_here) ** -0.5
    rate = factor * LOG2E
    strip = pl.program_id(1)
    q, k, v, dout = q_ref[0], k_ref[0], v_ref[0], dout_ref[0]
    bias = key_bias(live(info_ref, strip), length)
    k_turned = k.T
    dq_turned = jnp.zeros((GROUP, length), jnp.float32)
    dk = jnp.zeros((length, GROUP), jnp.float32)
    dv = jnp.zeros((length, GROUP), jnp.float32)
    row = lax.broadcasted_iota(jnp.int32, (GROUP, 1), 0)
    size = GROUP // heads_here
    for head in range(heads_here):
        mine, at_spare, _ = head_parts(head, heads_here)
        head_q = jnp.where(mine, q, low(jnp.where(at_spare, 1.0, 0.0)))
        head_dout = jnp.where(mine, dout, jnp.bfloat16(0.0))
        scores = dot(jnp.where(at_spare, bias, k), head_q, NT)
        highest = jnp.max(scores, axis=0, keepdims=True)
        terms = jnp.exp2((scores - highest) * rate)
        probs = terms * (1.0 / jnp.sum(terms, axis=0, keepdims=True))
        weighted = probs * dot(v, head_dout, NT)
        dscores = low(weighted - probs * jnp.sum(weighted, axis=0, keepdims=True))
        dk = jnp.where(mine, dot(dscores, q, NN), dk)
        dv = jnp.where(mine, dot(low(probs), dout, NN), dv)
        mine_row = (row >= head * size) & (row < (head + 1) * size)
        dq_turned = jnp.where(mine_row, dot(k_turned, dscores, NN), dq_turned)
    dq, dk, dv = low(dq_turned.T * factor), low(dk * factor), low(dv)
    grad_ref[0, 0] = dq
    grad_ref[1, 0] = dk
    grad_ref[2, 0] = dv
    term = dot(n_ref[0], jnp.concatenate([dq, dk, dv], axis=1), TN)
    half = kept_ref.shape[0]
    last = pl.num_programs(1) - 1

    @pl.when(strip == 0)
    def begin():
        total_ref[...] = term

    @pl.when(strip > 0)
    def more():
        total_ref[...] += term

    @pl.when(strip == last)
    def finish():
        kept_ref[...] = low(total_ref[pl.ds(pl.multiple_of(info_ref[0] * half, 8), half), :])
        sent_ref[...] = low(total_ref[pl.ds(pl.multiple_of((1 - info_ref[0]) * half, 8), half), :])


def attend_back_call(packed, dmixed, normed, info, heads, live, part, parts, after, name):
    strips, length, triple = packed.shape
    width = triple // 3
    heads_here = GROUP // (width // heads)
    groups = width // GROUP
    here = groups // parts
    third = lambda j: pl.BlockSpec(
        (1, length, GROUP), lambda g, s, _: (s, 0, g + part * here + j * groups)
    )
    product = pl.BlockSpec((width // 2, 3 * GROUP), lambda g, s, _: (0, g))
    return call(
        functools.partial(attend_back_kernel, heads_here=heads_here, live=live),
        (
            sds((3, strips, length, here * GROUP)),
            sds((width // 2, here * 3 * GROUP)),
            sds((width // 2, here * 3 * GROUP)),
        ),
        (here, strips),
        [
            third(0),
            third(1),
            third(2),
            third(0),
            pl.BlockSpec((1, length, width), lambda g, s, _: (s, 0, 0)),
        ],
        (pl.BlockSpec((3, 1, length, GROUP), lambda g, s, _: (0, s, 0, g)), product, product),
        (strips * heads * length * length * GROUP * 12 + 6 * strips * length * width * width) // parts,
        strips * length * width * 14 // parts,
        exps=strips * heads * length * length // parts,
        after=after,
        name=name,
        scratch=[pltpu.VMEM((width, 3 * GROUP), jnp.float32)],
    )(info, packed, packed, packed, dmixed, normed)


def encoder_ff_kernel(
    info_ref,
    x_ref,
    mixed_ref,
    gain_ref,
    shift_ref,
    w_out_ref,
    bias_out_ref,
    w_up_ref,
    bias_up_ref,
    w_down_ref,
    w_proj_ref,
    bias_proj_ref,
    mid_ref,
    n_ref,
    act_ref,
    slope_ref,
    y_ref,
    encoded_ref,
    projected_ref,
    *,
    chunk,
    length
):
    x = live_rows(x_ref[...], pl.program_id(1) * x_ref.shape[0], length)
    mid = x + dot(mixed_ref[...], w_out_ref[...], NN) + row_of(bias_out_ref, 0)
    mid_ref[...] = mid
    normed, _, _ = norm(mid, row_of(gain_ref, 1), row_of(shift_ref, 1))
    normed = low(normed)
    n_ref[...] = normed
    bias_up = vector_of(bias_up_ref)
    y = mid + row_of(bias_out_ref, 1)
    for start in range(0, w_up_ref.shape[1], chunk):
        part = slice(start, start + chunk)
        hidden = dot(normed, w_up_ref[:, part], NN) + bias_up[:, part]
        act, slope = gelu_parts(hidden)
        act = low(act)
        act_ref[:, part] = act
        slope_ref[:, part] = low(slope)
        y = y + dot(act, w_down_ref[part, :], NN)
    y_ref[...] = y
    encoded, _, _ = norm(y, row_of(gain_ref, 2), row_of(shift_ref, 2))
    encoded = low(encoded)
    encoded_ref[...] = encoded
    projected_ref[...] = low(dot(encoded, w_proj_ref[...], NN) + vector_of(bias_proj_ref))


def encoder_ff_call(
    sizes, info, x, mixed, gains, shifts, w_out, bias_out, w_up, bias_up, w_down, w_proj, bias_proj
):
    rows, width = sizes.rows, x.shape[2]
    units = w_up.shape[1]
    narrow = w_proj.shape[1]
    flat = sizes.flat
    weights = (gains, shifts, w_out, bias_out, w_up, bias_up, w_down, w_proj, bias_proj)
    return call(
        functools.partial(encoder_ff_kernel, chunk=units // 4, length=sizes.length),
        (
            sds((rows, width), jnp.float32),
            sds((rows, width)),
            sds((rows, units)),
            sds((rows, units)),
            sds((rows, width), jnp.float32),
            sds((rows, width)),
            sds((rows, narrow)),
        ),
        sizes.grid,
        [sizes.raw(width), flat(width)] + [whole(w) for w in weights],
        (flat(width), flat(width), flat(units), flat(units), flat(width), flat(width), flat(narrow)),
        2 * rows * width * (width + 2 * units + narrow),
        rows * (width * 16 + units * 4) + 2 * width * (width + 2 * units + narrow),
        exps=rows * units,
        name="encoder_feed_forward",
    )(info, x, mixed, *weights)


def decoder_ff_kernel(
    info_ref,
    x_ref,
    mixed_ref,
    cot_ref,
    gain_ref,
    shift_ref,
    w_out_ref,
    bias_out_ref,
    w_up_ref,
    bias_up_ref,
    w_down_ref,
    kept_ref,
    sent_ref,
    cot_low_ref,
    n_ref,
    act_ref,
    dhidden_ref,
    gm_ref,
    gb_ref,
    dmixed_ref,
    sums_ref,
    up_sums_ref,
    *,
    chunk,
    length
):
    mid = x_ref[...] + dot(mixed_ref[...], w_out_ref[...], NN) + row_of(bias_out_ref, 0)
    gain = row_of(gain_ref, 1)
    normed, unit, inverse = norm(mid, gain, row_of(shift_ref, 1))
    normed = low(normed)
    n_ref[...] = normed
    grad = live_rows(cot_ref[...], pl.program_id(1) * cot_ref.shape[0], length)
    cot = low(grad)
    cot_low_ref[...] = cot
    bias_up = vector_of(bias_up_ref)
    y = mid + row_of(bias_out_ref, 1)
    dnormed = jnp.zeros(y.shape, jnp.float32)
    up_sums = []
    for start in range(0, w_up_ref.shape[1], chunk):
        part = slice(start, start + chunk)
        hidden = dot(normed, w_up_ref[:, part], NN) + bias_up[:, part]
        act, slope = gelu_parts(hidden)
        act = low(act)
        act_ref[:, part] = act
        y = y + dot(act, w_down_ref[part, :], NN)
        dhidden = low(dot(cot, w_down_ref[part, :], NT) * slope)
        dhidden_ref[:, part] = dhidden
        up_sums.append(col_sum(dhidden.astype(jnp.float32)))
        dnormed = dnormed + dot(dhidden, w_up_ref[:, part], NT)
    store_halves(info_ref, kept_ref, sent_ref, y)
    gm = grad + norm_back(dnormed, unit, inverse, gain)
    gm_ref[...] = gm
    gb = low(gm)
    gb_ref[...] = gb
    dmixed_ref[...] = low(dot(gb, w_out_ref[...], NT))
    add_rows(
        sums_ref,
        (col_sum(dnormed * unit), col_sum(dnormed), col_sum(gb.astype(jnp.float32)), col_sum(grad)),
    )
    add_rows(up_sums_ref, (jnp.concatenate(up_sums, axis=1),))


def decoder_ff_call(
    sizes, info, x, mixed, cot, gains, shifts, w_out, bias_out, w_up, bias_up, w_down
):
    rows, width = x.shape
    units = w_up.shape[1]
    flat = sizes.flat
    weights = (gains, shifts, w_out, bias_out, w_up, bias_up, w_down)
    half = sds((sizes.strips, sizes.length, width // 2))
    return call(
        functools.partial(decoder_ff_kernel, chunk=units // 4, length=sizes.length),
        (
            half,
            half,
            sds((rows, width)),
            sds((rows, width)),
            sds((rows, units)),
            sds((rows, units)),
            sds((rows, width), jnp.float32),
            sds((rows, width)),
            sds((rows, width)),
            sds((8, width), jnp.float32),
            sds((8, units), jnp.float32),
        ),
        sizes.grid,
        [flat(width), flat(width), sizes.raw(width)] + [whole(w) for w in weights],
        (
            sizes.half(width // 2),
            sizes.half(width // 2),
            flat(width),
            flat(width),
            flat(units),
            flat(units),
            flat(width),
            flat(width),
            flat(width),
            sizes.sums(width),
            sizes.sums(units),
        ),
        2 * rows * width * (2 * width + 4 * units),
        rows * (width * 22 + units * 4) + 2 * width * (width + 2 * units),
        exps=rows * units,
        name="decoder_feed_forward",
    )(info, x, mixed, cot, *weights)


def encoder_ff_back_kernel(
    info_ref,
    grad_ref,
    mid_ref,
    slope_ref,
    gain_ref,
    shift_ref,
    w_out_ref,
    w_up_ref,
    w_down_ref,
    dhidden_ref,
    gm_ref,
    gb_ref,
    dmixed_ref,
    sums_ref,
    up_sums_ref,
    *,
    chunk
):
    gain = row_of(gain_ref, 1)
    _, unit, inverse = norm(mid_ref[...], gain, row_of(shift_ref, 1))
    grad = grad_ref[...]
    grad_low = low(grad)
    dnormed = jnp.zeros(grad.shape, jnp.float32)
    up_sums = []
    for start in range(0, w_up_ref.shape[1], chunk):
        part = slice(start, start + chunk)
        slope = slope_ref[:, part].astype(jnp.float32)
        dhidden = low(dot(grad_low, w_down_ref[part, :], NT) * slope)
        dhidden_ref[:, part] = dhidden
        up_sums.append(col_sum(dhidden.astype(jnp.float32)))
        dnormed = dnormed + dot(dhidden, w_up_ref[:, part], NT)
    gm = grad + norm_back(dnormed, unit, inverse, gain)
    gm_ref[...] = gm
    gb = low(gm)
    gb_ref[...] = gb
    dmixed_ref[...] = low(dot(gb, w_out_ref[...], NT))
    add_rows(
        sums_ref,
        (
            col_sum(dnormed * unit),
            col_sum(dnormed),
            col_sum(gb.astype(jnp.float32)),
            col_sum(grad_low.astype(jnp.float32)),
        ),
    )
    add_rows(up_sums_ref, (jnp.concatenate(up_sums, axis=1),))


def encoder_ff_back_call(sizes, info, grad, mid, slope, gains, shifts, w_out, w_up, w_down, after):
    rows, width = grad.shape
    units = w_up.shape[1]
    flat = sizes.flat
    weights = (gains, shifts, w_out, w_up, w_down)
    return call(
        functools.partial(encoder_ff_back_kernel, chunk=units // 4),
        (
            sds((rows, units)),
            sds((rows, width), jnp.float32),
            sds((rows, width)),
            sds((rows, width)),
            sds((8, width), jnp.float32),
            sds((8, units), jnp.float32),
        ),
        sizes.grid,
        [flat(width), flat(width), flat(units)] + [whole(w) for w in weights],
        (flat(units), flat(width), flat(width), flat(width), sizes.sums(width), sizes.sums(units)),
        2 * rows * width * (width + 2 * units),
        rows * (width * 16 + units * 4) + 2 * width * (width + 2 * units),
        after=after,
        name="encoder_feed_forward_back",
    )(info, grad, mid, slope, *weights)


def packed_back(grad_refs, w_ref):
    width = w_ref.shape[0]
    total = None
    for part, grad_ref in enumerate(grad_refs):
        here = grad_ref.shape[-1]
        for j in range(3):
            start = j * width + part * here
            term = dot(grad_ref[j], w_ref[:, start : start + here], NT)
            total = term if total is None else total + term
    return total


def decoder_back_kernel(
    info_ref,
    dpacked_ref,
    gm_ref,
    x_ref,
    source_ref,
    y_ref,
    encoded_ref,
    gain_ref,
    shift_ref,
    w_ref,
    w_proj_ref,
    enc_gain_ref,
    enc_shift_ref,
    grad_ref,
    grad_low_ref,
    sums_ref,
    enc_sums_ref,
    kept_ref,
    sent_ref,
    total_ref,
):
    dnormed = packed_back((dpacked_ref,), w_ref)
    gain = row_of(gain_ref, 0)
    _, unit, inverse = norm(x_ref[...], gain, row_of(shift_ref, 0))
    dx = gm_ref[...] + norm_back(dnormed, unit, inverse, gain)
    picker = picker_of(source_ref, info_ref[STRIP + pl.program_id(0)])
    taken = dot(picker, low(dx), NN)
    last = taken.shape[0] - 1
    dproj = low(jnp.where(last_row(taken.shape[0]), 0.0, taken))
    term = dot(encoded_ref[...], dproj, TN)
    half = kept_ref.shape[0]

    @pl.when(pl.program_id(0) == 0)
    def begin():
        total_ref[...] = term

    @pl.when(pl.program_id(0) > 0)
    def more():
        total_ref[...] += term

    @pl.when(pl.program_id(0) == pl.num_programs(0) - 1)
    def finish():
        kept_ref[...] = low(total_ref[pl.ds(pl.multiple_of(info_ref[0] * half, 8), half), :])
        sent_ref[...] = low(total_ref[pl.ds(pl.multiple_of((1 - info_ref[0]) * half, 8), half), :])

    dencoded = low(dot(dproj, w_proj_ref[...], NT)).astype(jnp.float32)
    enc_gain = row_of(enc_gain_ref, 2)
    _, unit_final, inverse_final = norm(y_ref[...], enc_gain, row_of(enc_shift_ref, 2))
    grad = norm_back(dencoded, unit_final, inverse_final, enc_gain)
    grad_ref[...] = grad
    grad_low_ref[...] = low(grad)
    add_rows(
        sums_ref,
        (
            col_sum(dnormed * unit),
            col_sum(dnormed),
            taken[last : last + 1],
            col_sum(dproj.astype(jnp.float32)),
        ),
    )
    add_rows(enc_sums_ref, (col_sum(dencoded * unit_final), col_sum(dencoded)))


def decoder_back_call(
    sizes,
    info,
    dpacked,
    gm,
    x,
    source,
    y,
    encoded,
    gains,
    shifts,
    w_qkv,
    w_proj,
    enc_gains,
    enc_shifts,
    after,
):
    strips, padded, rows = sizes.strips, sizes.padded, sizes.rows
    width = x.shape[2]
    wide = y.shape[2]
    weights = (gains, shifts, w_qkv, w_proj, enc_gains, enc_shifts)
    strip = sizes.strip
    return call(
        decoder_back_kernel,
        (
            sds((strips, padded, wide), jnp.float32),
            sds((strips, padded, wide)),
            sds((8, width), jnp.float32),
            sds((8, wide), jnp.float32),
            sds((wide // 2, width)),
            sds((wide // 2, width)),
        ),
        (strips, 1),
        [
            pl.BlockSpec((3, None, padded, width), lambda s, i, info: (0, s, 0, 0)),
            strip(width),
            strip(width),
            whole(source),
            strip(wide),
            strip(wide),
        ]
        + [whole(w) for w in weights],
        (
            strip(wide),
            strip(wide),
            sizes.sums(width),
            sizes.sums(wide),
            pl.BlockSpec((wide // 2, width), lambda s, i, info: (0, 0)),
            pl.BlockSpec((wide // 2, width), lambda s, i, info: (0, 0)),
        ),
        2 * rows * width * (3 * width + padded + 2 * wide),
        rows * (width * 16 + wide * 8) + 2 * width * (3 * width + wide),
        after=after,
        name="decoder_packed_back",
        scratch=[pltpu.VMEM((wide, width), jnp.float32)],
    )(info, dpacked, gm, x, source, y, encoded, *weights)


def encoder_back_kernel(
    info_ref, first_ref, second_ref, gm_ref, x_ref, gain_ref, shift_ref, w_ref, kept_ref, sent_ref, sums_ref, *, length
):
    dnormed = packed_back((first_ref, second_ref), w_ref)
    gain = row_of(gain_ref, 0)
    x = live_rows(x_ref[...], pl.program_id(1) * x_ref.shape[0], length)
    _, unit, inverse = norm(x, gain, row_of(shift_ref, 0))
    store_halves(
        info_ref, kept_ref, sent_ref, gm_ref[...] + norm_back(dnormed, unit, inverse, gain)
    )
    add_rows(sums_ref, (col_sum(dnormed * unit), col_sum(dnormed)))


def encoder_back_call(sizes, info, dpacked, gm, x, gains, shifts, w_qkv, after):
    rows, width = gm.shape
    weights = (gains, shifts, w_qkv)
    half = sds((1, sizes.length, width // 2))
    three = [part.reshape(3, rows, part.shape[-1]) for part in dpacked]
    return call(
        functools.partial(encoder_back_kernel, length=sizes.length),
        (half, half, sds((8, width), jnp.float32)),
        sizes.grid,
        [sizes.flat_three(part.shape[-1]) for part in three]
        + [sizes.flat(width), sizes.raw(width)]
        + [whole(w) for w in weights],
        (sizes.half(width // 2), sizes.half(width // 2), sizes.sums(width)),
        6 * rows * width * width,
        rows * width * 14 + 6 * width * width,
        after=after,
        name=f"encoder_packed_back_{sizes.at}",
    )(info, *three, gm, x, *weights)


class Job:
    def __init__(self, left, right, row_step, col_step, offset):
        self.half = left.shape[1] // 2
        self.width = right.shape[1]
        self.rows = left.shape[0]
        self.row_step, self.col_step, self.offset = row_step, col_step, offset
        self.down = self.half // row_step
        self.across = self.width // col_step
        self.count = self.down * self.across

    def at(self, step):
        here = jnp.clip(step - self.offset, 0, self.count - 1)
        if self.across == 1:
            return here, 0
        if self.down == 1:
            return 0, here
        return here // self.across, here % self.across

    def left(self, pick):
        return pl.BlockSpec(
            (self.rows, self.row_step),
            lambda step, info: (0, pick(info[0]) * self.down + self.at(step)[0]),
        )

    def right(self):
        return pl.BlockSpec((self.rows, self.col_step), lambda step, info: (0, self.at(step)[1]))

    def out(self):
        return pl.BlockSpec((self.row_step, self.col_step), lambda step, info: self.at(step))


def product_kernel(info_ref, *refs, jobs):
    step = pl.program_id(0)
    out = 3 * len(jobs)
    for place, (offset, count) in enumerate(jobs):
        mine_ref, other_ref, right_ref = refs[3 * place : 3 * place + 3]
        kept_ref, sent_ref = refs[out + 2 * place : out + 2 * place + 2]

        @pl.when((step >= offset) & (step < offset + count))
        def product():
            right = right_ref[...]
            sent_ref[...] = low(dot(other_ref[...], right, TN))
            kept_ref[...] = low(dot(mine_ref[...], right, TN))


def product_call(info, products, name, after=()):
    jobs, operands, in_specs, out_specs, out_shape = [], [], [], [], []
    offset = flops = moved = 0
    for left, right, row_step, col_step in products:
        job = Job(left, right, row_step, col_step, offset)
        offset += job.count
        jobs.append(job)
        operands += [left, left, right]
        in_specs += [job.left(lambda own: own), job.left(lambda own: 1 - own), job.right()]
        out_specs += [job.out(), job.out()]
        out_shape += [sds((job.half, job.width))] * 2
        flops += 4 * job.rows * job.half * job.width
        moved += 2 * job.rows * (2 * job.half + job.width) + 4 * job.half * job.width
    outs = call(
        functools.partial(product_kernel, jobs=[(job.offset, job.count) for job in jobs]),
        tuple(out_shape),
        (offset,),
        in_specs,
        tuple(out_specs),
        flops,
        moved,
        after=after,
        name=name,
    )(info, *operands)
    return [outs[2 * place : 2 * place + 2] for place in range(len(jobs))]


def decoder_products_kernel(
    info_ref, n_ref, dhid_ref, act_ref, cot_ref, mixed_ref, gb_ref, out_ref, *, steps, col_step, row_step, share
):
    step = pl.program_id(0)
    width = cot_ref.shape[1]
    folds = steps

    @pl.when(step < steps)
    def up():
        start = pl.multiple_of(step * col_step, GROUP)
        out_ref[:, pl.ds(start, col_step)] = low(dot(n_ref[...], dhid_ref[...], TN))

    @pl.when((step >= steps) & (step < 2 * steps))
    def down():
        product = dot(act_ref[...], cot_ref[...], TN).reshape(-1, folds, share, width)
        here = row_step // folds
        start = pl.multiple_of((step - steps) * here, share)
        for fold in range(folds):
            place = width * (folds + 1 + fold)
            out_ref[pl.ds(start, here), place : place + width] = low(
                product[:, fold].reshape(here, width)
            )

    @pl.when(step == 2 * steps)
    def out():
        out_ref[:, width * folds : width * (folds + 1)] = low(dot(mixed_ref[...], gb_ref[...], TN))


def decoder_products_call(info, n, dhid, act, cot, mixed, gb, share, name):
    rows, width = cot.shape
    units = dhid.shape[1]
    steps = units // width
    shape = (width, 2 * units + width)
    at = lambda first: lambda step, info: (0, jnp.clip(step - first, 0, steps - 1))
    return call(
        functools.partial(
            decoder_products_kernel, steps=steps, col_step=width, row_step=width, share=share
        ),
        sds(shape),
        (2 * steps + 1,),
        [
            whole(n),
            pl.BlockSpec((rows, width), at(0)),
            pl.BlockSpec((rows, width), at(steps)),
            whole(cot),
            whole(mixed),
            whole(gb),
        ],
        pl.BlockSpec(shape, lambda step, info: (0, 0)),
        2 * rows * width * (2 * units + width),
        2 * rows * (2 * units + 4 * width) + 2 * shape[0] * shape[1],
        name=name,
    )(info, n, dhid, act, cot, mixed, gb)


class Chain:
    def __init__(self, pairs, order, parts):
        self.pairs = pairs
        self.bits = list(range(pairs.bit_length() - 1))
        self.order = [bit for bit in order if bit < len(self.bits)]
        self.order += [bit for bit in self.bits if bit not in self.order]
        self.widths = [kept.shape[1] for kept, _ in parts]
        self.parts = [
            (kept.reshape(pairs, -1, kept.shape[1]), arrived.reshape(pairs, -1, kept.shape[1]))
            for kept, arrived in parts
        ]
        self.done = None

    def item(self):
        kept = self.parts[0][0]
        if not self.order:
            return ("last", self.parts, self.widths, None)
        bit = self.order[0]
        lower = sum(1 for other in self.bits if other < bit)
        return ("halve", self.parts, (kept.shape[0] >> (lower + 1), 1 << lower), bit)

    def take(self, outs):
        if not self.order:
            self.done = outs
            return []
        bit = self.order.pop(0)
        self.bits.remove(bit)
        kept, sent = outs
        route = [(place, place ^ (1 << bit)) for place in range(self.pairs)]
        self.parts = [(kept, lax.ppermute(sent, "dp", route))]
        return [sent]


class Total:
    def __init__(self, pairs, values):
        self.pairs = pairs
        bits = [1 << bit for bit in range((2 * pairs).bit_length() - 1)]
        bits = bits[-1:] + bits[:-1]
        self.left = [bits[place : place + 2] for place in range(0, len(bits), 2)]
        self.done = None
        self.launch(values)

    def launch(self, values):
        group = self.left.pop(0)
        masks = group + [sum(group)] if len(group) > 1 else group
        count = 2 * self.pairs
        arrived = [
            lax.ppermute(values, ("section", "dp"), [(place, place ^ mask) for place in range(count)])
            for mask in masks
        ]
        self.parts = [(values, *arrived)]
        self.sent = values

    def item(self):
        return ("add", self.parts, None, None)

    def take(self, outs):
        (values,) = outs
        if not self.left:
            self.done = values
            return []
        self.launch(values)
        return [values]


def round_kernel(info_ref, *refs, items, counts):
    place = 0
    out = sum(sum(widths) for _, widths, _, _ in items)
    for (kind, widths, how, bit), count in zip(items, counts):
        pairs = []
        for width in widths:
            pairs.append(refs[place : place + width])
            place += width
        outs = refs[out : out + count]
        out += count
        if kind == "add":
            outs[0][...] = sum(ref[...] for ref in pairs[0])
            continue

        def total(pair, index):
            return pair[0][index].astype(jnp.float32) + pair[1][index].astype(jnp.float32)

        if kind == "last":
            start = 0
            values = [total(pair, 0) for pair in pairs]
            whole_row = values[0] if len(values) == 1 else jnp.concatenate(values, axis=1)
            for ref, width in zip(outs, how):
                ref[...] = whole_row[:, start : start + width]
                start += width
            continue
        high, lower = how
        mine = (info_ref[BLOCK] >> bit) & 1
        for h in range(high):
            for l in range(lower):
                start = 0
                for pair in pairs:
                    width = pair[0].shape[-1]
                    for ref, chosen in zip(outs, (mine, 1 - mine)):
                        index = (h * 2 + chosen) * lower + l
                        ref[h * lower + l, :, start : start + width] = low(total(pair, index))
                    start += width


def round_call(info, chains, name, after=()):
    items = [chain.item() for chain in chains]
    operands, out_shape, counts, moved = [], [], [], 0
    for kind, parts, how, _ in items:
        for part in parts:
            operands += part
            moved += len(part) * part[0].size * part[0].dtype.itemsize
        shape = parts[0][0].shape
        if kind == "add":
            out_shape.append(sds(shape, jnp.float32))
            counts.append(1)
        elif kind == "last":
            out_shape += [sds((shape[1], width), jnp.float32) for width in how]
            counts.append(len(how))
        else:
            width = sum(part[0].shape[-1] for part in parts)
            out_shape += [sds((shape[0] // 2, shape[1], width))] * 2
            counts.append(2)
    plain = [(kind, [len(part) for part in parts], how, bit) for kind, parts, how, bit in items]
    outs = call(
        functools.partial(round_kernel, items=plain, counts=counts),
        tuple(out_shape),
        (1,),
        [whole(operand) for operand in operands],
        tuple(whole(shape) for shape in out_shape),
        moved,
        2 * moved,
        after=after,
        name=name,
    )(info, *operands)
    sent, start = [], 0
    for chain, count in zip(chains, counts):
        sent += chain.take(outs[start : start + count])
        start += count
    return sent


def across(values):
    return lax.ppermute(values, "section", [(0, 1), (1, 0)])


def arrange_kernel(info_ref, *refs, strips):
    *sources, out_ref = refs
    holder = info_ref[STRIP + 2 * strips + pl.program_id(0)]
    slot = info_ref[STRIP + 4 * strips + pl.program_id(0)]
    per = len(sources) // 2
    values = None
    for place in range(strips):
        kept, arrived = (
            (sources[place][0], sources[per + place][0])
            if per == strips
            else (sources[0][place], sources[1][place])
        )
        chosen = jnp.where(holder == info_ref[0], kept, arrived)
        values = chosen if values is None else jnp.where(slot == place, chosen, values)
    out_ref[0] = values


def arrange_call(info, kept, arrived, strips, name, after=()):
    _, length, half = kept[0].shape
    return call(
        functools.partial(arrange_kernel, strips=strips),
        sds((2 * strips, length, half)),
        (2 * strips,),
        [whole(array) for array in (*kept, *arrived)],
        pl.BlockSpec((1, length, half), lambda k, info: (k, 0, 0)),
        1,
        strips * length * half * 12,
        name=name,
        after=after,
    )(info, *kept, *arrived)


def gather_small_kernel(
    info_ref, up_enc, up_dec, enc, dec, dec_in, final, *rest
):
    *enc_in, out_ref = rest
    out_ref[...] = jnp.zeros_like(out_ref)
    wide, narrow = enc.shape[1], dec.shape[1]
    out_ref[0:1, : up_enc.shape[1]] = up_enc[0:1, :]
    out_ref[1:2, : up_dec.shape[1]] = up_dec[0:1, :]
    out_ref[2:6, :wide] = enc[0:4, :]
    out_ref[2:6, wide : wide + narrow] = dec[0:4, :]
    out_ref[2:6, wide + narrow : wide + 2 * narrow] = dec_in[0:4, :]
    out_ref[6:8, :wide] = final[0:2, :]
    out_ref[6:8, wide : 2 * wide] = sum(ref[0:2, :] for ref in enc_in)


def gather_small_call(info, values):
    shape = (8, values[0].shape[1])
    return call(
        gather_small_kernel,
        sds(shape, jnp.float32),
        (1,),
        [whole(value) for value in values],
        pl.BlockSpec(shape, lambda i, info: (0, 0)),
        shape[1],
        shape[1] * 64,
        name="small_rows",
    )(info, *values)


def unshuffled(parts):
    return jnp.concatenate(
        [
            part[:, (3 * group + j) * GROUP : (3 * group + j + 1) * GROUP]
            for j in range(3)
            for part in parts
            for group in range(part.shape[1] // (3 * GROUP))
        ],
        axis=1,
    )


def shares_kernel(info_ref, rows_ref, dec_qkv_ref, *refs, parts, wide, narrow, units, dec_units, count):
    block = info_ref[BLOCK]

    def share(first, last, start, width):
        values = rows_ref[first:last, start : start + width]
        part = width // count
        return pltpu.roll(values, width - block * part, 1)[:, :part]

    enc_qkv = [ref[...] for ref in refs[:parts]]
    outs = refs[parts:]
    bias_up_enc = share(0, 1, 0, units)
    bias_up_dec = share(1, 2, 0, dec_units)
    enc = share(2, 6, 0, wide)
    dec = share(2, 6, wide, narrow)
    dec_in = share(2, 6, wide + narrow, narrow)
    final = share(6, 8, 0, wide)
    enc_in = share(6, 8, wide, wide)
    for ref, value in zip(
        outs,
        (
            jnp.concatenate([enc_in[0:1], enc[0:1], final[0:1]], axis=0),
            jnp.concatenate([enc_in[1:2], enc[1:2], final[1:2]], axis=0),
            enc[2:4],
            bias_up_enc,
            dec_in[3:4],
            dec_in[2:3],
            jnp.concatenate([dec_in[0:1], dec[0:1]], axis=0),
            jnp.concatenate([dec_in[1:2], dec[1:2]], axis=0),
            dec[2:4],
            bias_up_dec,
            unshuffled([dec_qkv_ref[...]]),
            unshuffled(enc_qkv),
        ),
    ):
        ref[...] = value


def shares_call(info, rows, dec_qkv, enc_qkv, wide, narrow, units, dec_units, count):
    shapes = [
        (height, width // count)
        for height, width in (
            (3, wide),
            (3, wide),
            (2, wide),
            (1, units),
            (1, narrow),
            (1, narrow),
            (2, narrow),
            (2, narrow),
            (2, narrow),
            (1, dec_units),
        )
    ] + [dec_qkv.shape, (wide // count, 3 * wide)]
    return call(
        functools.partial(
            shares_kernel,
            parts=len(enc_qkv),
            wide=wide,
            narrow=narrow,
            units=units,
            dec_units=dec_units,
            count=count,
        ),
        tuple(sds(shape, jnp.float32) for shape in shapes),
        (1,),
        [whole(array) for array in (rows, dec_qkv, *enc_qkv)],
        tuple(pl.BlockSpec(shape, lambda i, info: (0, 0)) for shape in shapes),
        rows.size,
        rows.size * 4,
        name="shares",
    )(info, rows, dec_qkv, *enc_qkv)


def decoder_shares_kernel(info_ref, rows_ref, up_ref, out_ref, down_ref):
    width = out_ref.shape[1]
    units = up_ref.shape[1]
    share = up_ref.shape[0]
    rows = rows_ref[...].astype(jnp.float32)
    up_ref[...] = rows[:, :units]
    out_ref[...] = rows[:, units : units + width]
    for fold in range(units // width):
        start = units + (fold + 1) * width
        down_ref[fold * share : (fold + 1) * share, :] = rows[:, start : start + width]


def decoder_shares_call(info, rows, width, units, after):
    share = rows.shape[0]
    shapes = ((share, units), (share, width), (share * units // width, width))
    return call(
        decoder_shares_kernel,
        tuple(sds(shape, jnp.float32) for shape in shapes),
        (1,),
        [whole(rows)],
        tuple(pl.BlockSpec(shape, lambda i, info: (0, 0)) for shape in shapes),
        rows.size,
        rows.size * 6,
        name="decoder_shares",
        after=after,
    )(info, rows)


def place_table(length_rows, model_width):
    halfway = model_width // 2
    places = np.arange(length_rows, dtype=np.float64)[:, None]
    rates = np.exp(np.arange(halfway, dtype=np.float64) * (-math.log(10000.0) / halfway))[None, :]
    return np.concatenate([np.sin(places * rates), np.cos(places * rates)], axis=1).astype(
        np.float32
    )


def local(
    patches,
    visible,
    source,
    enc_gains,
    enc_shifts,
    enc_qkv,
    enc_out,
    enc_bias_out,
    enc_up,
    enc_bias_up,
    enc_down,
    enc_proj,
    proj_bias,
    mask_token,
    dec_gains,
    dec_shifts,
    dec_qkv,
    dec_out,
    dec_bias_out,
    dec_up,
    dec_bias_up,
    dec_down,
    cotangent,
):
    pairs = lax.axis_size("dp")
    count = 2 * pairs
    length = patches.shape[1]
    wide = patches.shape[2]
    narrow = dec_qkv.shape[0]
    strips = patches.shape[0] // 2
    padded = -(-(length + 1) // ROW_STEP) * ROW_STEP
    sizes = Sizes(strips, length, padded)
    rows = sizes.rows
    info = place_info(visible, strips)
    taken = jnp.pad(
        jnp.where(source < 0, padded - 1, source),
        ((0, 0), (0, padded - length)),
        constant_values=padded - 1,
    )
    places = jnp.asarray(place_table(padded, narrow))
    strip_form = lambda array: array.reshape(strips, padded, array.shape[-1])
    row_form = lambda array: array.reshape(rows, array.shape[-1])

    n1_enc, packed_enc = packed_call(sizes, info, patches, enc_gains, enc_shifts, enc_qkv)
    packed_enc = strip_form(packed_enc)
    enc_live = visible_live(strips)
    mixed_enc = row_form(attend_call(packed_enc, info, HEADS_ENC, enc_live, "encoder_attention"))
    mid_enc, n2_enc, act_enc, slope_enc, y_enc, encoded, projected = encoder_ff_call(
        sizes,
        info,
        patches,
        mixed_enc,
        enc_gains,
        enc_shifts,
        enc_out,
        enc_bias_out,
        enc_up,
        enc_bias_up,
        enc_down,
        enc_proj,
        proj_bias,
    )
    x_dec, n1_dec, packed_dec = decoder_in_call(
        sizes, info, projected, taken, mask_token, places, dec_gains, dec_shifts, dec_qkv
    )
    dec_live = all_live(length)
    mixed_dec = row_form(attend_call(packed_dec, info, HEADS_DEC, dec_live, "decoder_attention"))
    (
        kept_dec,
        sent_dec,
        cot,
        n2_dec,
        act_dec,
        dhid_dec,
        gm_dec,
        gb_dec,
        dmixed_dec,
        sums_dec,
        up_sums_dec,
    ) = decoder_ff_call(
        sizes,
        info,
        row_form(x_dec),
        mixed_dec,
        cotangent,
        dec_gains,
        dec_shifts,
        dec_out,
        dec_bias_out,
        dec_up,
        dec_bias_up,
        dec_down,
    )
    dec_half, enc_half = narrow // 2, wide // 2
    share = narrow // count
    folded = share % 8 == 0
    if folded:
        beside = decoder_products_call(
            info, n2_dec, dhid_dec, act_dec, cot, mixed_dec, gb_dec, share, "grad_dec_weights"
        )
        summed = lax.psum_scatter(
            beside.reshape(count, share, -1), ("section", "dp"), scatter_dimension=0, tiled=True
        )[0]
        first_sent = (beside,)
    else:
        pieces = product_call(
            info,
            [
                (act_dec, cot, narrow, narrow),
                (n2_dec, dhid_dec, dec_half, narrow),
                (mixed_dec, gb_dec, dec_half, narrow),
            ],
            "grad_dec_weights",
        )
        first_sent = tuple(sent for _, sent in pieces)
        dec_chains = [
            Chain(pairs, (1, 0, 2, 3), ((kept, across(sent)),)) for kept, sent in pieces
        ]
    arrived_dec = across(sent_dec)
    dpacked_dec, kept_dqkv, sent_dqkv = attend_back_call(
        packed_dec,
        strip_form(dmixed_dec),
        n1_dec,
        info,
        HEADS_DEC,
        dec_live,
        0,
        1,
        (*first_sent, sent_dec),
        "decoder_attention_back",
    )
    arrived_dqkv = across(sent_dqkv)
    grad_enc, grad_enc_low, sums_dec_in, sums_final, kept_proj, sent_proj = decoder_back_call(
        sizes,
        info,
        dpacked_dec,
        strip_form(gm_dec),
        x_dec,
        taken,
        strip_form(y_enc),
        strip_form(encoded),
        dec_gains,
        dec_shifts,
        dec_qkv,
        enc_proj,
        enc_gains,
        enc_shifts,
        (sent_dqkv,),
    )
    grad_enc, grad_enc_low = map(row_form, (grad_enc, grad_enc_low))
    arrived_proj = across(sent_proj)
    qkv_dec = Chain(pairs, (0, 1, 2, 3), ((kept_dqkv, arrived_dqkv),))
    sent = round_call(info, [qkv_dec], "round_1", (grad_enc_low,))
    ((kept_edown, sent_edown),) = product_call(
        info, [(act_enc, grad_enc_low, enc_half, wide)], "grad_enc_down", (*sent, sent_proj)
    )
    arrived_edown = across(sent_edown)
    sent = round_call(info, [qkv_dec], "round_2", (kept_edown,))
    dhid_enc, gm_enc, gb_enc, dmixed_enc, sums_enc, up_sums_enc = encoder_ff_back_call(
        sizes,
        info,
        grad_enc,
        mid_enc,
        slope_enc,
        enc_gains,
        enc_shifts,
        enc_out,
        enc_up,
        enc_down,
        (*sent, sent_edown),
    )
    down_enc = Chain(pairs, (1, 2, 0, 3), ((kept_edown, arrived_edown),))
    sent = round_call(info, [qkv_dec], "round_3", (gb_enc,))
    (kept_eup, sent_eup), (kept_eout, sent_eout) = product_call(
        info,
        [(n2_enc, dhid_enc, enc_half, wide), (mixed_enc, gb_enc, enc_half, wide)],
        "grad_enc_up_out",
        sent,
    )
    arrived_eup, arrived_eout = map(across, (sent_eup, sent_eout))
    sent = round_call(info, [down_enc, qkv_dec], "round_4", (kept_eout,))
    half_back = lambda part, after: attend_back_call(
        packed_enc,
        strip_form(dmixed_enc),
        strip_form(n1_enc),
        info,
        HEADS_ENC,
        enc_live,
        part,
        2,
        after,
        f"encoder_attention_back_{part}",
    )
    dpacked_one, kept_one, sent_one = half_back(0, (*sent, sent_eup, sent_eout))
    arrived_one = across(sent_one)
    up_enc = Chain(pairs, (0, 1, 2, 3), ((kept_eup, arrived_eup),))
    out_enc = Chain(pairs, (2, 0, 1, 3), ((kept_eout, arrived_eout), (kept_proj, arrived_proj)))
    chains = [up_enc, down_enc, out_enc]
    sent = round_call(info, [*chains, qkv_dec], "round_5", (kept_one,))
    dpacked_two, kept_two, sent_two = half_back(1, (*sent, sent_one))
    arrived_two = across(sent_two)
    one_chain = Chain(pairs, (2, 0, 1, 3), ((kept_one, arrived_one),))
    chains += [one_chain]
    sent = round_call(info, chains, "round_6", (kept_two,))
    decoded = arrange_call(info, [kept_dec], [arrived_dec], strips, "decoded_strips", (kept_two,))
    back = lambda strip, after: encoder_back_call(
        OneStrip(sizes, strip),
        info,
        (dpacked_one, dpacked_two),
        gm_enc,
        patches,
        enc_gains,
        enc_shifts,
        enc_qkv,
        after,
    )
    kept_enc, arrived_enc, sums_enc_in = [], [], []
    after = (*sent, sent_two)
    for strip in range(strips):
        kept, sent_here, sums = back(strip, after)
        kept_enc.append(kept)
        arrived_enc.append(across(sent_here))
        sums_enc_in.append(sums)
        if strip == 0:
            two_chain = Chain(pairs, (1, 0, 2, 3), ((kept_two, arrived_two),))
            chains = [two_chain, *chains]
            sent = round_call(info, chains, "round_7", (sums,))
            after = (*sent, sent_here)
    small = Total(
        pairs,
        gather_small_call(
            info,
            (up_sums_enc, up_sums_dec, sums_enc, sums_dec, sums_dec_in, sums_final, *sums_enc_in),
        ),
    )
    after = (small.sent, sent_here)
    if not folded:
        chains += dec_chains
    number = 8
    every = [*chains, qkv_dec, small]
    while any(chain.done is None for chain in every):
        active = [chain for chain in every if chain.done is None]
        sent = round_call(info, active, f"round_{number}", after)
        if number == 8:
            patch_grad = arrange_call(
                info, kept_enc, arrived_enc, strips, "patch_grad_strips", tuple(sent)
            )
            after = (patch_grad,)
        else:
            after = ()
        number += 1
    (g_dqkv,), (g_one,), (g_two,) = qkv_dec.done, one_chain.done, two_chain.done
    shares = shares_call(
        info, small.done, g_dqkv, (g_one, g_two), wide, narrow, enc_up.shape[1], dec_up.shape[1], count
    )
    if folded:
        g_dup, g_dout, g_ddown = decoder_shares_call(
            info, summed, narrow, dec_up.shape[1], (kept_two,)
        )
    else:
        (g_ddown,), (g_dup,), (g_dout,) = [chain.done for chain in dec_chains]
    (g_edown,), (g_eup,), (g_eout, g_proj) = down_enc.done, up_enc.done, out_enc.done
    return (
        decoded,
        patch_grad,
        shares[0],
        shares[1],
        shares[11],
        g_eout,
        shares[2],
        g_eup,
        shares[3].reshape(-1),
        g_edown,
        g_proj,
        shares[4].reshape(-1),
        shares[5].reshape(-1),
        shares[6],
        shares[7],
        shares[10],
        g_dout,
        shares[8],
        g_dup,
        shares[9].reshape(-1),
        g_ddown,
    )


def solution(mesh):
    return jax.shard_map(
        local,
        mesh=mesh,
        in_specs=(
            P("dp", None, None),
            P("dp"),
            P("dp", None),
            P(),
            P(),
            P(),
            P(),
            P(),
            P(),
            P(),
            P(),
            P(),
            P(),
            P(),
            P(),
            P(),
            P(),
            P(),
            P(),
            P(),
            P(),
            P(),
            P("dp", None, None),
        ),
        out_specs=(
            P("dp", None, "section"),
            P("dp", None, "section"),
            P(None, ("section", "dp")),
            P(None, ("section", "dp")),
            P(("section", "dp"), None),
            P(("section", "dp"), None),
            P(None, ("section", "dp")),
            P(("section", "dp"), None),
            P(("section", "dp")),
            P(("section", "dp"), None),
            P(("section", "dp"), None),
            P(("section", "dp")),
            P(("section", "dp")),
            P(None, ("section", "dp")),
            P(None, ("section", "dp")),
            P(("section", "dp"), None),
            P(("section", "dp"), None),
            P(None, ("section", "dp")),
            P(("section", "dp"), None),
            P(("section", "dp")),
            P(("section", "dp"), None),
        ),
        check_vma=False,
    )
```

```python
import functools
import math

import jax
import jax.numpy as jnp
import numpy as np
from jax import lax
from jax.experimental import pallas as pl
from jax.experimental.pallas import tpu as pltpu
from jax.sharding import PartitionSpec as P

HEADS_ENC = 12
HEADS_DEC = 16
ROW_STEP = 32
GROUP = 128
PARTS = 2
VMEM_BYTES = 56 * 1024 * 1024
MASKED = -1e30
LOG2E = math.log2(math.e)

epsilon = 1e-06

NN = (((1,), (0,)), ((), ()))
NT = (((1,), (1,)), ((), ()))
TN = (((0,), (0,)), ((), ()))


def dot(left_side, right_side, dims):
    return lax.dot_general(left_side, right_side, dims, preferred_element_type=jnp.float32)


def low(values):
    return values.astype(jnp.bfloat16)


def call(
    kernel, out_shape, grid, in_specs, out_specs, flops, moved, scalars=1, exps=0, after=(), name=None, scratch=(), through=()
):
    count = scalars + len(in_specs)
    ordered = [pl.BlockSpec(memory_space=pl.ANY)] * (len(after) + len(through))
    aliases = {}
    if through:
        outs = len(out_shape)
        aliases = {count + len(after) + place: outs + place for place in range(len(through))}
        out_shape = tuple(out_shape) + tuple(sds(array.shape, array.dtype) for array in through)
        out_specs = tuple(out_specs) + (pl.BlockSpec(memory_space=pl.ANY),) * len(through)

    def body(*refs):
        ins, rest = refs[:count], refs[count + len(after) + len(through) :]
        if through:
            rest = rest[:outs] + rest[outs + len(through) :]
        kernel(*ins, *rest)

    made = pl.pallas_call(
        body,
        out_shape=out_shape,
        grid_spec=pltpu.PrefetchScalarGridSpec(
            num_scalar_prefetch=scalars,
            grid=grid,
            in_specs=list(in_specs) + ordered,
            out_specs=out_specs,
            scratch_shapes=list(scratch),
        ),
        input_output_aliases=aliases,
        compiler_params=pltpu.CompilerParams(vmem_limit_bytes=VMEM_BYTES),
        cost_estimate=pl.CostEstimate(flops=flops // 256, bytes_accessed=moved // 256, transcendentals=0),
        name=name,
    )
    return lambda *operands: made(*operands, *after, *through)


def whole(array):
    rank = array.ndim
    return pl.BlockSpec(array.shape, lambda *unused: (0,) * rank)


def row_of(ref, place):
    return ref[place : place + 1, :].astype(jnp.float32)


def vector_of(ref):
    return ref[...].astype(jnp.float32).reshape(1, -1)


def live_rows(values, start, count):
    row = lax.broadcasted_iota(jnp.int32, (values.shape[0], 1), 0) + start
    return jnp.where(row < count, values.astype(jnp.float32), 0.0)


def sds(shape, kind=jnp.bfloat16):
    return jax.ShapeDtypeStruct(shape, kind)


def norm(values, gain_row, shift_row):
    center = values - jnp.mean(values, axis=-1, keepdims=True)
    inverse = lax.rsqrt(jnp.mean(center * center, axis=-1, keepdims=True) + epsilon)
    unit = center * inverse
    return unit * gain_row + shift_row, unit, inverse


def norm_back(grad_out, unit, inverse, gain_row):
    scaled = grad_out * gain_row
    return inverse * (
        scaled
        - jnp.mean(scaled, axis=-1, keepdims=True)
        - unit * jnp.mean(scaled * unit, axis=-1, keepdims=True)
    )


def col_sum(values):
    return jnp.sum(values, axis=0, keepdims=True)


def gelu_parts(values):
    share = 0.5 + 0.5 * lax.erf(values * math.sqrt(0.5))
    bell = jnp.exp2(values * values * (-0.5 * LOG2E)) * (1.0 / math.sqrt(2.0 * math.pi))
    return values * share, share + values * bell


def add_rows(ref, rows):
    @pl.when((pl.program_id(0) == 0) & (pl.program_id(1) == 0))
    def start():
        ref[...] = jnp.zeros_like(ref)

    for place, row in enumerate(rows):
        ref[place : place + 1, :] += row


BLOCK = 1
STRIP = 2


def place_info(visible, strips):
    section_index = lax.axis_index("section")
    block = section_index * lax.axis_size("dp") + lax.axis_index("dp")
    mine = section_index * strips + jnp.arange(strips, dtype=jnp.int32)
    every = jnp.arange(2 * strips, dtype=jnp.int32)
    return jnp.concatenate(
        [
            jnp.stack([section_index, block]),
            mine,
            lax.dynamic_slice_in_dim(visible, section_index * strips, strips, 0),
            every // strips,
            every % strips,
        ]
    ).astype(jnp.int32)


class Sizes:
    def __init__(self, strips, length, padded):
        self.strips, self.length, self.padded = strips, length, padded
        self.rows = strips * padded

    def place(self, strip):
        return slice(strip * self.padded, (strip + 1) * self.padded)

    def raw(self, width):
        return [
            pl.BlockSpec(
                (None, self.padded, width), lambda *step, s=s: (step[-1][STRIP + s], 0, 0)
            )
            for s in range(self.strips)
        ]

    def all(self, width):
        return pl.BlockSpec((self.rows, width), lambda *step: (0, 0))

    def cols(self, width):
        return pl.BlockSpec((self.rows, width), lambda i, info: (0, i))

    def half(self, width):
        return pl.BlockSpec((self.strips, self.padded, width), lambda *step: (0, 0, 0))

    def sums(self, width):
        return pl.BlockSpec((8, width), lambda *step: (0, 0))

    def strip(self, width):
        return pl.BlockSpec((None, self.padded, width), lambda s, i, info: (s, 0, 0))


def first_step(run):
    pl.when(pl.program_id(0) == 0)(run)


def last_step(run):
    pl.when(pl.program_id(0) == pl.num_programs(0) - 1)(run)


def store_halves(info_ref, kept_ref, sent_ref, values):
    half = kept_ref.shape[-1]
    first = info_ref[0] == 0
    kept_ref[...] = low(jnp.where(first, values[:, :half], values[:, half:]))
    sent_ref[...] = low(jnp.where(first, values[:, half:], values[:, :half]))


def set_rows(ref, rows):
    for place, row in enumerate(rows):
        ref[place : place + 1, :] = row


def packed_kernel(info_ref, *refs, sizes):
    x_refs = refs[: sizes.strips]
    gain_ref, shift_ref, w_ref, n_ref, packed_ref = refs[sizes.strips :]

    @first_step
    def normalize():
        for strip, x_ref in enumerate(x_refs):
            x = live_rows(x_ref[...], 0, sizes.length)
            normed, _, _ = norm(x, row_of(gain_ref, 0), row_of(shift_ref, 0))
            n_ref[sizes.place(strip), :] = low(normed)

    packed_ref[...] = low(dot(n_ref[...], w_ref[...], NN))


def packed_call(sizes, info, x, gains, shifts, w_qkv):
    rows, width = sizes.rows, x.shape[2]
    return call(
        functools.partial(packed_kernel, sizes=sizes),
        (sds((rows, width)), sds((rows, 3 * width))),
        (3,),
        sizes.raw(width)
        + [whole(gains), whole(shifts), pl.BlockSpec((width, width), lambda i, info: (0, i))],
        (sizes.all(width), sizes.cols(width)),
        6 * rows * width * width,
        rows * width * 10 + 6 * width * width,
        name="encoder_packed",
    )(info, *[x] * sizes.strips, gains, shifts, w_qkv)


def picker_of(source_ref, strip):
    taken = source_ref[pl.ds(strip, 1), :]
    length = taken.shape[1]
    return low(jnp.where(taken == lax.broadcasted_iota(jnp.int32, (length, length), 0), 1.0, 0.0))


def last_row(length):
    return lax.broadcasted_iota(jnp.int32, (length, 1), 0) == length - 1


def decoder_in_kernel(
    info_ref,
    rows_ref,
    source_ref,
    mask_ref,
    places_ref,
    gain_ref,
    shift_ref,
    w_ref,
    x_ref,
    n_ref,
    packed_ref,
    *,
    sizes
):
    @first_step
    def gather():
        for strip in range(sizes.strips):
            place = sizes.place(strip)
            picker = picker_of(source_ref, info_ref[STRIP + strip])
            rows = jnp.where(
                last_row(sizes.padded), vector_of(mask_ref), rows_ref[place, :].astype(jnp.float32)
            )
            x = dot(picker, low(rows), TN) + places_ref[...]
            x_ref[place, :] = x
            normed, _, _ = norm(x, row_of(gain_ref, 0), row_of(shift_ref, 0))
            n_ref[place, :] = low(normed)

    packed_ref[...] = low(dot(n_ref[...], w_ref[...], NN))


def decoder_in_call(sizes, info, projected, source, mask_row, places, gains, shifts, w_qkv):
    width = projected.shape[1]
    rows = sizes.rows
    return call(
        functools.partial(decoder_in_kernel, sizes=sizes),
        (sds((rows, width), jnp.float32), sds((rows, width)), sds((rows, 3 * width))),
        (3,),
        [sizes.all(width), whole(source), whole(mask_row), whole(places), whole(gains), whole(shifts)]
        + [pl.BlockSpec((width, width), lambda i, info: (0, i))],
        (sizes.all(width), sizes.all(width), sizes.cols(width)),
        6 * rows * width * width + 2 * rows * sizes.padded * width,
        rows * width * 18 + 6 * width * width,
        name="decoder_packed",
    )(info, projected, source, mask_row, places, gains, shifts, w_qkv)


def head_parts(head, heads_here):
    lane = lax.broadcasted_iota(jnp.int32, (1, GROUP), 1)
    size = GROUP // heads_here
    mine = (lane >= head * size) & (lane < (head + 1) * size)
    spare = ((head + 1) % heads_here) * size
    return mine, lane == spare, spare


def key_bias(live, length):
    row = lax.broadcasted_iota(jnp.int32, (length, 1), 0)
    return low(jnp.where(row < live, 0.0, MASKED))


def attend_kernel(info_ref, q_ref, k_ref, v_ref, out_ref, *, heads_here, live):
    length = q_ref.shape[1]
    rate = (GROUP // heads_here) ** -0.5 * LOG2E
    bias = key_bias(live(info_ref, pl.program_id(0)), length)
    one = jnp.bfloat16(1.0)
    half = length // 2
    for start in range(0, q_ref.shape[2], GROUP):
        group = slice(start, start + GROUP)
        k, v = k_ref[0, :, group], v_ref[0, :, group]
        for begin in range(0, length, half):
            q = q_ref[0, begin : begin + half, group]
            mixed = jnp.zeros((half, GROUP), jnp.float32)
            for head in range(heads_here):
                mine, at_spare, spare = head_parts(head, heads_here)
                head_q = jnp.where(mine, q, low(jnp.where(at_spare, 1.0, 0.0)))
                scores = dot(head_q, jnp.where(at_spare, bias, k), NT)
                highest = jnp.max(scores, axis=1, keepdims=True)
                terms = low(jnp.exp2((scores - highest) * rate))
                product = dot(terms, jnp.where(at_spare, one, v), NN)
                total = product[:, spare : spare + 1]
                mixed = jnp.where(mine, product * (1.0 / total), mixed)
            out_ref[0, begin : begin + half, group] = low(mixed)


def all_live(length):
    return lambda info_ref, strip: length


def visible_live(strips):
    return lambda info_ref, strip: info_ref[STRIP + strips + strip]


def attend_call(packed, info, heads, live, name):
    strips, length, triple = packed.shape
    width = triple // 3
    heads_here = GROUP // (width // heads)
    groups = 2
    part = width // groups
    third = lambda j: pl.BlockSpec((1, length, part), lambda s, g, _: (s, 0, g + j * groups))
    return call(
        functools.partial(attend_kernel, heads_here=heads_here, live=live),
        sds((strips, length, width)),
        (strips, groups),
        [third(0), third(1), third(2)],
        third(0),
        strips * heads * length * length * GROUP * 6,
        strips * length * width * 8,
        exps=strips * heads * length * length,
        name=name,
    )(info, packed, packed, packed)


def attend_back_kernel(
    info_ref,
    q_ref,
    k_ref,
    v_ref,
    dout_ref,
    n_ref,
    grad_ref,
    kept_ref,
    sent_ref,
    total_ref,
    *,
    heads_here,
    live
):
    length = q_ref.shape[1]
    factor = (GROUP // heads_here) ** -0.5
    rate = factor * LOG2E
    strip = pl.program_id(1)
    q, k, v, dout = q_ref[0], k_ref[0], v_ref[0], dout_ref[0]
    bias = key_bias(live(info_ref, strip), length)
    k_turned = k.T
    dq_turned = []
    dk = jnp.zeros((length, GROUP), jnp.float32)
    dv = jnp.zeros((length, GROUP), jnp.float32)
    size = GROUP // heads_here
    for head in range(heads_here):
        mine, at_spare, _ = head_parts(head, heads_here)
        head_q = jnp.where(mine, q, low(jnp.where(at_spare, 1.0, 0.0)))
        head_dout = jnp.where(mine, dout, jnp.bfloat16(0.0))
        scores = dot(jnp.where(at_spare, bias, k), head_q, NT)
        highest = jnp.max(scores, axis=0, keepdims=True)
        terms = jnp.exp2((scores - highest) * rate)
        probs = terms * (1.0 / jnp.sum(terms, axis=0, keepdims=True))
        weighted = probs * dot(v, head_dout, NT)
        dscores = low(weighted - probs * jnp.sum(weighted, axis=0, keepdims=True))
        dk = jnp.where(mine, dot(dscores, q, NN), dk)
        dv = jnp.where(mine, dot(low(probs), dout, NN), dv)
        dq_turned.append(dot(k_turned[head * size : (head + 1) * size], dscores, NN))
    dq = low(jnp.concatenate(dq_turned, axis=0).T * factor)
    dk, dv = low(dk * factor), low(dv)
    grad_ref[0, 0] = dq
    grad_ref[1, 0] = dk
    grad_ref[2, 0] = dv
    term = dot(n_ref[0], jnp.concatenate([dq, dk, dv], axis=1), TN)
    half = kept_ref.shape[0]
    last = pl.num_programs(1) - 1

    @pl.when(strip == 0)
    def begin():
        total_ref[...] = term

    @pl.when(strip > 0)
    def more():
        total_ref[...] += term

    @pl.when(strip == last)
    def finish():
        kept_ref[...] = low(total_ref[pl.ds(pl.multiple_of(info_ref[0] * half, 8), half), :])
        sent_ref[...] = low(total_ref[pl.ds(pl.multiple_of((1 - info_ref[0]) * half, 8), half), :])


def attend_back_call(packed, dmixed, normed, info, heads, live, part, parts, after, name):
    strips, length, triple = packed.shape
    width = triple // 3
    heads_here = GROUP // (width // heads)
    groups = width // GROUP
    here = groups // parts
    third = lambda j: pl.BlockSpec(
        (1, length, GROUP), lambda g, s, _: (s, 0, g + part * here + j * groups)
    )
    product = pl.BlockSpec((width // 2, 3 * GROUP), lambda g, s, _: (0, g))
    return call(
        functools.partial(attend_back_kernel, heads_here=heads_here, live=live),
        (
            sds((3, strips, length, here * GROUP)),
            sds((width // 2, here * 3 * GROUP)),
            sds((width // 2, here * 3 * GROUP)),
        ),
        (here, strips),
        [
            third(0),
            third(1),
            third(2),
            third(0),
            pl.BlockSpec((1, length, width), lambda g, s, _: (s, 0, 0)),
        ],
        (pl.BlockSpec((3, 1, length, GROUP), lambda g, s, _: (0, s, 0, g)), product, product),
        (strips * heads * length * length * GROUP * 12 + 6 * strips * length * width * width) // parts,
        strips * length * width * 14 // parts,
        exps=strips * heads * length * length // parts,
        after=after,
        name=name,
        scratch=[pltpu.VMEM((width, 3 * GROUP), jnp.float32)],
    )(info, packed, packed, packed, dmixed, normed)


def encoder_ff_kernel(info_ref, *refs, sizes):
    x_refs = refs[: sizes.strips]
    (
        mixed_ref,
        gain_ref,
        shift_ref,
        w_out_ref,
        bias_out_ref,
        w_up_ref,
        bias_up_ref,
        w_down_ref,
        w_proj_ref,
        bias_proj_ref,
        mid_ref,
        n_ref,
        act_ref,
        slope_ref,
        y_low_ref,
        encoded_ref,
        projected_ref,
        y_ref,
        bias_ref,
    ) = refs[sizes.strips :]
    places = [sizes.place(strip) for strip in range(sizes.strips)]

    @first_step
    def middle():
        bias_ref[...] = vector_of(bias_up_ref)
        for place, x_ref in zip(places, x_refs):
            x = live_rows(x_ref[...], 0, sizes.length)
            mid = x + dot(mixed_ref[place, :], w_out_ref[...], NN) + row_of(bias_out_ref, 0)
            mid_ref[place, :] = low(mid)
            normed, _, _ = norm(mid, row_of(gain_ref, 1), row_of(shift_ref, 1))
            n_ref[place, :] = low(normed)
            y_ref[place, :] = mid + row_of(bias_out_ref, 1)

    chunk = w_up_ref.shape[1]
    bias = bias_ref[:, pl.ds(pl.multiple_of(pl.program_id(0) * chunk, GROUP), chunk)]
    hidden = [dot(n_ref[place, :], w_up_ref[...], NN) + bias for place in places]
    for place, values in zip(places, hidden):
        act, slope = gelu_parts(values)
        act = low(act)
        act_ref[place, :] = act
        slope_ref[place, :] = low(slope)
        y_ref[place, :] += dot(act, w_down_ref[...], NN)

    @last_step
    def finish():
        for place in places:
            y = y_ref[place, :]
            y_low_ref[place, :] = low(y)
            encoded, _, _ = norm(y, row_of(gain_ref, 2), row_of(shift_ref, 2))
            encoded = low(encoded)
            encoded_ref[place, :] = encoded
            projected_ref[place, :] = low(
                dot(encoded, w_proj_ref[...], NN) + vector_of(bias_proj_ref)
            )


def encoder_ff_call(
    sizes, info, x, mixed, gains, shifts, w_out, bias_out, w_up, bias_up, w_down, w_proj, bias_proj
):
    rows, width = sizes.rows, x.shape[2]
    units = w_up.shape[1]
    narrow = w_proj.shape[1]
    chunk = units // 4
    return call(
        functools.partial(encoder_ff_kernel, sizes=sizes),
        (
            sds((rows, width)),
            sds((rows, width)),
            sds((rows, units)),
            sds((rows, units)),
            sds((rows, width)),
            sds((rows, width)),
            sds((rows, narrow)),
        ),
        (4,),
        sizes.raw(width)
        + [sizes.all(width)]
        + [whole(w) for w in (gains, shifts, w_out, bias_out)]
        + [
            pl.BlockSpec((width, chunk), lambda i, info: (0, i)),
            whole(bias_up),
            pl.BlockSpec((chunk, width), lambda i, info: (i, 0)),
            whole(w_proj),
            whole(bias_proj),
        ],
        (
            sizes.all(width),
            sizes.all(width),
            sizes.cols(chunk),
            sizes.cols(chunk),
            sizes.all(width),
            sizes.all(width),
            sizes.all(narrow),
        ),
        2 * rows * width * (width + 2 * units + narrow),
        rows * (width * 16 + units * 4) + 2 * width * (width + 2 * units + narrow),
        exps=rows * units,
        name="encoder_feed_forward",
        scratch=[pltpu.VMEM((rows, width), jnp.float32), pltpu.VMEM((1, units), jnp.float32)],
    )(
        info,
        *[x] * sizes.strips,
        mixed,
        gains,
        shifts,
        w_out,
        bias_out,
        w_up,
        bias_up,
        w_down,
        w_proj,
        bias_proj,
    )


def decoder_ff_kernel(info_ref, *refs, sizes, folds, share, units):
    cot_refs = refs[: sizes.strips]
    (
        x_ref,
        mixed_ref,
        gain_ref,
        shift_ref,
        w_out_ref,
        bias_out_ref,
        w_up_ref,
        bias_up_ref,
        w_down_ref,
        kept_ref,
        sent_ref,
        gb_ref,
        dmixed_ref,
        sums_ref,
        up_sums_ref,
        kept_up_ref,
        sent_up_ref,
        *down_refs,
        cot_ref,
        n_ref,
        act_ref,
        dhidden_ref,
        mid_ref,
        y_ref,
        dnormed_ref,
        bias_ref,
        beside_ref,
        down_ref,
    ) = refs[sizes.strips :]
    places = [sizes.place(strip) for strip in range(sizes.strips)]
    gain, shift = row_of(gain_ref, 1), row_of(shift_ref, 1)

    @first_step
    def middle():
        bias_ref[...] = vector_of(bias_up_ref)
        dnormed_ref[...] = jnp.zeros_like(dnormed_ref)
        for place, cot_here in zip(places, cot_refs):
            mid = x_ref[place, :] + dot(mixed_ref[place, :], w_out_ref[...], NN) + row_of(bias_out_ref, 0)
            mid_ref[place, :] = mid
            normed, _, _ = norm(mid, gain, shift)
            n_ref[place, :] = low(normed)
            y_ref[place, :] = mid + row_of(bias_out_ref, 1)
            cot_ref[place, :] = low(live_rows(cot_here[...], 0, sizes.length))

    chunk = w_up_ref.shape[1]
    bias = bias_ref[:, pl.ds(pl.multiple_of(pl.program_id(0) * chunk, GROUP), chunk)]
    hidden = [dot(n_ref[place, :], w_up_ref[...], NN) + bias for place in places]
    dact = [dot(cot_ref[place, :], w_down_ref[...], NT) for place in places]
    up_sums = jnp.zeros((1, chunk), jnp.float32)
    for place, values, grads in zip(places, hidden, dact):
        act, slope = gelu_parts(values)
        act = low(act)
        act_ref[place, :] = act
        y_ref[place, :] += dot(act, w_down_ref[...], NN)
        dhidden = low(grads * slope)
        dhidden_ref[place, :] = dhidden
        up_sums = up_sums + col_sum(dhidden.astype(jnp.float32))
        dnormed_ref[place, :] += dot(dhidden, w_up_ref[...], NT)
    up_sums_ref[0:1, :] = up_sums
    step, width = pl.program_id(0), n_ref.shape[1]
    beside_ref[:, pl.ds(pl.multiple_of(step * chunk, GROUP), chunk)] = low(
        dot(n_ref[...], dhidden_ref[...], TN)
    )
    down = dot(act_ref[...], cot_ref[...], TN)
    if folds:
        down = down.reshape(-1, folds, share, width)
        here = chunk // folds
        rows = pl.ds(pl.multiple_of(step * here, share), here)
        for fold in range(folds):
            start = (folds + 1 + fold) * width
            beside_ref[rows, start : start + width] = low(down[:, fold].reshape(here, width))
    else:
        down_ref[pl.ds(pl.multiple_of(step * chunk, GROUP), chunk), :] = low(down)

    @last_step
    def finish():
        totals = []
        for strip, place in enumerate(places):
            store_halves(info_ref, kept_ref.at[strip], sent_ref.at[strip], y_ref[place, :])
            _, unit, inverse = norm(mid_ref[place, :], gain, shift)
            grad = cot_ref[place, :].astype(jnp.float32)
            dnormed = dnormed_ref[place, :]
            gb = low(grad + norm_back(dnormed, unit, inverse, gain))
            gb_ref[place, :] = gb
            dmixed_ref[place, :] = low(dot(gb, w_out_ref[...], NT))
            totals.append(
                (
                    col_sum(dnormed * unit),
                    col_sum(dnormed),
                    col_sum(gb.astype(jnp.float32)),
                    col_sum(grad),
                )
            )
        set_rows(sums_ref, [sum(rows) for rows in zip(*totals)])
        beside_ref[:, units : units + width] = low(dot(mixed_ref[...], gb_ref[...], TN))
        for kept, sent, whole_ref in zip(
            (kept_up_ref, *down_refs[:1]), (sent_up_ref, *down_refs[1:]), (beside_ref, down_ref)
        ):
            half = kept.shape[0]
            kept[...] = whole_ref[pl.ds(pl.multiple_of(info_ref[0] * half, 16), half), :]
            sent[...] = whole_ref[pl.ds(pl.multiple_of((1 - info_ref[0]) * half, 16), half), :]


def decoder_ff_call(
    sizes, info, x, mixed, cot, gains, shifts, w_out, bias_out, w_up, bias_up, w_down, share
):
    rows, width = x.shape
    units = w_up.shape[1]
    chunk = units // 4
    all_rows = sizes.all(width)
    half = sds((sizes.strips, sizes.length, width // 2))
    up_sums = pl.BlockSpec((8, chunk), lambda i, info: (0, i))
    folds = units // width if share % 8 == 0 else 0
    beside = units + width + (units if folds else 0)
    halves = [(width // 2, beside)] * 2 + ([] if folds else [(units // 2, width)] * 2)
    return call(
        functools.partial(decoder_ff_kernel, sizes=sizes, folds=folds, share=share, units=units),
        (
            half,
            half,
            sds((rows, width)),
            sds((rows, width)),
            sds((8, width), jnp.float32),
            sds((8, units), jnp.float32),
            *[sds(shape) for shape in halves],
        ),
        (4,),
        sizes.raw(width)
        + [all_rows, all_rows]
        + [whole(w) for w in (gains, shifts, w_out, bias_out)]
        + [
            pl.BlockSpec((width, chunk), lambda i, info: (0, i)),
            whole(bias_up),
            pl.BlockSpec((chunk, width), lambda i, info: (i, 0)),
        ],
        (
            sizes.half(width // 2),
            sizes.half(width // 2),
            all_rows,
            all_rows,
            sizes.sums(width),
            up_sums,
            *[pl.BlockSpec(shape, lambda i, info: (0, 0)) for shape in halves],
        ),
        2 * rows * width * (3 * width + 6 * units),
        rows * width * 16 + 4 * width * (width + 2 * units),
        exps=rows * units,
        name="decoder_feed_forward",
        scratch=[
            pltpu.VMEM((rows, width), jnp.bfloat16),
            pltpu.VMEM((rows, width), jnp.bfloat16),
            pltpu.VMEM((rows, chunk), jnp.bfloat16),
            pltpu.VMEM((rows, chunk), jnp.bfloat16),
            pltpu.VMEM((rows, width), jnp.float32),
            pltpu.VMEM((rows, width), jnp.float32),
            pltpu.VMEM((rows, width), jnp.float32),
            pltpu.VMEM((1, units), jnp.float32),
            pltpu.VMEM((width, beside), jnp.bfloat16),
            pltpu.VMEM((16 if folds else units, width), jnp.bfloat16),
        ],
    )(info, *[cot] * sizes.strips, x, mixed, gains, shifts, w_out, bias_out, w_up, bias_up, w_down)


def encoder_ff_back_kernel(
    info_ref,
    grad_ref,
    mid_ref,
    slope_ref,
    gain_ref,
    shift_ref,
    w_out_ref,
    w_up_ref,
    w_down_ref,
    dhidden_ref,
    gb_ref,
    dmixed_ref,
    sums_ref,
    up_sums_ref,
    dnormed_ref,
    *,
    sizes
):
    places = [sizes.place(strip) for strip in range(sizes.strips)]

    @first_step
    def begin():
        dnormed_ref[...] = jnp.zeros_like(dnormed_ref)

    dact = [dot(grad_ref[place, :], w_down_ref[...], NT) for place in places]
    up_sums = jnp.zeros((1, w_up_ref.shape[1]), jnp.float32)
    for place, values in zip(places, dact):
        dhidden = low(values * slope_ref[place, :].astype(jnp.float32))
        dhidden_ref[place, :] = dhidden
        up_sums = up_sums + col_sum(dhidden.astype(jnp.float32))
        dnormed_ref[place, :] += dot(dhidden, w_up_ref[...], NT)
    up_sums_ref[0:1, :] = up_sums

    @last_step
    def finish():
        gain, shift = row_of(gain_ref, 1), row_of(shift_ref, 1)
        totals = []
        for place in places:
            _, unit, inverse = norm(mid_ref[place, :].astype(jnp.float32), gain, shift)
            grad = grad_ref[place, :].astype(jnp.float32)
            dnormed = dnormed_ref[place, :]
            gb = low(grad + norm_back(dnormed, unit, inverse, gain))
            gb_ref[place, :] = gb
            dmixed_ref[place, :] = low(dot(gb, w_out_ref[...], NT))
            totals.append(
                (
                    col_sum(dnormed * unit),
                    col_sum(dnormed),
                    col_sum(gb.astype(jnp.float32)),
                    col_sum(grad),
                )
            )
        set_rows(sums_ref, [sum(rows) for rows in zip(*totals)])


def encoder_ff_back_call(sizes, info, grad, mid, slope, gains, shifts, w_out, w_up, w_down, after):
    rows, width = grad.shape
    units = w_up.shape[1]
    chunk = units // 4
    all_rows, cols = sizes.all(width), sizes.cols(chunk)
    return call(
        functools.partial(encoder_ff_back_kernel, sizes=sizes),
        (
            sds((rows, units)),
            sds((rows, width)),
            sds((rows, width)),
            sds((8, width), jnp.float32),
            sds((8, units), jnp.float32),
        ),
        (4,),
        [all_rows, all_rows, cols, whole(gains), whole(shifts), whole(w_out)]
        + [
            pl.BlockSpec((width, chunk), lambda i, info: (0, i)),
            pl.BlockSpec((chunk, width), lambda i, info: (i, 0)),
        ],
        (
            cols,
            all_rows,
            all_rows,
            sizes.sums(width),
            pl.BlockSpec((8, chunk), lambda i, info: (0, i)),
        ),
        2 * rows * width * (width + 2 * units),
        rows * (width * 16 + units * 4) + 2 * width * (width + 2 * units),
        after=after,
        name="encoder_feed_forward_back",
        scratch=[pltpu.VMEM((rows, width), jnp.float32)],
    )(info, grad, mid, slope, gains, shifts, w_out, w_up, w_down)


def packed_back(grad_ref, w_ref):
    width = w_ref.shape[0]
    return sum(dot(grad_ref[j], w_ref[:, j * width : (j + 1) * width], NT) for j in range(3))


def decoder_back_kernel(
    info_ref,
    dpacked_ref,
    gm_ref,
    x_ref,
    source_ref,
    y_ref,
    encoded_ref,
    gain_ref,
    shift_ref,
    w_ref,
    w_proj_ref,
    enc_gain_ref,
    enc_shift_ref,
    grad_ref,
    sums_ref,
    enc_sums_ref,
    kept_ref,
    sent_ref,
    total_ref,
):
    dnormed = packed_back(dpacked_ref, w_ref)
    gain = row_of(gain_ref, 0)
    _, unit, inverse = norm(x_ref[...], gain, row_of(shift_ref, 0))
    dx = gm_ref[...].astype(jnp.float32) + norm_back(dnormed, unit, inverse, gain)
    picker = picker_of(source_ref, info_ref[STRIP + pl.program_id(0)])
    taken = dot(picker, low(dx), NN)
    last = taken.shape[0] - 1
    dproj = low(jnp.where(last_row(taken.shape[0]), 0.0, taken))
    term = dot(encoded_ref[...], dproj, TN)
    half = kept_ref.shape[0]

    @pl.when(pl.program_id(0) == 0)
    def begin():
        total_ref[...] = term

    @pl.when(pl.program_id(0) > 0)
    def more():
        total_ref[...] += term

    @pl.when(pl.program_id(0) == pl.num_programs(0) - 1)
    def finish():
        kept_ref[...] = low(total_ref[pl.ds(pl.multiple_of(info_ref[0] * half, 8), half), :])
        sent_ref[...] = low(total_ref[pl.ds(pl.multiple_of((1 - info_ref[0]) * half, 8), half), :])

    dencoded = low(dot(dproj, w_proj_ref[...], NT)).astype(jnp.float32)
    enc_gain = row_of(enc_gain_ref, 2)
    _, unit_final, inverse_final = norm(
        y_ref[...].astype(jnp.float32), enc_gain, row_of(enc_shift_ref, 2)
    )
    grad_ref[...] = low(norm_back(dencoded, unit_final, inverse_final, enc_gain))
    add_rows(
        sums_ref,
        (
            col_sum(dnormed * unit),
            col_sum(dnormed),
            taken[last : last + 1],
            col_sum(dproj.astype(jnp.float32)),
        ),
    )
    add_rows(enc_sums_ref, (col_sum(dencoded * unit_final), col_sum(dencoded)))


def decoder_back_call(
    sizes,
    info,
    dpacked,
    gm,
    x,
    source,
    y,
    encoded,
    gains,
    shifts,
    w_qkv,
    w_proj,
    enc_gains,
    enc_shifts,
    after,
):
    strips, padded, rows = sizes.strips, sizes.padded, sizes.rows
    width = x.shape[2]
    wide = y.shape[2]
    weights = (gains, shifts, w_qkv, w_proj, enc_gains, enc_shifts)
    strip = sizes.strip
    return call(
        decoder_back_kernel,
        (
            sds((strips, padded, wide)),
            sds((8, width), jnp.float32),
            sds((8, wide), jnp.float32),
            sds((wide // 2, width)),
            sds((wide // 2, width)),
        ),
        (strips, 1),
        [
            pl.BlockSpec((3, None, padded, width), lambda s, i, info: (0, s, 0, 0)),
            strip(width),
            strip(width),
            whole(source),
            strip(wide),
            strip(wide),
        ]
        + [whole(w) for w in weights],
        (
            strip(wide),
            sizes.sums(width),
            sizes.sums(wide),
            pl.BlockSpec((wide // 2, width), lambda s, i, info: (0, 0)),
            pl.BlockSpec((wide // 2, width), lambda s, i, info: (0, 0)),
        ),
        2 * rows * width * (3 * width + padded + 2 * wide),
        rows * (width * 16 + wide * 8) + 2 * width * (3 * width + wide),
        after=after,
        name="decoder_packed_back",
        scratch=[pltpu.VMEM((wide, width), jnp.float32)],
    )(info, dpacked, gm, x, source, y, encoded, *weights)


def encoder_back_kernel(info_ref, *refs, parts, length):
    grad_refs, w_refs = refs[:parts], refs[parts : 2 * parts]
    gb_ref, x_ref, gain_ref, shift_ref, kept_ref, sent_ref, sums_ref, dnormed_ref = refs[2 * parts :]
    term = sum(dot(grad_ref[...], w_ref[...], NT) for grad_ref, w_ref in zip(grad_refs, w_refs))

    @first_step
    def begin():
        dnormed_ref[...] = term

    @pl.when(pl.program_id(0) > 0)
    def more():
        dnormed_ref[...] += term

    @last_step
    def finish():
        dnormed = dnormed_ref[...]
        gain = row_of(gain_ref, 0)
        x = live_rows(x_ref[...], 0, length)
        _, unit, inverse = norm(x, gain, row_of(shift_ref, 0))
        dx = gb_ref[...].astype(jnp.float32) + norm_back(dnormed, unit, inverse, gain)
        store_halves(info_ref, kept_ref, sent_ref, dx)
        set_rows(sums_ref, (col_sum(dnormed * unit), col_sum(dnormed)))


def encoder_back_call(sizes, info, dpacked, gb, x, gains, shifts, w_qkv, strip, after):
    rows, width = gb.shape
    padded = sizes.padded
    half = sds((1, sizes.length, width // 2))
    parts = len(dpacked)
    here = width // parts
    half_spec = pl.BlockSpec((None, padded, width // 2), lambda j, info: (0, 0, 0))
    return call(
        functools.partial(encoder_back_kernel, parts=parts, length=sizes.length),
        (half, half, sds((8, width), jnp.float32)),
        (3,),
        [pl.BlockSpec((None, None, padded, here), lambda j, info: (j, strip, 0, 0))] * parts
        + [
            pl.BlockSpec((width, here), lambda j, info, part=part: (0, j * parts + part))
            for part in range(parts)
        ]
        + [
            pl.BlockSpec((padded, width), lambda j, info: (strip, 0)),
            sizes.raw(width)[strip],
            whole(gains),
            whole(shifts),
        ],
        (half_spec, half_spec, sizes.sums(width)),
        6 * rows * width * width // sizes.strips,
        rows * width * 12 // sizes.strips + 6 * width * width,
        after=after,
        name=f"encoder_packed_back_{strip}",
        scratch=[pltpu.VMEM((padded, width), jnp.float32)],
    )(info, *dpacked, *[w_qkv] * parts, gb, x, gains, shifts)


class Job:
    def __init__(self, left, right, row_step, col_step, offset):
        self.half = left.shape[1] // 2
        self.width = right.shape[1]
        self.rows = left.shape[0]
        self.row_step, self.col_step, self.offset = row_step, col_step, offset
        self.down = self.half // row_step
        self.across = self.width // col_step
        self.count = self.down * self.across

    def at(self, step):
        here = jnp.clip(step - self.offset, 0, self.count - 1)
        if self.across == 1:
            return here, 0
        if self.down == 1:
            return 0, here
        return here // self.across, here % self.across

    def left(self, pick):
        return pl.BlockSpec(
            (self.rows, self.row_step),
            lambda step, info: (0, pick(info[0]) * self.down + self.at(step)[0]),
        )

    def right(self):
        return pl.BlockSpec((self.rows, self.col_step), lambda step, info: (0, self.at(step)[1]))

    def out(self):
        return pl.BlockSpec((self.row_step, self.col_step), lambda step, info: self.at(step))


def product_kernel(info_ref, *refs, jobs):
    step = pl.program_id(0)
    out = 3 * len(jobs)
    for place, (offset, count) in enumerate(jobs):
        mine_ref, other_ref, right_ref = refs[3 * place : 3 * place + 3]
        kept_ref, sent_ref = refs[out + 2 * place : out + 2 * place + 2]

        @pl.when((step >= offset) & (step < offset + count))
        def product():
            right = right_ref[...]
            sent_ref[...] = low(dot(other_ref[...], right, TN))
            kept_ref[...] = low(dot(mine_ref[...], right, TN))


def product_call(info, products, name, after=()):
    jobs, operands, in_specs, out_specs, out_shape = [], [], [], [], []
    offset = flops = moved = 0
    for left, right, row_step, col_step in products:
        job = Job(left, right, row_step, col_step, offset)
        offset += job.count
        jobs.append(job)
        operands += [left, left, right]
        in_specs += [job.left(lambda own: own), job.left(lambda own: 1 - own), job.right()]
        out_specs += [job.out(), job.out()]
        out_shape += [sds((job.half, job.width))] * 2
        flops += 4 * job.rows * job.half * job.width
        moved += 2 * job.rows * (2 * job.half + job.width) + 4 * job.half * job.width
    outs = call(
        functools.partial(product_kernel, jobs=[(job.offset, job.count) for job in jobs]),
        tuple(out_shape),
        (offset,),
        in_specs,
        tuple(out_specs),
        flops,
        moved,
        after=after,
        name=name,
    )(info, *operands)
    return [outs[2 * place : 2 * place + 2] for place in range(len(jobs))]


class Chain:
    def __init__(self, pairs, order, parts):
        self.pairs = pairs
        self.bits = list(range(pairs.bit_length() - 1))
        self.order = [bit for bit in order if bit < len(self.bits)]
        self.order += [bit for bit in self.bits if bit not in self.order]
        self.parts, self.widths = [], []
        for kept, arrived in parts:
            width = kept.shape[1]
            self.widths.append(width)
            self.parts.append(tuple(array.reshape(pairs, -1, width) for array in (kept, arrived)))
        self.done = None

    def item(self):
        kept = self.parts[0][0]
        if not self.order:
            return ("last", self.parts, self.widths, None)
        bit = self.order[0]
        lower = sum(1 for other in self.bits if other < bit)
        return ("halve", self.parts, (kept.shape[0] >> (lower + 1), 1 << lower), bit)

    def take(self, outs):
        if not self.order:
            self.done = outs
            return []
        bit = self.order.pop(0)
        self.bits.remove(bit)
        kept, sent = outs
        route = [(place, place ^ (1 << bit)) for place in range(self.pairs)]
        self.parts = [(kept, lax.ppermute(sent, "dp", route))]
        return [sent]


class Total:
    def __init__(self, pairs, values):
        self.pairs = pairs
        bits = [1 << bit for bit in range((2 * pairs).bit_length() - 1)]
        self.left = [bits[-1:]] + [bits[place : place + 2] for place in range(0, len(bits) - 1, 2)]
        self.done = None
        self.launch(values)

    def launch(self, values):
        group = self.left.pop(0)
        masks = group + [sum(group)] if len(group) > 1 else group
        count = 2 * self.pairs
        arrived = [
            lax.ppermute(values, ("section", "dp"), [(place, place ^ mask) for place in range(count)])
            for mask in masks
        ]
        self.parts = [(values, *arrived)]
        self.sent = values

    def item(self):
        return ("add", self.parts, None, None)

    def take(self, outs):
        (values,) = outs
        if not self.left:
            self.done = values
            return []
        self.launch(values)
        return [values]


def in_thirds(kind, parts):
    return kind == "halve" and len(parts) == 1 and parts[0][0].shape[-1] % (3 * GROUP) == 0


def round_kernel(info_ref, *refs, items):
    place = 0
    out = sum(sum(widths) for _, widths, _, _, _, _ in items)
    for kind, widths, how, bit, count, split in items:
        pairs = []
        for width in widths:
            pairs.append(refs[place : place + width])
            place += width
        outs = refs[out : out + count]
        out += count
        run = functools.partial(round_item, info_ref, kind, pairs, how, bit, outs)
        if split:
            run()
        else:
            first_step(run)


def round_item(info_ref, kind, pairs, how, bit, outs):
    if kind == "add":
        outs[0][...] = sum(ref[...] for ref in pairs[0])
        return

    def total(pair, index):
        return pair[0][index].astype(jnp.float32) + pair[1][index].astype(jnp.float32)

    if kind == "last":
        start = 0
        values = [total(pair, 0) for pair in pairs]
        whole_row = values[0] if len(values) == 1 else jnp.concatenate(values, axis=1)
        for ref, width in zip(outs, how):
            ref[...] = whole_row[:, start : start + width]
            start += width
        return
    high, lower = how
    mine = (info_ref[BLOCK] >> bit) & 1
    for h in range(high):
        for l in range(lower):
            start = 0
            for pair in pairs:
                width = pair[0].shape[-1]
                for ref, chosen in zip(outs, (mine, 1 - mine)):
                    index = (h * 2 + chosen) * lower + l
                    ref[h * lower + l, :, start : start + width] = low(total(pair, index))
                start += width


def round_call(info, chains, name, after=(), through=()):
    items = [chain.item() for chain in chains]
    operands, specs, out_shape, out_specs, plain, counts, moved = [], [], [], [], [], [], 0
    for kind, parts, how, bit in items:
        split = in_thirds(kind, parts)
        for part in parts:
            operands += part
            moved += len(part) * part[0].size * part[0].dtype.itemsize
            if split:
                block = (*part[0].shape[:-1], part[0].shape[-1] // 3)
                specs += [pl.BlockSpec(block, lambda i, info: (0, 0, i))] * len(part)
            else:
                specs += [whole(array) for array in part]
        shape = parts[0][0].shape
        if kind == "add":
            shapes = [sds(shape, jnp.float32)]
        elif kind == "last":
            shapes = [sds((shape[1], width), jnp.float32) for width in how]
        else:
            width = sum(part[0].shape[-1] for part in parts)
            shapes = [sds((shape[0] // 2, shape[1], width))] * 2
        out_shape += shapes
        if split:
            out_specs += [
                pl.BlockSpec((*shape.shape[:-1], shape.shape[-1] // 3), lambda i, info: (0, 0, i))
                for shape in shapes
            ]
        else:
            out_specs += [whole(shape) for shape in shapes]
        counts.append(len(shapes))
        plain.append((kind, [len(part) for part in parts], how, bit, len(shapes), split))
    outs = call(
        functools.partial(round_kernel, items=plain),
        tuple(out_shape),
        (3 if any(item[-1] for item in plain) else 1,),
        specs,
        tuple(out_specs),
        moved,
        2 * moved,
        after=after,
        through=through,
        name=name,
    )(info, *operands)
    sent, start = [], 0
    for chain, count in zip(chains, counts):
        sent += chain.take(outs[start : start + count])
        start += count
    return sent, outs[start:]


def across(values):
    return lax.ppermute(values, "section", [(0, 1), (1, 0)])


def arrange_kernel(info_ref, *refs, strips):
    *sources, out_ref = refs
    holder = info_ref[STRIP + 2 * strips + pl.program_id(0)]
    slot = info_ref[STRIP + 4 * strips + pl.program_id(0)]
    per = len(sources) // 2
    values = None
    for place in range(strips):
        kept, arrived = (
            (sources[place][0], sources[per + place][0])
            if per == strips
            else (sources[0][place], sources[1][place])
        )
        chosen = jnp.where(holder == info_ref[0], kept, arrived)
        values = chosen if values is None else jnp.where(slot == place, chosen, values)
    out_ref[0] = values


def arrange_call(info, kept, arrived, strips, name, after=()):
    _, length, half = kept[0].shape
    return call(
        functools.partial(arrange_kernel, strips=strips),
        sds((2 * strips, length, half)),
        (2 * strips,),
        [whole(array) for array in (*kept, *arrived)],
        pl.BlockSpec((1, length, half), lambda k, info: (k, 0, 0)),
        1,
        strips * length * half * 12,
        name=name,
        after=after,
    )(info, *kept, *arrived)


def gather_small_kernel(
    info_ref, up_enc, up_dec, enc, dec, dec_in, final, *rest
):
    *enc_in, out_ref = rest
    out_ref[...] = jnp.zeros_like(out_ref)
    wide, narrow = enc.shape[1], dec.shape[1]
    out_ref[0:1, : up_enc.shape[1]] = up_enc[0:1, :]
    out_ref[1:2, : up_dec.shape[1]] = up_dec[0:1, :]
    out_ref[2:6, :wide] = enc[0:4, :]
    out_ref[2:6, wide : wide + narrow] = dec[0:4, :]
    out_ref[2:6, wide + narrow : wide + 2 * narrow] = dec_in[0:4, :]
    out_ref[6:8, :wide] = final[0:2, :]
    out_ref[6:8, wide : 2 * wide] = sum(ref[0:2, :] for ref in enc_in)


def gather_small_call(info, values):
    shape = (8, values[0].shape[1])
    return call(
        gather_small_kernel,
        sds(shape, jnp.float32),
        (1,),
        [whole(value) for value in values],
        pl.BlockSpec(shape, lambda i, info: (0, 0)),
        shape[1],
        shape[1] * 64,
        name="small_rows",
    )(info, *values)


def unshuffled(parts):
    return jnp.concatenate(
        [
            part[:, (3 * group + j) * GROUP : (3 * group + j + 1) * GROUP]
            for j in range(3)
            for part in parts
            for group in range(part.shape[1] // (3 * GROUP))
        ],
        axis=1,
    )


def shares_kernel(info_ref, rows_ref, dec_qkv_ref, *refs, parts, wide, narrow, units, dec_units, count):
    block = info_ref[BLOCK]

    def share(first, last, start, width):
        values = rows_ref[first:last, start : start + width]
        part = width // count
        return pltpu.roll(values, width - block * part, 1)[:, :part]

    enc_qkv = [ref[...] for ref in refs[:parts]]
    outs = refs[parts:]
    bias_up_enc = share(0, 1, 0, units)
    bias_up_dec = share(1, 2, 0, dec_units)
    enc = share(2, 6, 0, wide)
    dec = share(2, 6, wide, narrow)
    dec_in = share(2, 6, wide + narrow, narrow)
    final = share(6, 8, 0, wide)
    enc_in = share(6, 8, wide, wide)
    for ref, value in zip(
        outs,
        (
            jnp.concatenate([enc_in[0:1], enc[0:1], final[0:1]], axis=0),
            jnp.concatenate([enc_in[1:2], enc[1:2], final[1:2]], axis=0),
            enc[2:4],
            bias_up_enc,
            dec_in[3:4],
            dec_in[2:3],
            jnp.concatenate([dec_in[0:1], dec[0:1]], axis=0),
            jnp.concatenate([dec_in[1:2], dec[1:2]], axis=0),
            dec[2:4],
            bias_up_dec,
            unshuffled([dec_qkv_ref[...]]),
            unshuffled(enc_qkv),
        ),
    ):
        ref[...] = value


def shares_call(info, rows, dec_qkv, enc_qkv, wide, narrow, units, dec_units, count):
    shapes = [
        (height, width // count)
        for height, width in (
            (3, wide),
            (3, wide),
            (2, wide),
            (1, units),
            (1, narrow),
            (1, narrow),
            (2, narrow),
            (2, narrow),
            (2, narrow),
            (1, dec_units),
        )
    ] + [dec_qkv.shape, (wide // count, 3 * wide)]
    return call(
        functools.partial(
            shares_kernel,
            parts=len(enc_qkv),
            wide=wide,
            narrow=narrow,
            units=units,
            dec_units=dec_units,
            count=count,
        ),
        tuple(sds(shape, jnp.float32) for shape in shapes),
        (1,),
        [whole(array) for array in (rows, dec_qkv, *enc_qkv)],
        tuple(pl.BlockSpec(shape, lambda i, info: (0, 0)) for shape in shapes),
        rows.size,
        rows.size * 4,
        name="shares",
    )(info, rows, dec_qkv, *enc_qkv)


def decoder_shares_kernel(info_ref, rows_ref, up_ref, out_ref, down_ref):
    width = out_ref.shape[1]
    units = up_ref.shape[1]
    share = up_ref.shape[0]
    rows = rows_ref[...]
    up_ref[...] = rows[:, :units]
    out_ref[...] = rows[:, units : units + width]
    for fold in range(units // width):
        start = units + (fold + 1) * width
        down_ref[fold * share : (fold + 1) * share, :] = rows[:, start : start + width]


def decoder_shares_call(info, rows, width, units, after):
    share = rows.shape[0]
    shapes = ((share, units), (share, width), (share * units // width, width))
    return call(
        decoder_shares_kernel,
        tuple(sds(shape, jnp.float32) for shape in shapes),
        (1,),
        [whole(rows)],
        tuple(pl.BlockSpec(shape, lambda i, info: (0, 0)) for shape in shapes),
        rows.size,
        rows.size * 6,
        name="decoder_shares",
        after=after,
    )(info, rows)


def place_table(length_rows, model_width):
    halfway = model_width // 2
    places = np.arange(length_rows, dtype=np.float64)[:, None]
    rates = np.exp(np.arange(halfway, dtype=np.float64) * (-math.log(10000.0) / halfway))[None, :]
    return np.concatenate([np.sin(places * rates), np.cos(places * rates)], axis=1).astype(
        np.float32
    )


def local(
    patches,
    visible,
    source,
    enc_gains,
    enc_shifts,
    enc_qkv,
    enc_out,
    enc_bias_out,
    enc_up,
    enc_bias_up,
    enc_down,
    enc_proj,
    proj_bias,
    mask_token,
    dec_gains,
    dec_shifts,
    dec_qkv,
    dec_out,
    dec_bias_out,
    dec_up,
    dec_bias_up,
    dec_down,
    cotangent,
):
    pairs = lax.axis_size("dp")
    count = 2 * pairs
    length = patches.shape[1]
    wide = patches.shape[2]
    narrow = dec_qkv.shape[0]
    strips = patches.shape[0] // 2
    padded = -(-(length + 1) // ROW_STEP) * ROW_STEP
    sizes = Sizes(strips, length, padded)
    rows = sizes.rows
    info = place_info(visible, strips)
    taken = jnp.pad(
        jnp.where(source < 0, padded - 1, source),
        ((0, 0), (0, padded - length)),
        constant_values=padded - 1,
    )
    places = jnp.asarray(place_table(padded, narrow))
    strip_form = lambda array: array.reshape(strips, padded, array.shape[-1])
    row_form = lambda array: array.reshape(rows, array.shape[-1])

    n1_enc, packed_enc = packed_call(sizes, info, patches, enc_gains, enc_shifts, enc_qkv)
    packed_enc = strip_form(packed_enc)
    enc_live = visible_live(strips)
    mixed_enc = row_form(attend_call(packed_enc, info, HEADS_ENC, enc_live, "encoder_attention"))
    mid_enc, n2_enc, act_enc, slope_enc, y_enc, encoded, projected = encoder_ff_call(
        sizes,
        info,
        patches,
        mixed_enc,
        enc_gains,
        enc_shifts,
        enc_out,
        enc_bias_out,
        enc_up,
        enc_bias_up,
        enc_down,
        enc_proj,
        proj_bias,
    )
    x_dec, n1_dec, packed_dec = decoder_in_call(
        sizes, info, projected, taken, mask_token, places, dec_gains, dec_shifts, dec_qkv
    )
    x_dec, n1_dec, packed_dec = map(strip_form, (x_dec, n1_dec, packed_dec))
    dec_live = all_live(length)
    mixed_dec = row_form(attend_call(packed_dec, info, HEADS_DEC, dec_live, "decoder_attention"))
    share = narrow // count
    (
        kept_dec,
        sent_dec,
        gb_dec,
        dmixed_dec,
        sums_dec,
        up_sums_dec,
        kept_beside,
        sent_beside,
        *apart,
    ) = decoder_ff_call(
        sizes,
        info,
        row_form(x_dec),
        mixed_dec,
        cotangent,
        dec_gains,
        dec_shifts,
        dec_out,
        dec_bias_out,
        dec_up,
        dec_bias_up,
        dec_down,
        share,
    )
    arrived_beside, arrived_dec = map(across, (sent_beside, sent_dec))
    enc_half = wide // 2
    dpacked_dec, kept_dqkv, sent_dqkv = attend_back_call(
        packed_dec,
        strip_form(dmixed_dec),
        n1_dec,
        info,
        HEADS_DEC,
        dec_live,
        0,
        1,
        (sent_beside, sent_dec),
        "decoder_attention_back",
    )
    arrived_dqkv = across(sent_dqkv)
    decoded = arrange_call(info, [kept_dec], [arrived_dec], strips, "decoded_strips", (dpacked_dec,))
    grad_enc, sums_dec_in, sums_final, kept_proj, sent_proj = decoder_back_call(
        sizes,
        info,
        dpacked_dec,
        strip_form(gb_dec),
        x_dec,
        taken,
        strip_form(y_enc),
        strip_form(encoded),
        dec_gains,
        dec_shifts,
        dec_qkv,
        enc_proj,
        enc_gains,
        enc_shifts,
        (sent_dqkv, decoded),
    )
    grad_enc = row_form(grad_enc)
    arrived_proj = across(sent_proj)
    ((kept_edown, sent_edown),) = product_call(
        info, [(act_enc, grad_enc, enc_half, wide)], "grad_enc_down", (sent_proj,)
    )
    grads_dec = Chain(
        pairs, (0, 1, 2, 3), ((kept_beside, arrived_beside), (kept_dqkv, arrived_dqkv))
    )
    sent, (sent_edown,) = round_call(
        info, [grads_dec], "round_1", (kept_edown, arrived_proj), (sent_edown,)
    )
    arrived_edown = across(sent_edown)
    dhid_enc, gb_enc, dmixed_enc, sums_enc, up_sums_enc = encoder_ff_back_call(
        sizes,
        info,
        grad_enc,
        mid_enc,
        slope_enc,
        enc_gains,
        enc_shifts,
        enc_out,
        enc_up,
        enc_down,
        (*sent, sent_edown),
    )
    (kept_eup, sent_eup), (kept_eout, sent_eout) = product_call(
        info,
        [(n2_enc, dhid_enc, enc_half, wide), (mixed_enc, gb_enc, enc_half, wide)],
        "grad_enc_up_out",
        sent,
    )
    down_enc = Chain(pairs, (0, 2, 1, 3), ((kept_edown, arrived_edown),))
    sent, (sent_eup, sent_eout) = round_call(
        info, [down_enc, grads_dec], "round_2", (kept_eout,), (sent_eup, sent_eout)
    )
    arrived_eup, arrived_eout = map(across, (sent_eup, sent_eout))
    up_enc = Chain(pairs, (1, 0, 2, 3), ((kept_eup, arrived_eup),))
    out_enc = Chain(pairs, (0, 1, 2, 3), ((kept_eout, arrived_eout), (kept_proj, arrived_proj)))
    every = [up_enc, down_enc, grads_dec, out_enc]
    active = lambda: [chain for chain in every if chain.done is None]
    after = (*sent, sent_eup, sent_eout)
    number, dpacked_enc, qkv_enc = 3, [], []
    by_y, by_z = (1, 0, 2, 3), (2, 0, 1, 3)
    for part in range(PARTS):
        dpacked, kept, sent_here = attend_back_call(
            packed_enc,
            strip_form(dmixed_enc),
            strip_form(n1_enc),
            info,
            HEADS_ENC,
            enc_live,
            part,
            PARTS,
            after,
            f"encoder_attention_back_{part}",
        )
        dpacked_enc.append(dpacked)
        sent, (sent_here,) = round_call(info, active(), f"round_{number}", (dpacked,), (sent_here,))
        chain = Chain(pairs, (by_z, by_y)[part % 2], ((kept, across(sent_here)),))
        number += 1
        qkv_enc.append(chain)
        every.append(chain)
        after = (*sent, sent_here)
    kept_enc, sent_enc, sums_enc_in = [], [], []
    for strip in range(strips):
        kept, sent_here, sums = encoder_back_call(
            sizes, info, dpacked_enc, gb_enc, patches, enc_gains, enc_shifts, enc_qkv, strip, after
        )
        kept_enc.append(kept)
        sums_enc_in.append(sums)
        sent_enc.append(sent_here)
        through = ()
        if strip == strips - 1:
            through = tuple(sent_enc)
            if apart:
                down_dec = Chain(pairs, by_y, ((apart[0], across(apart[1])),))
                every.append(down_dec)
            small = gather_small_call(
                info,
                (
                    up_sums_enc,
                    up_sums_dec,
                    sums_enc,
                    sums_dec,
                    sums_dec_in,
                    sums_final,
                    *sums_enc_in,
                ),
            )
            through += (small,)
        sent, through = round_call(info, active(), f"round_{number}", (sums,), through)
        number += 1
        after = (*sent,)
    *sent_enc, small = through
    arrived_enc = [across(array) for array in sent_enc]
    small = Total(pairs, small)
    every.append(small)
    patch_grad = arrange_call(info, kept_enc, arrived_enc, strips, "patch_grad_strips", after)
    after = (patch_grad,)
    while active():
        round_call(info, active(), f"round_{number}", after)
        after = ()
        number += 1
    g_beside, g_dqkv = grads_dec.done
    shares = shares_call(
        info,
        small.done,
        g_dqkv,
        [chain.done[0] for chain in qkv_enc],
        wide,
        narrow,
        enc_up.shape[1],
        dec_up.shape[1],
        count,
    )
    if apart:
        g_dup, g_dout = g_beside[:, : dec_up.shape[1]], g_beside[:, dec_up.shape[1] :]
        (g_ddown,) = down_dec.done
    else:
        g_dup, g_dout, g_ddown = decoder_shares_call(info, g_beside, narrow, dec_up.shape[1], ())
    (g_edown,), (g_eup,) = down_enc.done, up_enc.done
    g_eout, g_proj = out_enc.done
    return (
        decoded,
        patch_grad,
        shares[0],
        shares[1],
        shares[11],
        g_eout,
        shares[2],
        g_eup,
        shares[3].reshape(-1),
        g_edown,
        g_proj,
        shares[4].reshape(-1),
        shares[5].reshape(-1),
        shares[6],
        shares[7],
        shares[10],
        g_dout,
        shares[8],
        g_dup,
        shares[9].reshape(-1),
        g_ddown,
    )


def solution(mesh):
    return jax.shard_map(
        local,
        mesh=mesh,
        in_specs=(
            P("dp", None, None),
            P("dp"),
            P("dp", None),
            P(),
            P(),
            P(),
            P(),
            P(),
            P(),
            P(),
            P(),
            P(),
            P(),
            P(),
            P(),
            P(),
            P(),
            P(),
            P(),
            P(),
            P(),
            P(),
            P("dp", None, None),
        ),
        out_specs=(
            P("dp", None, "section"),
            P("dp", None, "section"),
            P(None, ("section", "dp")),
            P(None, ("section", "dp")),
            P(("section", "dp"), None),
            P(("section", "dp"), None),
            P(None, ("section", "dp")),
            P(("section", "dp"), None),
            P(("section", "dp")),
            P(("section", "dp"), None),
            P(("section", "dp"), None),
            P(("section", "dp")),
            P(("section", "dp")),
            P(None, ("section", "dp")),
            P(None, ("section", "dp")),
            P(("section", "dp"), None),
            P(("section", "dp"), None),
            P(None, ("section", "dp")),
            P(("section", "dp"), None),
            P(("section", "dp")),
            P(("section", "dp"), None),
        ),
        check_vma=False,
    )
```

```python
import functools
import math

import jax
import jax.numpy as jnp
import numpy as np
from jax import lax
from jax.experimental import pallas as pl
from jax.experimental.pallas import tpu as pltpu
from jax.sharding import PartitionSpec as P

HEADS_ENC = 12
HEADS_DEC = 16
ROW_STEP = 32
GROUP = 128
PARTS = 2
VMEM_BYTES = 63 * 1024 * 1024
MASKED = -1e30
LOG2E = math.log2(math.e)

epsilon = 1e-06

NN = (((1,), (0,)), ((), ()))
NT = (((1,), (1,)), ((), ()))
TN = (((0,), (0,)), ((), ()))


def dot(left_side, right_side, dims):
    return lax.dot_general(left_side, right_side, dims, preferred_element_type=jnp.float32)


def low(values):
    return values.astype(jnp.bfloat16)


def call(
    kernel, out_shape, grid, in_specs, out_specs, flops, moved, scalars=1, exps=0, after=(), name=None, scratch=(), through=()
):
    count = scalars + len(in_specs)
    ordered = [pl.BlockSpec(memory_space=pl.ANY)] * (len(after) + len(through))
    aliases = {}
    if through:
        outs = len(out_shape)
        aliases = {count + len(after) + place: outs + place for place in range(len(through))}
        out_shape = tuple(out_shape) + tuple(sds(array.shape, array.dtype) for array in through)
        out_specs = tuple(out_specs) + (pl.BlockSpec(memory_space=pl.ANY),) * len(through)

    def body(*refs):
        ins, rest = refs[:count], refs[count + len(after) + len(through) :]
        if through:
            rest = rest[:outs] + rest[outs + len(through) :]
        kernel(*ins, *rest)

    made = pl.pallas_call(
        body,
        out_shape=out_shape,
        grid_spec=pltpu.PrefetchScalarGridSpec(
            num_scalar_prefetch=scalars,
            grid=grid,
            in_specs=list(in_specs) + ordered,
            out_specs=out_specs,
            scratch_shapes=list(scratch),
        ),
        input_output_aliases=aliases,
        compiler_params=pltpu.CompilerParams(vmem_limit_bytes=VMEM_BYTES),
        cost_estimate=pl.CostEstimate(flops=flops // 256, bytes_accessed=moved // 256, transcendentals=0),
        name=name,
    )
    return lambda *operands: made(*operands, *after, *through)


def whole(array):
    rank = array.ndim
    return pl.BlockSpec(array.shape, lambda *unused: (0,) * rank)


def row_of(ref, place):
    return ref[place : place + 1, :].astype(jnp.float32)


def vector_of(ref):
    return ref[...].astype(jnp.float32).reshape(1, -1)


def live_rows(values, start, count):
    row = lax.broadcasted_iota(jnp.int32, (values.shape[0], 1), 0) + start
    return jnp.where(row < count, values.astype(jnp.float32), 0.0)


def sds(shape, kind=jnp.bfloat16):
    return jax.ShapeDtypeStruct(shape, kind)


def norm(values, gain_row, shift_row):
    center = values - jnp.mean(values, axis=-1, keepdims=True)
    inverse = lax.rsqrt(jnp.mean(center * center, axis=-1, keepdims=True) + epsilon)
    unit = center * inverse
    return unit * gain_row + shift_row, unit, inverse


def norm_back(grad_out, unit, inverse, gain_row):
    scaled = grad_out * gain_row
    return inverse * (
        scaled
        - jnp.mean(scaled, axis=-1, keepdims=True)
        - unit * jnp.mean(scaled * unit, axis=-1, keepdims=True)
    )


def col_sum(values):
    return jnp.sum(values, axis=0, keepdims=True)


def gelu_parts(values):
    share = 0.5 + 0.5 * lax.erf(values * math.sqrt(0.5))
    bell = jnp.exp2(values * values * (-0.5 * LOG2E)) * (1.0 / math.sqrt(2.0 * math.pi))
    return values * share, share + values * bell


def add_rows(ref, rows):
    @pl.when((pl.program_id(0) == 0) & (pl.program_id(1) == 0))
    def start():
        ref[...] = jnp.zeros_like(ref)

    for place, row in enumerate(rows):
        ref[place : place + 1, :] += row


BLOCK = 1
STRIP = 2


def place_info(visible, strips):
    section_index = lax.axis_index("section")
    block = section_index * lax.axis_size("dp") + lax.axis_index("dp")
    mine = section_index * strips + jnp.arange(strips, dtype=jnp.int32)
    every = jnp.arange(2 * strips, dtype=jnp.int32)
    return jnp.concatenate(
        [
            jnp.stack([section_index, block]),
            mine,
            lax.dynamic_slice_in_dim(visible, section_index * strips, strips, 0),
            every // strips,
            every % strips,
        ]
    ).astype(jnp.int32)


class Sizes:
    def __init__(self, strips, length, padded):
        self.strips, self.length, self.padded = strips, length, padded
        self.rows = strips * padded

    def place(self, strip):
        return slice(strip * self.padded, (strip + 1) * self.padded)

    def raw(self, width):
        return [
            pl.BlockSpec(
                (None, self.padded, width), lambda *step, s=s: (step[-1][STRIP + s], 0, 0)
            )
            for s in range(self.strips)
        ]

    def all(self, width):
        return pl.BlockSpec((self.rows, width), lambda *step: (0, 0))

    def cols(self, width):
        return pl.BlockSpec((self.rows, width), lambda i, info: (0, i))

    def half(self, width):
        return pl.BlockSpec((self.strips, self.padded, width), lambda *step: (0, 0, 0))

    def sums(self, width):
        return pl.BlockSpec((8, width), lambda *step: (0, 0))

    def strip(self, width):
        return pl.BlockSpec((None, self.padded, width), lambda s, i, info: (s, 0, 0))


def first_step(run):
    pl.when(pl.program_id(0) == 0)(run)


def last_step(run):
    pl.when(pl.program_id(0) == pl.num_programs(0) - 1)(run)


def store_halves(info_ref, kept_ref, sent_ref, values):
    half = kept_ref.shape[-1]
    first = info_ref[0] == 0
    kept_ref[...] = low(jnp.where(first, values[:, :half], values[:, half:]))
    sent_ref[...] = low(jnp.where(first, values[:, half:], values[:, :half]))


def set_rows(ref, rows):
    for place, row in enumerate(rows):
        ref[place : place + 1, :] = row


def packed_kernel(info_ref, *refs, sizes):
    x_refs = refs[: sizes.strips]
    gain_ref, shift_ref, w_ref, n_ref, packed_ref = refs[sizes.strips :]

    @first_step
    def normalize():
        for strip, x_ref in enumerate(x_refs):
            x = live_rows(x_ref[...], 0, sizes.length)
            normed, _, _ = norm(x, row_of(gain_ref, 0), row_of(shift_ref, 0))
            n_ref[sizes.place(strip), :] = low(normed)

    packed_ref[...] = low(dot(n_ref[...], w_ref[...], NN))


def packed_call(sizes, info, x, gains, shifts, w_qkv):
    rows, width = sizes.rows, x.shape[2]
    return call(
        functools.partial(packed_kernel, sizes=sizes),
        (sds((rows, width)), sds((rows, 3 * width))),
        (3,),
        sizes.raw(width)
        + [whole(gains), whole(shifts), pl.BlockSpec((width, width), lambda i, info: (0, i))],
        (sizes.all(width), sizes.cols(width)),
        6 * rows * width * width,
        rows * width * 10 + 6 * width * width,
        name="encoder_packed",
    )(info, *[x] * sizes.strips, gains, shifts, w_qkv)


def picker_of(source_ref, strip):
    taken = source_ref[pl.ds(strip, 1), :]
    length = taken.shape[1]
    return low(jnp.where(taken == lax.broadcasted_iota(jnp.int32, (length, length), 0), 1.0, 0.0))


def last_row(length):
    return lax.broadcasted_iota(jnp.int32, (length, 1), 0) == length - 1


def decoder_in_kernel(
    info_ref,
    rows_ref,
    source_ref,
    mask_ref,
    places_ref,
    gain_ref,
    shift_ref,
    w_ref,
    x_ref,
    n_ref,
    packed_ref,
    *,
    sizes
):
    @first_step
    def gather():
        for strip in range(sizes.strips):
            place = sizes.place(strip)
            picker = picker_of(source_ref, info_ref[STRIP + strip])
            rows = jnp.where(
                last_row(sizes.padded), vector_of(mask_ref), rows_ref[place, :].astype(jnp.float32)
            )
            x = dot(picker, low(rows), TN) + places_ref[...]
            x_ref[place, :] = x
            normed, _, _ = norm(x, row_of(gain_ref, 0), row_of(shift_ref, 0))
            n_ref[place, :] = low(normed)

    packed_ref[...] = low(dot(n_ref[...], w_ref[...], NN))


def decoder_in_call(sizes, info, projected, source, mask_row, places, gains, shifts, w_qkv):
    width = projected.shape[1]
    rows = sizes.rows
    return call(
        functools.partial(decoder_in_kernel, sizes=sizes),
        (sds((rows, width), jnp.float32), sds((rows, width)), sds((rows, 3 * width))),
        (3,),
        [sizes.all(width), whole(source), whole(mask_row), whole(places), whole(gains), whole(shifts)]
        + [pl.BlockSpec((width, width), lambda i, info: (0, i))],
        (sizes.all(width), sizes.all(width), sizes.cols(width)),
        6 * rows * width * width + 2 * rows * sizes.padded * width,
        rows * width * 18 + 6 * width * width,
        name="decoder_packed",
    )(info, projected, source, mask_row, places, gains, shifts, w_qkv)


def head_parts(head, heads_here):
    lane = lax.broadcasted_iota(jnp.int32, (1, GROUP), 1)
    size = GROUP // heads_here
    mine = (lane >= head * size) & (lane < (head + 1) * size)
    spare = ((head + 1) % heads_here) * size
    return mine, lane == spare, spare


def key_bias(live, length):
    row = lax.broadcasted_iota(jnp.int32, (length, 1), 0)
    return low(jnp.where(row < live, 0.0, MASKED))


def attend_kernel(info_ref, q_ref, k_ref, v_ref, out_ref, scale_ref, *, heads_here, live):
    length = q_ref.shape[1]
    rate = (GROUP // heads_here) ** -0.5 * LOG2E
    bias = key_bias(live(info_ref, pl.program_id(0)), length)
    one = jnp.bfloat16(1.0)
    middle = length // 2
    for group in range(q_ref.shape[2] // GROUP):
        columns = slice(group * GROUP, (group + 1) * GROUP)
        k, v = k_ref[0, :, columns], v_ref[0, :, columns]
        for rows in (slice(0, middle), slice(middle, length)):
            q = q_ref[0, rows, columns]
            mixed = jnp.zeros(q.shape, jnp.float32)
            tops = jnp.zeros(q.shape, jnp.float32)
            totals = jnp.ones(q.shape, jnp.float32)
            for head in range(heads_here):
                mine, at_spare, spare = head_parts(head, heads_here)
                head_q = jnp.where(mine, q, low(jnp.where(at_spare, 1.0, 0.0)))
                scores = dot(head_q, jnp.where(at_spare, bias, k), NT)
                highest = jnp.max(scores, axis=1, keepdims=True)
                terms = low(jnp.exp2((scores - highest) * rate))
                product = dot(terms, jnp.where(at_spare, one, v), NN)
                mixed = jnp.where(mine, product * (1.0 / product[:, spare : spare + 1]), mixed)
                tops = jnp.where(at_spare, highest, tops)
                totals = jnp.where(at_spare, product, totals)
            out_ref[0, rows, columns] = low(mixed)
            scales = (tops * rate + jnp.log2(totals)).T
            for head in range(heads_here):
                spare = head_parts(head, heads_here)[2]
                scale_ref[0, group, head : head + 1, rows] = scales[spare : spare + 1]


def all_live(length):
    return lambda info_ref, strip: length


def visible_live(strips):
    return lambda info_ref, strip: info_ref[STRIP + strips + strip]


def attend_call(packed, info, heads, live, name):
    strips, length, triple = packed.shape
    width = triple // 3
    heads_here = GROUP // (width // heads)
    steps = 2
    part = width // steps
    groups = part // GROUP
    third = lambda j: pl.BlockSpec((1, length, part), lambda s, g, _: (s, 0, g + j * steps))
    return call(
        functools.partial(attend_kernel, heads_here=heads_here, live=live),
        (sds((strips, length, width)), sds((strips, steps * groups, 8, length), jnp.float32)),
        (strips, steps),
        [third(0), third(1), third(2)],
        (third(0), pl.BlockSpec((1, groups, 8, length), lambda s, g, _: (s, g, 0, 0))),
        strips * heads * length * length * GROUP * 6,
        strips * length * width * 8,
        exps=strips * heads * length * length,
        name=name,
    )(info, packed, packed, packed)


def attend_back_kernel(
    info_ref,
    q_ref,
    k_ref,
    v_ref,
    dout_ref,
    mixed_ref,
    scale_ref,
    n_ref,
    grad_ref,
    kept_ref,
    sent_ref,
    total_ref,
    *,
    heads_here,
    live
):
    length = q_ref.shape[1]
    factor = (GROUP // heads_here) ** -0.5
    rate = factor * LOG2E
    strip = pl.program_id(1)
    q, k, v, dout = q_ref[0], k_ref[0], v_ref[0], dout_ref[0]
    bias = key_bias(live(info_ref, strip), length)
    k_turned = k.T
    agree = (dout.astype(jnp.float32) * mixed_ref[0].astype(jnp.float32)).T
    dq_turned = []
    dk = jnp.zeros((length, GROUP), jnp.float32)
    dv = jnp.zeros((length, GROUP), jnp.float32)
    size = GROUP // heads_here
    for head in range(heads_here):
        mine, at_spare, _ = head_parts(head, heads_here)
        head_q = jnp.where(mine, q, low(jnp.where(at_spare, 1.0, 0.0)))
        head_dout = jnp.where(mine, dout, jnp.bfloat16(0.0))
        scores = dot(jnp.where(at_spare, bias, k), head_q, NT)
        probs = jnp.exp2(scores * rate - scale_ref[0, 0, head : head + 1, :])
        average = jnp.sum(agree[head * size : (head + 1) * size], axis=0, keepdims=True)
        dscores = low(probs * (dot(v, head_dout, NT) - average))
        dk = jnp.where(mine, dot(dscores, q, NN), dk)
        dv = jnp.where(mine, dot(low(probs), dout, NN), dv)
        dq_turned.append(dot(k_turned[head * size : (head + 1) * size], dscores, NN))
    dq = low(jnp.concatenate(dq_turned, axis=0).T * factor)
    dk, dv = low(dk * factor), low(dv)
    grad_ref[0, 0] = dq
    grad_ref[1, 0] = dk
    grad_ref[2, 0] = dv
    term = dot(n_ref[0], jnp.concatenate([dq, dk, dv], axis=1), TN)
    half = kept_ref.shape[0]
    last = pl.num_programs(1) - 1

    @pl.when(strip == 0)
    def begin():
        total_ref[...] = term

    @pl.when(strip > 0)
    def more():
        total_ref[...] += term

    @pl.when(strip == last)
    def finish():
        kept_ref[...] = low(total_ref[pl.ds(pl.multiple_of(info_ref[0] * half, 8), half), :])
        sent_ref[...] = low(total_ref[pl.ds(pl.multiple_of((1 - info_ref[0]) * half, 8), half), :])


def attend_back_call(
    packed, dmixed, mixed, scales, normed, info, heads, live, part, parts, after, name
):
    strips, length, triple = packed.shape
    width = triple // 3
    heads_here = GROUP // (width // heads)
    groups = width // GROUP
    here = groups // parts
    third = lambda j: pl.BlockSpec(
        (1, length, GROUP), lambda g, s, _: (s, 0, g + part * here + j * groups)
    )
    product = pl.BlockSpec((width // 2, 3 * GROUP), lambda g, s, _: (0, g))
    return call(
        functools.partial(attend_back_kernel, heads_here=heads_here, live=live),
        (
            sds((3, strips, length, here * GROUP)),
            sds((width // 2, here * 3 * GROUP)),
            sds((width // 2, here * 3 * GROUP)),
        ),
        (here, strips),
        [
            third(0),
            third(1),
            third(2),
            third(0),
            third(0),
            pl.BlockSpec((1, 1, 8, length), lambda g, s, _: (s, g + part * here, 0, 0)),
            pl.BlockSpec((1, length, width), lambda g, s, _: (s, 0, 0)),
        ],
        (pl.BlockSpec((3, 1, length, GROUP), lambda g, s, _: (0, s, 0, g)), product, product),
        (strips * heads * length * length * GROUP * 12 + 6 * strips * length * width * width) // parts,
        strips * length * width * 14 // parts,
        exps=strips * heads * length * length // parts,
        after=after,
        name=name,
        scratch=[pltpu.VMEM((width, 3 * GROUP), jnp.float32)],
    )(info, packed, packed, packed, dmixed, mixed, scales, normed)


def encoder_ff_kernel(info_ref, *refs, sizes):
    x_refs = refs[: sizes.strips]
    (
        mixed_ref,
        gain_ref,
        shift_ref,
        w_out_ref,
        bias_out_ref,
        w_up_ref,
        bias_up_ref,
        w_down_ref,
        w_proj_ref,
        bias_proj_ref,
        mid_ref,
        n_ref,
        act_ref,
        slope_ref,
        y_low_ref,
        encoded_ref,
        projected_ref,
        y_ref,
        bias_ref,
    ) = refs[sizes.strips :]
    places = [sizes.place(strip) for strip in range(sizes.strips)]

    @first_step
    def middle():
        bias_ref[...] = vector_of(bias_up_ref)
        for place, x_ref in zip(places, x_refs):
            x = live_rows(x_ref[...], 0, sizes.length)
            mid = x + dot(mixed_ref[place, :], w_out_ref[...], NN) + row_of(bias_out_ref, 0)
            mid_ref[place, :] = low(mid)
            normed, _, _ = norm(mid, row_of(gain_ref, 1), row_of(shift_ref, 1))
            n_ref[place, :] = low(normed)
            y_ref[place, :] = mid + row_of(bias_out_ref, 1)

    chunk = w_up_ref.shape[1]
    bias = bias_ref[:, pl.ds(pl.multiple_of(pl.program_id(0) * chunk, GROUP), chunk)]
    hidden = [dot(n_ref[place, :], w_up_ref[...], NN) + bias for place in places]
    for place, values in zip(places, hidden):
        act, slope = gelu_parts(values)
        act = low(act)
        act_ref[place, :] = act
        slope_ref[place, :] = low(slope)
        y_ref[place, :] += dot(act, w_down_ref[...], NN)

    @last_step
    def finish():
        for place in places:
            y = y_ref[place, :]
            y_low_ref[place, :] = low(y)
            encoded, _, _ = norm(y, row_of(gain_ref, 2), row_of(shift_ref, 2))
            encoded = low(encoded)
            encoded_ref[place, :] = encoded
            projected_ref[place, :] = low(
                dot(encoded, w_proj_ref[...], NN) + vector_of(bias_proj_ref)
            )


def encoder_ff_call(
    sizes, info, x, mixed, gains, shifts, w_out, bias_out, w_up, bias_up, w_down, w_proj, bias_proj
):
    rows, width = sizes.rows, x.shape[2]
    units = w_up.shape[1]
    narrow = w_proj.shape[1]
    chunk = units // 4
    return call(
        functools.partial(encoder_ff_kernel, sizes=sizes),
        (
            sds((rows, width)),
            sds((rows, width)),
            sds((rows, units)),
            sds((rows, units)),
            sds((rows, width)),
            sds((rows, width)),
            sds((rows, narrow)),
        ),
        (4,),
        sizes.raw(width)
        + [sizes.all(width)]
        + [whole(w) for w in (gains, shifts, w_out, bias_out)]
        + [
            pl.BlockSpec((width, chunk), lambda i, info: (0, i)),
            whole(bias_up),
            pl.BlockSpec((chunk, width), lambda i, info: (i, 0)),
            whole(w_proj),
            whole(bias_proj),
        ],
        (
            sizes.all(width),
            sizes.all(width),
            sizes.cols(chunk),
            sizes.cols(chunk),
            sizes.all(width),
            sizes.all(width),
            sizes.all(narrow),
        ),
        2 * rows * width * (width + 2 * units + narrow),
        rows * (width * 16 + units * 4) + 2 * width * (width + 2 * units + narrow),
        exps=rows * units,
        name="encoder_feed_forward",
        scratch=[pltpu.VMEM((rows, width), jnp.float32), pltpu.VMEM((1, units), jnp.float32)],
    )(
        info,
        *[x] * sizes.strips,
        mixed,
        gains,
        shifts,
        w_out,
        bias_out,
        w_up,
        bias_up,
        w_down,
        w_proj,
        bias_proj,
    )


def decoder_ff_kernel(info_ref, *refs, sizes, folds, share, units):
    cot_refs = refs[: sizes.strips]
    (
        x_ref,
        mixed_ref,
        gain_ref,
        shift_ref,
        w_out_ref,
        bias_out_ref,
        w_up_ref,
        bias_up_ref,
        w_down_ref,
        kept_ref,
        sent_ref,
        gb_ref,
        dmixed_ref,
        sums_ref,
        up_sums_ref,
        kept_up_ref,
        sent_up_ref,
        *down_refs,
        cot_ref,
        n_ref,
        act_ref,
        dhidden_ref,
        mid_ref,
        y_ref,
        dnormed_ref,
        bias_ref,
        beside_ref,
        down_ref,
    ) = refs[sizes.strips :]
    places = [sizes.place(strip) for strip in range(sizes.strips)]
    gain, shift = row_of(gain_ref, 1), row_of(shift_ref, 1)

    @first_step
    def middle():
        bias_ref[...] = vector_of(bias_up_ref)
        dnormed_ref[...] = jnp.zeros_like(dnormed_ref)
        for place, cot_here in zip(places, cot_refs):
            mid = x_ref[place, :] + dot(mixed_ref[place, :], w_out_ref[...], NN) + row_of(bias_out_ref, 0)
            mid_ref[place, :] = mid
            normed, _, _ = norm(mid, gain, shift)
            n_ref[place, :] = low(normed)
            y_ref[place, :] = mid + row_of(bias_out_ref, 1)
            cot_ref[place, :] = low(live_rows(cot_here[...], 0, sizes.length))

    chunk = w_up_ref.shape[1]
    bias = bias_ref[:, pl.ds(pl.multiple_of(pl.program_id(0) * chunk, GROUP), chunk)]
    hidden = [dot(n_ref[place, :], w_up_ref[...], NN) + bias for place in places]
    dact = [dot(cot_ref[place, :], w_down_ref[...], NT) for place in places]
    up_sums = jnp.zeros((1, chunk), jnp.float32)
    for place, values, grads in zip(places, hidden, dact):
        act, slope = gelu_parts(values)
        act = low(act)
        act_ref[place, :] = act
        y_ref[place, :] += dot(act, w_down_ref[...], NN)
        dhidden = low(grads * slope)
        dhidden_ref[place, :] = dhidden
        up_sums = up_sums + col_sum(dhidden.astype(jnp.float32))
        dnormed_ref[place, :] += dot(dhidden, w_up_ref[...], NT)
    up_sums_ref[0:1, :] = up_sums
    step, width = pl.program_id(0), n_ref.shape[1]
    beside_ref[:, pl.ds(pl.multiple_of(step * chunk, GROUP), chunk)] = low(
        dot(n_ref[...], dhidden_ref[...], TN)
    )
    down = dot(act_ref[...], cot_ref[...], TN)
    if folds:
        down = down.reshape(-1, folds, share, width)
        here = chunk // folds
        rows = pl.ds(pl.multiple_of(step * here, share), here)
        for fold in range(folds):
            start = (folds + 1 + fold) * width
            beside_ref[rows, start : start + width] = low(down[:, fold].reshape(here, width))
    else:
        down_ref[pl.ds(pl.multiple_of(step * chunk, GROUP), chunk), :] = low(down)

    @last_step
    def finish():
        totals = []
        for strip, place in enumerate(places):
            store_halves(info_ref, kept_ref.at[strip], sent_ref.at[strip], y_ref[place, :])
            _, unit, inverse = norm(mid_ref[place, :], gain, shift)
            grad = cot_ref[place, :].astype(jnp.float32)
            dnormed = dnormed_ref[place, :]
            gb = low(grad + norm_back(dnormed, unit, inverse, gain))
            gb_ref[place, :] = gb
            dmixed_ref[place, :] = low(dot(gb, w_out_ref[...], NT))
            totals.append(
                (
                    col_sum(dnormed * unit),
                    col_sum(dnormed),
                    col_sum(gb.astype(jnp.float32)),
                    col_sum(grad),
                )
            )
        set_rows(sums_ref, [sum(rows) for rows in zip(*totals)])
        beside_ref[:, units : units + width] = low(dot(mixed_ref[...], gb_ref[...], TN))
        for kept, sent, whole_ref in zip(
            (kept_up_ref, *down_refs[:1]), (sent_up_ref, *down_refs[1:]), (beside_ref, down_ref)
        ):
            half = kept.shape[0]
            kept[...] = whole_ref[pl.ds(pl.multiple_of(info_ref[0] * half, 16), half), :]
            sent[...] = whole_ref[pl.ds(pl.multiple_of((1 - info_ref[0]) * half, 16), half), :]


def decoder_ff_call(
    sizes, info, x, mixed, cot, gains, shifts, w_out, bias_out, w_up, bias_up, w_down, share
):
    rows, width = x.shape
    units = w_up.shape[1]
    chunk = units // 4
    all_rows = sizes.all(width)
    half = sds((sizes.strips, sizes.length, width // 2))
    up_sums = pl.BlockSpec((8, chunk), lambda i, info: (0, i))
    folds = units // width if share % 8 == 0 else 0
    beside = units + width + (units if folds else 0)
    halves = [(width // 2, beside)] * 2 + ([] if folds else [(units // 2, width)] * 2)
    return call(
        functools.partial(decoder_ff_kernel, sizes=sizes, folds=folds, share=share, units=units),
        (
            half,
            half,
            sds((rows, width)),
            sds((rows, width)),
            sds((8, width), jnp.float32),
            sds((8, units), jnp.float32),
            *[sds(shape) for shape in halves],
        ),
        (4,),
        sizes.raw(width)
        + [all_rows, all_rows]
        + [whole(w) for w in (gains, shifts, w_out, bias_out)]
        + [
            pl.BlockSpec((width, chunk), lambda i, info: (0, i)),
            whole(bias_up),
            pl.BlockSpec((chunk, width), lambda i, info: (i, 0)),
        ],
        (
            sizes.half(width // 2),
            sizes.half(width // 2),
            all_rows,
            all_rows,
            sizes.sums(width),
            up_sums,
            *[pl.BlockSpec(shape, lambda i, info: (0, 0)) for shape in halves],
        ),
        2 * rows * width * (3 * width + 6 * units),
        rows * width * 16 + 4 * width * (width + 2 * units),
        exps=rows * units,
        name="decoder_feed_forward",
        scratch=[
            pltpu.VMEM((rows, width), jnp.bfloat16),
            pltpu.VMEM((rows, width), jnp.bfloat16),
            pltpu.VMEM((rows, chunk), jnp.bfloat16),
            pltpu.VMEM((rows, chunk), jnp.bfloat16),
            pltpu.VMEM((rows, width), jnp.float32),
            pltpu.VMEM((rows, width), jnp.float32),
            pltpu.VMEM((rows, width), jnp.float32),
            pltpu.VMEM((1, units), jnp.float32),
            pltpu.VMEM((width, beside), jnp.bfloat16),
            pltpu.VMEM((16 if folds else units, width), jnp.bfloat16),
        ],
    )(info, *[cot] * sizes.strips, x, mixed, gains, shifts, w_out, bias_out, w_up, bias_up, w_down)


def encoder_ff_back_kernel(
    info_ref,
    grad_ref,
    mid_ref,
    slope_ref,
    gain_ref,
    shift_ref,
    w_out_ref,
    w_up_ref,
    w_down_ref,
    dhidden_ref,
    gb_ref,
    dmixed_ref,
    sums_ref,
    up_sums_ref,
    dnormed_ref,
    *,
    sizes
):
    places = [sizes.place(strip) for strip in range(sizes.strips)]

    @first_step
    def begin():
        dnormed_ref[...] = jnp.zeros_like(dnormed_ref)

    dact = [dot(grad_ref[place, :], w_down_ref[...], NT) for place in places]
    up_sums = jnp.zeros((1, w_up_ref.shape[1]), jnp.float32)
    for place, values in zip(places, dact):
        dhidden = low(values * slope_ref[place, :].astype(jnp.float32))
        dhidden_ref[place, :] = dhidden
        up_sums = up_sums + col_sum(dhidden.astype(jnp.float32))
        dnormed_ref[place, :] += dot(dhidden, w_up_ref[...], NT)
    up_sums_ref[0:1, :] = up_sums

    @last_step
    def finish():
        gain, shift = row_of(gain_ref, 1), row_of(shift_ref, 1)
        totals = []
        for place in places:
            _, unit, inverse = norm(mid_ref[place, :].astype(jnp.float32), gain, shift)
            grad = grad_ref[place, :].astype(jnp.float32)
            dnormed = dnormed_ref[place, :]
            gb = low(grad + norm_back(dnormed, unit, inverse, gain))
            gb_ref[place, :] = gb
            dmixed_ref[place, :] = low(dot(gb, w_out_ref[...], NT))
            totals.append(
                (
                    col_sum(dnormed * unit),
                    col_sum(dnormed),
                    col_sum(gb.astype(jnp.float32)),
                    col_sum(grad),
                )
            )
        set_rows(sums_ref, [sum(rows) for rows in zip(*totals)])


def encoder_ff_back_call(sizes, info, grad, mid, slope, gains, shifts, w_out, w_up, w_down, after):
    rows, width = grad.shape
    units = w_up.shape[1]
    chunk = units // 4
    all_rows, cols = sizes.all(width), sizes.cols(chunk)
    return call(
        functools.partial(encoder_ff_back_kernel, sizes=sizes),
        (
            sds((rows, units)),
            sds((rows, width)),
            sds((rows, width)),
            sds((8, width), jnp.float32),
            sds((8, units), jnp.float32),
        ),
        (4,),
        [all_rows, all_rows, cols, whole(gains), whole(shifts), whole(w_out)]
        + [
            pl.BlockSpec((width, chunk), lambda i, info: (0, i)),
            pl.BlockSpec((chunk, width), lambda i, info: (i, 0)),
        ],
        (
            cols,
            all_rows,
            all_rows,
            sizes.sums(width),
            pl.BlockSpec((8, chunk), lambda i, info: (0, i)),
        ),
        2 * rows * width * (width + 2 * units),
        rows * (width * 16 + units * 4) + 2 * width * (width + 2 * units),
        after=after,
        name="encoder_feed_forward_back",
        scratch=[pltpu.VMEM((rows, width), jnp.float32)],
    )(info, grad, mid, slope, gains, shifts, w_out, w_up, w_down)


def packed_back(grad_ref, w_ref):
    width = w_ref.shape[0]
    return sum(dot(grad_ref[j], w_ref[:, j * width : (j + 1) * width], NT) for j in range(3))


def decoder_back_kernel(
    info_ref,
    dpacked_ref,
    gm_ref,
    x_ref,
    source_ref,
    y_ref,
    encoded_ref,
    gain_ref,
    shift_ref,
    w_ref,
    w_proj_ref,
    enc_gain_ref,
    enc_shift_ref,
    grad_ref,
    sums_ref,
    enc_sums_ref,
    kept_ref,
    sent_ref,
    total_ref,
):
    dnormed = packed_back(dpacked_ref, w_ref)
    gain = row_of(gain_ref, 0)
    _, unit, inverse = norm(x_ref[...], gain, row_of(shift_ref, 0))
    dx = gm_ref[...].astype(jnp.float32) + norm_back(dnormed, unit, inverse, gain)
    picker = picker_of(source_ref, info_ref[STRIP + pl.program_id(0)])
    taken = dot(picker, low(dx), NN)
    last = taken.shape[0] - 1
    dproj = low(jnp.where(last_row(taken.shape[0]), 0.0, taken))
    term = dot(encoded_ref[...], dproj, TN)
    half = kept_ref.shape[0]

    @pl.when(pl.program_id(0) == 0)
    def begin():
        total_ref[...] = term

    @pl.when(pl.program_id(0) > 0)
    def more():
        total_ref[...] += term

    @pl.when(pl.program_id(0) == pl.num_programs(0) - 1)
    def finish():
        kept_ref[...] = low(total_ref[pl.ds(pl.multiple_of(info_ref[0] * half, 8), half), :])
        sent_ref[...] = low(total_ref[pl.ds(pl.multiple_of((1 - info_ref[0]) * half, 8), half), :])

    dencoded = low(dot(dproj, w_proj_ref[...], NT)).astype(jnp.float32)
    enc_gain = row_of(enc_gain_ref, 2)
    _, unit_final, inverse_final = norm(
        y_ref[...].astype(jnp.float32), enc_gain, row_of(enc_shift_ref, 2)
    )
    grad_ref[...] = low(norm_back(dencoded, unit_final, inverse_final, enc_gain))
    add_rows(
        sums_ref,
        (
            col_sum(dnormed * unit),
            col_sum(dnormed),
            taken[last : last + 1],
            col_sum(dproj.astype(jnp.float32)),
        ),
    )
    add_rows(enc_sums_ref, (col_sum(dencoded * unit_final), col_sum(dencoded)))


def decoder_back_call(
    sizes,
    info,
    dpacked,
    gm,
    x,
    source,
    y,
    encoded,
    gains,
    shifts,
    w_qkv,
    w_proj,
    enc_gains,
    enc_shifts,
    after,
):
    strips, padded, rows = sizes.strips, sizes.padded, sizes.rows
    width = x.shape[2]
    wide = y.shape[2]
    weights = (gains, shifts, w_qkv, w_proj, enc_gains, enc_shifts)
    strip = sizes.strip
    return call(
        decoder_back_kernel,
        (
            sds((strips, padded, wide)),
            sds((8, width), jnp.float32),
            sds((8, wide), jnp.float32),
            sds((wide // 2, width)),
            sds((wide // 2, width)),
        ),
        (strips, 1),
        [
            pl.BlockSpec((3, None, padded, width), lambda s, i, info: (0, s, 0, 0)),
            strip(width),
            strip(width),
            whole(source),
            strip(wide),
            strip(wide),
        ]
        + [whole(w) for w in weights],
        (
            strip(wide),
            sizes.sums(width),
            sizes.sums(wide),
            pl.BlockSpec((wide // 2, width), lambda s, i, info: (0, 0)),
            pl.BlockSpec((wide // 2, width), lambda s, i, info: (0, 0)),
        ),
        2 * rows * width * (3 * width + padded + 2 * wide),
        rows * (width * 16 + wide * 8) + 2 * width * (3 * width + wide),
        after=after,
        name="decoder_packed_back",
        scratch=[pltpu.VMEM((wide, width), jnp.float32)],
    )(info, dpacked, gm, x, source, y, encoded, *weights)


def encoder_back_kernel(info_ref, *refs, parts, length):
    grad_refs, w_refs = refs[:parts], refs[parts : 2 * parts]
    gb_ref, x_ref, gain_ref, shift_ref, kept_ref, sent_ref, sums_ref, dnormed_ref = refs[2 * parts :]
    term = sum(dot(grad_ref[...], w_ref[...], NT) for grad_ref, w_ref in zip(grad_refs, w_refs))

    @first_step
    def begin():
        dnormed_ref[...] = term

    @pl.when(pl.program_id(0) > 0)
    def more():
        dnormed_ref[...] += term

    @last_step
    def finish():
        dnormed = dnormed_ref[...]
        gain = row_of(gain_ref, 0)
        x = live_rows(x_ref[...], 0, length)
        _, unit, inverse = norm(x, gain, row_of(shift_ref, 0))
        dx = gb_ref[...].astype(jnp.float32) + norm_back(dnormed, unit, inverse, gain)
        store_halves(info_ref, kept_ref, sent_ref, dx)
        set_rows(sums_ref, (col_sum(dnormed * unit), col_sum(dnormed)))


def encoder_back_call(sizes, info, dpacked, gb, x, gains, shifts, w_qkv, strip, after):
    rows, width = gb.shape
    padded = sizes.padded
    half = sds((1, sizes.length, width // 2))
    parts = len(dpacked)
    here = width // parts
    half_spec = pl.BlockSpec((None, padded, width // 2), lambda j, info: (0, 0, 0))
    return call(
        functools.partial(encoder_back_kernel, parts=parts, length=sizes.length),
        (half, half, sds((8, width), jnp.float32)),
        (3,),
        [pl.BlockSpec((None, None, padded, here), lambda j, info: (j, strip, 0, 0))] * parts
        + [
            pl.BlockSpec((width, here), lambda j, info, part=part: (0, j * parts + part))
            for part in range(parts)
        ]
        + [
            pl.BlockSpec((padded, width), lambda j, info: (strip, 0)),
            sizes.raw(width)[strip],
            whole(gains),
            whole(shifts),
        ],
        (half_spec, half_spec, sizes.sums(width)),
        6 * rows * width * width // sizes.strips,
        rows * width * 12 // sizes.strips + 6 * width * width,
        after=after,
        name=f"encoder_packed_back_{strip}",
        scratch=[pltpu.VMEM((padded, width), jnp.float32)],
    )(info, *dpacked, *[w_qkv] * parts, gb, x, gains, shifts)


class Job:
    def __init__(self, left, right, row_step, col_step, offset):
        self.half = left.shape[1] // 2
        self.width = right.shape[1]
        self.rows = left.shape[0]
        self.row_step, self.col_step, self.offset = row_step, col_step, offset
        self.down = self.half // row_step
        self.across = self.width // col_step
        self.count = self.down * self.across

    def at(self, step):
        here = jnp.clip(step - self.offset, 0, self.count - 1)
        if self.across == 1:
            return here, 0
        if self.down == 1:
            return 0, here
        return here // self.across, here % self.across

    def left(self, pick):
        return pl.BlockSpec(
            (self.rows, self.row_step),
            lambda step, info: (0, pick(info[0]) * self.down + self.at(step)[0]),
        )

    def right(self):
        return pl.BlockSpec((self.rows, self.col_step), lambda step, info: (0, self.at(step)[1]))

    def out(self):
        return pl.BlockSpec((self.row_step, self.col_step), lambda step, info: self.at(step))


def product_kernel(info_ref, *refs, jobs):
    step = pl.program_id(0)
    out = 3 * len(jobs)
    for place, (offset, count) in enumerate(jobs):
        mine_ref, other_ref, right_ref = refs[3 * place : 3 * place + 3]
        kept_ref, sent_ref = refs[out + 2 * place : out + 2 * place + 2]

        @pl.when((step >= offset) & (step < offset + count))
        def product():
            right = right_ref[...]
            sent_ref[...] = low(dot(other_ref[...], right, TN))
            kept_ref[...] = low(dot(mine_ref[...], right, TN))


def product_call(info, products, name, after=()):
    jobs, operands, in_specs, out_specs, out_shape = [], [], [], [], []
    offset = flops = moved = 0
    for left, right, row_step, col_step in products:
        job = Job(left, right, row_step, col_step, offset)
        offset += job.count
        jobs.append(job)
        operands += [left, left, right]
        in_specs += [job.left(lambda own: own), job.left(lambda own: 1 - own), job.right()]
        out_specs += [job.out(), job.out()]
        out_shape += [sds((job.half, job.width))] * 2
        flops += 4 * job.rows * job.half * job.width
        moved += 2 * job.rows * (2 * job.half + job.width) + 4 * job.half * job.width
    outs = call(
        functools.partial(product_kernel, jobs=[(job.offset, job.count) for job in jobs]),
        tuple(out_shape),
        (offset,),
        in_specs,
        tuple(out_specs),
        flops,
        moved,
        after=after,
        name=name,
    )(info, *operands)
    return [outs[2 * place : 2 * place + 2] for place in range(len(jobs))]


class Chain:
    def __init__(self, pairs, order, parts):
        self.pairs = pairs
        self.bits = list(range(pairs.bit_length() - 1))
        self.order = [bit for bit in order if bit < len(self.bits)]
        self.order += [bit for bit in self.bits if bit not in self.order]
        self.parts, self.widths = [], []
        for kept, arrived in parts:
            width = kept.shape[1]
            self.widths.append(width)
            self.parts.append(tuple(array.reshape(pairs, -1, width) for array in (kept, arrived)))
        self.done = None

    def item(self):
        kept = self.parts[0][0]
        if not self.order:
            return ("last", self.parts, self.widths, None)
        bit = self.order[0]
        lower = sum(1 for other in self.bits if other < bit)
        return ("halve", self.parts, (kept.shape[0] >> (lower + 1), 1 << lower), bit)

    def take(self, outs):
        if not self.order:
            self.done = outs
            return []
        bit = self.order.pop(0)
        self.bits.remove(bit)
        kept, sent = outs
        route = [(place, place ^ (1 << bit)) for place in range(self.pairs)]
        self.parts = [(kept, lax.ppermute(sent, "dp", route))]
        return [sent]


class Total:
    def __init__(self, pairs, values):
        self.pairs = pairs
        bits = [1 << bit for bit in range((2 * pairs).bit_length() - 1)]
        self.left = [bits[-1:]] + [bits[place : place + 2] for place in range(0, len(bits) - 1, 2)]
        self.done = None
        self.launch(values)

    def launch(self, values):
        group = self.left.pop(0)
        masks = group + [sum(group)] if len(group) > 1 else group
        count = 2 * self.pairs
        arrived = [
            lax.ppermute(values, ("section", "dp"), [(place, place ^ mask) for place in range(count)])
            for mask in masks
        ]
        self.parts = [(values, *arrived)]
        self.sent = values

    def item(self):
        return ("add", self.parts, None, None)

    def take(self, outs):
        (values,) = outs
        if not self.left:
            self.done = values
            return []
        self.launch(values)
        return [values]


def in_thirds(kind, parts):
    return kind == "halve" and len(parts) == 1 and parts[0][0].shape[-1] % (3 * GROUP) == 0


def round_kernel(info_ref, *refs, items):
    place = 0
    out = sum(sum(widths) for _, widths, _, _, _, _ in items)
    for kind, widths, how, bit, count, split in items:
        pairs = []
        for width in widths:
            pairs.append(refs[place : place + width])
            place += width
        outs = refs[out : out + count]
        out += count
        run = functools.partial(round_item, info_ref, kind, pairs, how, bit, outs)
        if split:
            run()
        else:
            first_step(run)


def round_item(info_ref, kind, pairs, how, bit, outs):
    if kind == "add":
        outs[0][...] = sum(ref[...] for ref in pairs[0])
        return

    def total(pair, index):
        return pair[0][index].astype(jnp.float32) + pair[1][index].astype(jnp.float32)

    if kind == "last":
        start = 0
        values = [total(pair, 0) for pair in pairs]
        whole_row = values[0] if len(values) == 1 else jnp.concatenate(values, axis=1)
        for ref, width in zip(outs, how):
            ref[...] = whole_row[:, start : start + width]
            start += width
        return
    high, lower = how
    mine = (info_ref[BLOCK] >> bit) & 1
    for h in range(high):
        for l in range(lower):
            start = 0
            for pair in pairs:
                width = pair[0].shape[-1]
                for ref, chosen in zip(outs, (mine, 1 - mine)):
                    index = (h * 2 + chosen) * lower + l
                    ref[h * lower + l, :, start : start + width] = pair[0][index] + pair[1][index]
                start += width


def round_call(info, chains, name, after=(), through=()):
    items = [chain.item() for chain in chains]
    operands, specs, out_shape, out_specs, plain, counts, moved = [], [], [], [], [], [], 0
    for kind, parts, how, bit in items:
        split = in_thirds(kind, parts)
        for part in parts:
            operands += part
            moved += len(part) * part[0].size * part[0].dtype.itemsize
            if split:
                block = (*part[0].shape[:-1], part[0].shape[-1] // 3)
                specs += [pl.BlockSpec(block, lambda i, info: (0, 0, i))] * len(part)
            else:
                specs += [whole(array) for array in part]
        shape = parts[0][0].shape
        if kind == "add":
            shapes = [sds(shape, jnp.float32)]
        elif kind == "last":
            shapes = [sds((shape[1], width), jnp.float32) for width in how]
        else:
            width = sum(part[0].shape[-1] for part in parts)
            shapes = [sds((shape[0] // 2, shape[1], width))] * 2
        out_shape += shapes
        if split:
            out_specs += [
                pl.BlockSpec((*shape.shape[:-1], shape.shape[-1] // 3), lambda i, info: (0, 0, i))
                for shape in shapes
            ]
        else:
            out_specs += [whole(shape) for shape in shapes]
        counts.append(len(shapes))
        plain.append((kind, [len(part) for part in parts], how, bit, len(shapes), split))
    outs = call(
        functools.partial(round_kernel, items=plain),
        tuple(out_shape),
        (3 if any(item[-1] for item in plain) else 1,),
        specs,
        tuple(out_specs),
        moved,
        2 * moved,
        after=after,
        through=through,
        name=name,
    )(info, *operands)
    sent, start = [], 0
    for chain, count in zip(chains, counts):
        sent += chain.take(outs[start : start + count])
        start += count
    return sent, outs[start:]


def across(values):
    return lax.ppermute(values, "section", [(0, 1), (1, 0)])


def arrange_kernel(info_ref, *refs, strips):
    *sources, out_ref = refs
    holder = info_ref[STRIP + 2 * strips + pl.program_id(0)]
    slot = info_ref[STRIP + 4 * strips + pl.program_id(0)]
    per = len(sources) // 2
    values = None
    for place in range(strips):
        kept, arrived = (
            (sources[place][0], sources[per + place][0])
            if per == strips
            else (sources[0][place], sources[1][place])
        )
        chosen = jnp.where(holder == info_ref[0], kept, arrived)
        values = chosen if values is None else jnp.where(slot == place, chosen, values)
    out_ref[0] = values


def arrange_call(info, kept, arrived, strips, name, after=()):
    _, length, half = kept[0].shape
    return call(
        functools.partial(arrange_kernel, strips=strips),
        sds((2 * strips, length, half)),
        (2 * strips,),
        [whole(array) for array in (*kept, *arrived)],
        pl.BlockSpec((1, length, half), lambda k, info: (k, 0, 0)),
        1,
        strips * length * half * 12,
        name=name,
        after=after,
    )(info, *kept, *arrived)


def gather_small_kernel(
    info_ref, up_enc, up_dec, enc, dec, dec_in, final, *rest
):
    *enc_in, out_ref = rest
    out_ref[...] = jnp.zeros_like(out_ref)
    wide, narrow = enc.shape[1], dec.shape[1]
    out_ref[0:1, : up_enc.shape[1]] = up_enc[0:1, :]
    out_ref[1:2, : up_dec.shape[1]] = up_dec[0:1, :]
    out_ref[2:6, :wide] = enc[0:4, :]
    out_ref[2:6, wide : wide + narrow] = dec[0:4, :]
    out_ref[2:6, wide + narrow : wide + 2 * narrow] = dec_in[0:4, :]
    out_ref[6:8, :wide] = final[0:2, :]
    out_ref[6:8, wide : 2 * wide] = sum(ref[0:2, :] for ref in enc_in)


def gather_small_call(info, values):
    shape = (8, values[0].shape[1])
    return call(
        gather_small_kernel,
        sds(shape, jnp.float32),
        (1,),
        [whole(value) for value in values],
        pl.BlockSpec(shape, lambda i, info: (0, 0)),
        shape[1],
        shape[1] * 64,
        name="small_rows",
    )(info, *values)


def unshuffled(parts):
    return jnp.concatenate(
        [
            part[:, (3 * group + j) * GROUP : (3 * group + j + 1) * GROUP]
            for j in range(3)
            for part in parts
            for group in range(part.shape[1] // (3 * GROUP))
        ],
        axis=1,
    )


def shares_kernel(info_ref, rows_ref, dec_qkv_ref, *refs, parts, wide, narrow, units, dec_units, count):
    block = info_ref[BLOCK]

    def share(first, last, start, width):
        values = rows_ref[first:last, start : start + width]
        part = width // count
        return pltpu.roll(values, width - block * part, 1)[:, :part]

    enc_qkv = [ref[...] for ref in refs[:parts]]
    outs = refs[parts:]
    bias_up_enc = share(0, 1, 0, units)
    bias_up_dec = share(1, 2, 0, dec_units)
    enc = share(2, 6, 0, wide)
    dec = share(2, 6, wide, narrow)
    dec_in = share(2, 6, wide + narrow, narrow)
    final = share(6, 8, 0, wide)
    enc_in = share(6, 8, wide, wide)
    for ref, value in zip(
        outs,
        (
            jnp.concatenate([enc_in[0:1], enc[0:1], final[0:1]], axis=0),
            jnp.concatenate([enc_in[1:2], enc[1:2], final[1:2]], axis=0),
            enc[2:4],
            bias_up_enc,
            dec_in[3:4],
            dec_in[2:3],
            jnp.concatenate([dec_in[0:1], dec[0:1]], axis=0),
            jnp.concatenate([dec_in[1:2], dec[1:2]], axis=0),
            dec[2:4],
            bias_up_dec,
            unshuffled([dec_qkv_ref[...]]),
            unshuffled(enc_qkv),
        ),
    ):
        ref[...] = value


def shares_call(info, rows, dec_qkv, enc_qkv, wide, narrow, units, dec_units, count):
    shapes = [
        (height, width // count)
        for height, width in (
            (3, wide),
            (3, wide),
            (2, wide),
            (1, units),
            (1, narrow),
            (1, narrow),
            (2, narrow),
            (2, narrow),
            (2, narrow),
            (1, dec_units),
        )
    ] + [dec_qkv.shape, (wide // count, 3 * wide)]
    return call(
        functools.partial(
            shares_kernel,
            parts=len(enc_qkv),
            wide=wide,
            narrow=narrow,
            units=units,
            dec_units=dec_units,
            count=count,
        ),
        tuple(sds(shape, jnp.float32) for shape in shapes),
        (1,),
        [whole(array) for array in (rows, dec_qkv, *enc_qkv)],
        tuple(pl.BlockSpec(shape, lambda i, info: (0, 0)) for shape in shapes),
        rows.size,
        rows.size * 4,
        name="shares",
    )(info, rows, dec_qkv, *enc_qkv)


def decoder_shares_kernel(info_ref, rows_ref, up_ref, out_ref, down_ref):
    width = out_ref.shape[1]
    units = up_ref.shape[1]
    share = up_ref.shape[0]
    rows = rows_ref[...]
    up_ref[...] = rows[:, :units]
    out_ref[...] = rows[:, units : units + width]
    for fold in range(units // width):
        start = units + (fold + 1) * width
        down_ref[fold * share : (fold + 1) * share, :] = rows[:, start : start + width]


def decoder_shares_call(info, rows, width, units, after):
    share = rows.shape[0]
    shapes = ((share, units), (share, width), (share * units // width, width))
    return call(
        decoder_shares_kernel,
        tuple(sds(shape, jnp.float32) for shape in shapes),
        (1,),
        [whole(rows)],
        tuple(pl.BlockSpec(shape, lambda i, info: (0, 0)) for shape in shapes),
        rows.size,
        rows.size * 6,
        name="decoder_shares",
        after=after,
    )(info, rows)


def place_table(length_rows, model_width):
    halfway = model_width // 2
    places = np.arange(length_rows, dtype=np.float64)[:, None]
    rates = np.exp(np.arange(halfway, dtype=np.float64) * (-math.log(10000.0) / halfway))[None, :]
    return np.concatenate([np.sin(places * rates), np.cos(places * rates)], axis=1).astype(
        np.float32
    )


def local(
    patches,
    visible,
    source,
    enc_gains,
    enc_shifts,
    enc_qkv,
    enc_out,
    enc_bias_out,
    enc_up,
    enc_bias_up,
    enc_down,
    enc_proj,
    proj_bias,
    mask_token,
    dec_gains,
    dec_shifts,
    dec_qkv,
    dec_out,
    dec_bias_out,
    dec_up,
    dec_bias_up,
    dec_down,
    cotangent,
):
    pairs = lax.axis_size("dp")
    count = 2 * pairs
    length = patches.shape[1]
    wide = patches.shape[2]
    narrow = dec_qkv.shape[0]
    strips = patches.shape[0] // 2
    padded = -(-(length + 1) // ROW_STEP) * ROW_STEP
    sizes = Sizes(strips, length, padded)
    rows = sizes.rows
    info = place_info(visible, strips)
    taken = jnp.pad(
        jnp.where(source < 0, padded - 1, source),
        ((0, 0), (0, padded - length)),
        constant_values=padded - 1,
    )
    places = jnp.asarray(place_table(padded, narrow))
    strip_form = lambda array: array.reshape(strips, padded, array.shape[-1])
    row_form = lambda array: array.reshape(rows, array.shape[-1])

    n1_enc, packed_enc = packed_call(sizes, info, patches, enc_gains, enc_shifts, enc_qkv)
    packed_enc = strip_form(packed_enc)
    enc_live = visible_live(strips)
    mixed_enc, scales_enc = attend_call(
        packed_enc, info, HEADS_ENC, enc_live, "encoder_attention"
    )
    mixed_enc = row_form(mixed_enc)
    mid_enc, n2_enc, act_enc, slope_enc, y_enc, encoded, projected = encoder_ff_call(
        sizes,
        info,
        patches,
        mixed_enc,
        enc_gains,
        enc_shifts,
        enc_out,
        enc_bias_out,
        enc_up,
        enc_bias_up,
        enc_down,
        enc_proj,
        proj_bias,
    )
    x_dec, n1_dec, packed_dec = decoder_in_call(
        sizes, info, projected, taken, mask_token, places, dec_gains, dec_shifts, dec_qkv
    )
    x_dec, n1_dec, packed_dec = map(strip_form, (x_dec, n1_dec, packed_dec))
    dec_live = all_live(length)
    mixed_dec, scales_dec = attend_call(
        packed_dec, info, HEADS_DEC, dec_live, "decoder_attention"
    )
    mixed_dec = row_form(mixed_dec)
    share = narrow // count
    (
        kept_dec,
        sent_dec,
        gb_dec,
        dmixed_dec,
        sums_dec,
        up_sums_dec,
        kept_beside,
        sent_beside,
        *apart,
    ) = decoder_ff_call(
        sizes,
        info,
        row_form(x_dec),
        mixed_dec,
        cotangent,
        dec_gains,
        dec_shifts,
        dec_out,
        dec_bias_out,
        dec_up,
        dec_bias_up,
        dec_down,
        share,
    )
    arrived_beside, arrived_dec = map(across, (sent_beside, sent_dec))
    enc_half = wide // 2
    dpacked_dec, kept_dqkv, sent_dqkv = attend_back_call(
        packed_dec,
        strip_form(dmixed_dec),
        strip_form(mixed_dec),
        scales_dec,
        n1_dec,
        info,
        HEADS_DEC,
        dec_live,
        0,
        1,
        (sent_beside, sent_dec),
        "decoder_attention_back",
    )
    arrived_dqkv = across(sent_dqkv)
    decoded = arrange_call(info, [kept_dec], [arrived_dec], strips, "decoded_strips", (dpacked_dec,))
    grad_enc, sums_dec_in, sums_final, kept_proj, sent_proj = decoder_back_call(
        sizes,
        info,
        dpacked_dec,
        strip_form(gb_dec),
        x_dec,
        taken,
        strip_form(y_enc),
        strip_form(encoded),
        dec_gains,
        dec_shifts,
        dec_qkv,
        enc_proj,
        enc_gains,
        enc_shifts,
        (sent_dqkv, decoded),
    )
    grad_enc = row_form(grad_enc)
    arrived_proj = across(sent_proj)
    ((kept_edown, sent_edown),) = product_call(
        info, [(act_enc, grad_enc, enc_half, wide)], "grad_enc_down", (sent_proj,)
    )
    grads_dec = Chain(
        pairs, (0, 1, 2, 3), ((kept_beside, arrived_beside), (kept_dqkv, arrived_dqkv))
    )
    sent, (sent_edown,) = round_call(
        info, [grads_dec], "round_1", (kept_edown, arrived_proj), (sent_edown,)
    )
    arrived_edown = across(sent_edown)
    dhid_enc, gb_enc, dmixed_enc, sums_enc, up_sums_enc = encoder_ff_back_call(
        sizes,
        info,
        grad_enc,
        mid_enc,
        slope_enc,
        enc_gains,
        enc_shifts,
        enc_out,
        enc_up,
        enc_down,
        (*sent, sent_edown),
    )
    (kept_eup, sent_eup), (kept_eout, sent_eout) = product_call(
        info,
        [(n2_enc, dhid_enc, enc_half, wide), (mixed_enc, gb_enc, enc_half, wide)],
        "grad_enc_up_out",
        sent,
    )
    down_enc = Chain(pairs, (0, 2, 1, 3), ((kept_edown, arrived_edown),))
    sent, (sent_eup, sent_eout) = round_call(
        info, [down_enc, grads_dec], "round_2", (kept_eout,), (sent_eup, sent_eout)
    )
    arrived_eup, arrived_eout = map(across, (sent_eup, sent_eout))
    up_enc = Chain(pairs, (1, 0, 2, 3), ((kept_eup, arrived_eup),))
    out_enc = Chain(pairs, (0, 1, 2, 3), ((kept_eout, arrived_eout), (kept_proj, arrived_proj)))
    every = [up_enc, down_enc, grads_dec, out_enc]
    active = lambda: [chain for chain in every if chain.done is None]
    after = (*sent, sent_eup, sent_eout)
    number, dpacked_enc, qkv_enc = 3, [], []
    by_y, by_z = (1, 0, 2, 3), (2, 0, 1, 3)
    for part in range(PARTS):
        dpacked, kept, sent_here = attend_back_call(
            packed_enc,
            strip_form(dmixed_enc),
            strip_form(mixed_enc),
            scales_enc,
            strip_form(n1_enc),
            info,
            HEADS_ENC,
            enc_live,
            part,
            PARTS,
            after,
            f"encoder_attention_back_{part}",
        )
        dpacked_enc.append(dpacked)
        sent, (sent_here,) = round_call(info, active(), f"round_{number}", (dpacked,), (sent_here,))
        chain = Chain(pairs, (by_z, by_y)[part % 2], ((kept, across(sent_here)),))
        number += 1
        qkv_enc.append(chain)
        every.append(chain)
        after = (*sent, sent_here)
    kept_enc, sent_enc, sums_enc_in = [], [], []
    for strip in range(strips):
        kept, sent_here, sums = encoder_back_call(
            sizes, info, dpacked_enc, gb_enc, patches, enc_gains, enc_shifts, enc_qkv, strip, after
        )
        kept_enc.append(kept)
        sums_enc_in.append(sums)
        sent_enc.append(sent_here)
        through = ()
        if strip == strips - 1:
            through = tuple(sent_enc)
            if apart:
                down_dec = Chain(pairs, by_y, ((apart[0], across(apart[1])),))
                every.append(down_dec)
            small = gather_small_call(
                info,
                (
                    up_sums_enc,
                    up_sums_dec,
                    sums_enc,
                    sums_dec,
                    sums_dec_in,
                    sums_final,
                    *sums_enc_in,
                ),
            )
            through += (small,)
        sent, through = round_call(info, active(), f"round_{number}", (sums,), through)
        number += 1
        after = (*sent,)
    *sent_enc, small = through
    arrived_enc = [across(array) for array in sent_enc]
    small = Total(pairs, small)
    every.append(small)
    patch_grad = arrange_call(info, kept_enc, arrived_enc, strips, "patch_grad_strips", after)
    after = (patch_grad,)
    while active():
        round_call(info, active(), f"round_{number}", after)
        after = ()
        number += 1
    g_beside, g_dqkv = grads_dec.done
    shares = shares_call(
        info,
        small.done,
        g_dqkv,
        [chain.done[0] for chain in qkv_enc],
        wide,
        narrow,
        enc_up.shape[1],
        dec_up.shape[1],
        count,
    )
    if apart:
        g_dup, g_dout = g_beside[:, : dec_up.shape[1]], g_beside[:, dec_up.shape[1] :]
        (g_ddown,) = down_dec.done
    else:
        g_dup, g_dout, g_ddown = decoder_shares_call(info, g_beside, narrow, dec_up.shape[1], ())
    (g_edown,), (g_eup,) = down_enc.done, up_enc.done
    g_eout, g_proj = out_enc.done
    return (
        decoded,
        patch_grad,
        shares[0],
        shares[1],
        shares[11],
        g_eout,
        shares[2],
        g_eup,
        shares[3].reshape(-1),
        g_edown,
        g_proj,
        shares[4].reshape(-1),
        shares[5].reshape(-1),
        shares[6],
        shares[7],
        shares[10],
        g_dout,
        shares[8],
        g_dup,
        shares[9].reshape(-1),
        g_ddown,
    )


def solution(mesh):
    return jax.shard_map(
        local,
        mesh=mesh,
        in_specs=(
            P("dp", None, None),
            P("dp"),
            P("dp", None),
            P(),
            P(),
            P(),
            P(),
            P(),
            P(),
            P(),
            P(),
            P(),
            P(),
            P(),
            P(),
            P(),
            P(),
            P(),
            P(),
            P(),
            P(),
            P(),
            P("dp", None, None),
        ),
        out_specs=(
            P("dp", None, "section"),
            P("dp", None, "section"),
            P(None, ("section", "dp")),
            P(None, ("section", "dp")),
            P(("section", "dp"), None),
            P(("section", "dp"), None),
            P(None, ("section", "dp")),
            P(("section", "dp"), None),
            P(("section", "dp")),
            P(("section", "dp"), None),
            P(("section", "dp"), None),
            P(("section", "dp")),
            P(("section", "dp")),
            P(None, ("section", "dp")),
            P(None, ("section", "dp")),
            P(("section", "dp"), None),
            P(("section", "dp"), None),
            P(None, ("section", "dp")),
            P(("section", "dp"), None),
            P(("section", "dp")),
            P(("section", "dp"), None),
        ),
        check_vma=False,
    )
```

```python
import functools
import math

import jax
import jax.numpy as jnp
import numpy as np
from jax import lax
from jax.experimental import pallas as pl
from jax.experimental.pallas import tpu as pltpu
from jax.sharding import PartitionSpec as P

HEADS_ENC = 12
HEADS_DEC = 16
ROW_STEP = 32
GROUP = 128
PARTS = 2
VMEM_BYTES = 63 * 1024 * 1024
MASKED = -1e30
LOG2E = math.log2(math.e)

epsilon = 1e-06

NN = (((1,), (0,)), ((), ()))
NT = (((1,), (1,)), ((), ()))
TN = (((0,), (0,)), ((), ()))


def dot(left_side, right_side, dims):
    return lax.dot_general(left_side, right_side, dims, preferred_element_type=jnp.float32)


def low(values):
    return values.astype(jnp.bfloat16)


def call(
    kernel, out_shape, grid, in_specs, out_specs, flops, moved, scalars=1, exps=0, after=(), name=None, scratch=(), through=()
):
    count = scalars + len(in_specs)
    ordered = [pl.BlockSpec(memory_space=pl.ANY)] * (len(after) + len(through))
    aliases = {}
    if through:
        outs = len(out_shape)
        aliases = {count + len(after) + place: outs + place for place in range(len(through))}
        out_shape = tuple(out_shape) + tuple(sds(array.shape, array.dtype) for array in through)
        out_specs = tuple(out_specs) + (pl.BlockSpec(memory_space=pl.ANY),) * len(through)

    def body(*refs):
        ins, rest = refs[:count], refs[count + len(after) + len(through) :]
        if through:
            rest = rest[:outs] + rest[outs + len(through) :]
        kernel(*ins, *rest)

    made = pl.pallas_call(
        body,
        out_shape=out_shape,
        grid_spec=pltpu.PrefetchScalarGridSpec(
            num_scalar_prefetch=scalars,
            grid=grid,
            in_specs=list(in_specs) + ordered,
            out_specs=out_specs,
            scratch_shapes=list(scratch),
        ),
        input_output_aliases=aliases,
        compiler_params=pltpu.CompilerParams(vmem_limit_bytes=VMEM_BYTES),
        cost_estimate=pl.CostEstimate(flops=flops, bytes_accessed=moved, transcendentals=exps),
        name=name,
    )
    return lambda *operands: made(*operands, *after, *through)


def whole(array):
    rank = array.ndim
    return pl.BlockSpec(array.shape, lambda *unused: (0,) * rank)


def row_of(ref, place):
    return ref[place : place + 1, :].astype(jnp.float32)


def vector_of(ref):
    return ref[...].astype(jnp.float32).reshape(1, -1)


def padded_rows(ref, pad_ref):
    length, padded = ref.shape[0], pad_ref.shape[0]
    first = length // 8 * 8
    pad_ref[first:, :] = jnp.zeros((padded - first, pad_ref.shape[1]), jnp.float32)
    pad_ref[:length, :] = ref[...].astype(jnp.float32)
    return pad_ref[...]


def sds(shape, kind=jnp.bfloat16):
    return jax.ShapeDtypeStruct(shape, kind)


def norm(values, gain_row, shift_row):
    center = values - jnp.mean(values, axis=-1, keepdims=True)
    inverse = lax.rsqrt(jnp.mean(center * center, axis=-1, keepdims=True) + epsilon)
    unit = center * inverse
    return unit * gain_row + shift_row, unit, inverse


def norm_back(grad_out, unit, inverse, gain_row):
    scaled = grad_out * gain_row
    return inverse * (
        scaled
        - jnp.mean(scaled, axis=-1, keepdims=True)
        - unit * jnp.mean(scaled * unit, axis=-1, keepdims=True)
    )


def col_sum(values):
    return jnp.sum(values, axis=0, keepdims=True)


def gelu_parts(values):
    share = 0.5 + 0.5 * lax.erf(values * math.sqrt(0.5))
    bell = jnp.exp2(values * values * (-0.5 * LOG2E)) * (1.0 / math.sqrt(2.0 * math.pi))
    return values * share, share + values * bell


def add_rows(ref, rows):
    @pl.when((pl.program_id(0) == 0) & (pl.program_id(1) == 0))
    def start():
        ref[...] = jnp.zeros_like(ref)

    for place, row in enumerate(rows):
        ref[place : place + 1, :] += row


BLOCK = 1
STRIP = 2


def place_info(visible, strips):
    section_index = lax.axis_index("section")
    block = section_index * lax.axis_size("dp") + lax.axis_index("dp")
    mine = section_index * strips + jnp.arange(strips, dtype=jnp.int32)
    every = jnp.arange(2 * strips, dtype=jnp.int32)
    return jnp.concatenate(
        [
            jnp.stack([section_index, block]),
            mine,
            lax.dynamic_slice_in_dim(visible, section_index * strips, strips, 0),
            every // strips,
            every % strips,
        ]
    ).astype(jnp.int32)


class Sizes:
    def __init__(self, strips, length, padded):
        self.strips, self.length, self.padded = strips, length, padded
        self.rows = strips * padded

    def place(self, strip):
        return slice(strip * self.padded, (strip + 1) * self.padded)

    def raw(self, width):
        return [
            pl.BlockSpec(
                (None, self.length, width), lambda *step, s=s: (step[-1][STRIP + s], 0, 0)
            )
            for s in range(self.strips)
        ]

    def all(self, width):
        return pl.BlockSpec((self.rows, width), lambda *step: (0, 0))

    def cols(self, width):
        return pl.BlockSpec((self.rows, width), lambda i, info: (0, i))

    def half(self, width):
        return pl.BlockSpec((self.strips, self.length, width), lambda *step: (0, 0, 0))

    def sums(self, width):
        return pl.BlockSpec((8, width), lambda *step: (0, 0))

    def strip(self, width):
        return pl.BlockSpec((None, self.padded, width), lambda s, i, info: (s, 0, 0))


def first_step(run):
    pl.when(pl.program_id(0) == 0)(run)


def last_step(run):
    pl.when(pl.program_id(0) == pl.num_programs(0) - 1)(run)


def store_halves(info_ref, kept_ref, sent_ref, values):
    length, half = kept_ref.shape
    first = info_ref[0] == 0
    values = values[:length]
    kept_ref[...] = low(jnp.where(first, values[:, :half], values[:, half:]))
    sent_ref[...] = low(jnp.where(first, values[:, half:], values[:, :half]))


def set_rows(ref, rows):
    for place, row in enumerate(rows):
        ref[place : place + 1, :] = row


def packed_kernel(info_ref, *refs, sizes):
    x_refs = refs[: sizes.strips]
    gain_ref, shift_ref, w_ref, n_ref, packed_ref, pad_ref = refs[sizes.strips :]

    @first_step
    def normalize():
        for strip, x_ref in enumerate(x_refs):
            x = padded_rows(x_ref, pad_ref)
            normed, _, _ = norm(x, row_of(gain_ref, 0), row_of(shift_ref, 0))
            n_ref[sizes.place(strip), :] = low(normed)

    packed_ref[...] = low(dot(n_ref[...], w_ref[...], NN))


def packed_call(sizes, info, x, gains, shifts, w_qkv):
    rows, width = sizes.rows, x.shape[2]
    return call(
        functools.partial(packed_kernel, sizes=sizes),
        (sds((rows, width)), sds((rows, 3 * width))),
        (3,),
        sizes.raw(width)
        + [whole(gains), whole(shifts), pl.BlockSpec((width, width), lambda i, info: (0, i))],
        (sizes.all(width), sizes.cols(width)),
        6 * rows * width * width,
        rows * width * 10 + 6 * width * width,
        name="encoder_packed",
        scratch=[pltpu.VMEM((sizes.padded, width), jnp.float32)],
    )(info, *[x] * sizes.strips, gains, shifts, w_qkv)


def picker_of(source_ref, strip):
    taken = source_ref[pl.ds(strip, 1), :]
    length = taken.shape[1]
    return low(jnp.where(taken == lax.broadcasted_iota(jnp.int32, (length, length), 0), 1.0, 0.0))


def last_row(length):
    return lax.broadcasted_iota(jnp.int32, (length, 1), 0) == length - 1


def decoder_in_kernel(
    info_ref,
    rows_ref,
    source_ref,
    mask_ref,
    places_ref,
    gain_ref,
    shift_ref,
    w_ref,
    x_ref,
    n_ref,
    packed_ref,
    *,
    sizes
):
    @first_step
    def gather():
        for strip in range(sizes.strips):
            place = sizes.place(strip)
            picker = picker_of(source_ref, info_ref[STRIP + strip])
            rows = jnp.where(
                last_row(sizes.padded), vector_of(mask_ref), rows_ref[place, :].astype(jnp.float32)
            )
            x = dot(picker, low(rows), TN) + places_ref[...]
            x_ref[place, :] = x
            normed, _, _ = norm(x, row_of(gain_ref, 0), row_of(shift_ref, 0))
            n_ref[place, :] = low(normed)

    packed_ref[...] = low(dot(n_ref[...], w_ref[...], NN))


def decoder_in_call(sizes, info, projected, source, mask_row, places, gains, shifts, w_qkv):
    width = projected.shape[1]
    rows = sizes.rows
    return call(
        functools.partial(decoder_in_kernel, sizes=sizes),
        (sds((rows, width), jnp.float32), sds((rows, width)), sds((rows, 3 * width))),
        (3,),
        [sizes.all(width), whole(source), whole(mask_row), whole(places), whole(gains), whole(shifts)]
        + [pl.BlockSpec((width, width), lambda i, info: (0, i))],
        (sizes.all(width), sizes.all(width), sizes.cols(width)),
        6 * rows * width * width + 2 * rows * sizes.padded * width,
        rows * width * 18 + 6 * width * width,
        name="decoder_packed",
    )(info, projected, source, mask_row, places, gains, shifts, w_qkv)


def head_parts(head, heads_here):
    lane = lax.broadcasted_iota(jnp.int32, (1, GROUP), 1)
    size = GROUP // heads_here
    mine = (lane >= head * size) & (lane < (head + 1) * size)
    spare = ((head + 1) % heads_here) * size
    return mine, lane == spare, spare


def key_bias(live, length):
    row = lax.broadcasted_iota(jnp.int32, (length, 1), 0)
    return low(jnp.where(row < live, 0.0, MASKED))


def attend_kernel(info_ref, q_ref, k_ref, v_ref, out_ref, scale_ref, *, heads_here, live):
    length = q_ref.shape[1]
    rate = (GROUP // heads_here) ** -0.5 * LOG2E
    bias = key_bias(live(info_ref, pl.program_id(0)), length)
    one = jnp.bfloat16(1.0)
    middle = length // 2
    for group in range(q_ref.shape[2] // GROUP):
        columns = slice(group * GROUP, (group + 1) * GROUP)
        k, v = k_ref[0, :, columns], v_ref[0, :, columns]
        for rows in (slice(0, middle), slice(middle, length)):
            q = q_ref[0, rows, columns]
            mixed = jnp.zeros(q.shape, jnp.float32)
            tops = jnp.zeros(q.shape, jnp.float32)
            totals = jnp.ones(q.shape, jnp.float32)
            for head in range(heads_here):
                mine, at_spare, spare = head_parts(head, heads_here)
                head_q = jnp.where(mine, q, low(jnp.where(at_spare, 1.0, 0.0)))
                scores = dot(head_q, jnp.where(at_spare, bias, k), NT)
                highest = jnp.max(scores, axis=1, keepdims=True)
                terms = low(jnp.exp2((scores - highest) * rate))
                product = dot(terms, jnp.where(at_spare, one, v), NN)
                mixed = jnp.where(mine, product * (1.0 / product[:, spare : spare + 1]), mixed)
                tops = jnp.where(at_spare, highest, tops)
                totals = jnp.where(at_spare, product, totals)
            out_ref[0, rows, columns] = low(mixed)
            scales = (tops * rate + jnp.log2(totals)).T
            for head in range(heads_here):
                spare = head_parts(head, heads_here)[2]
                scale_ref[0, group, head : head + 1, rows] = scales[spare : spare + 1]


def all_live(length):
    return lambda info_ref, strip: length


def visible_live(strips):
    return lambda info_ref, strip: info_ref[STRIP + strips + strip]


def attend_call(packed, info, heads, live, name):
    strips, length, triple = packed.shape
    width = triple // 3
    heads_here = GROUP // (width // heads)
    steps = 2
    part = width // steps
    groups = part // GROUP
    third = lambda j: pl.BlockSpec((1, length, part), lambda s, g, _: (s, 0, g + j * steps))
    return call(
        functools.partial(attend_kernel, heads_here=heads_here, live=live),
        (sds((strips, length, width)), sds((strips, steps * groups, 8, length), jnp.float32)),
        (strips, steps),
        [third(0), third(1), third(2)],
        (third(0), pl.BlockSpec((1, groups, 8, length), lambda s, g, _: (s, g, 0, 0))),
        strips * heads * length * length * GROUP * 6,
        strips * length * width * 8,
        exps=strips * heads * length * length,
        name=name,
    )(info, packed, packed, packed)


def attend_back_kernel(
    info_ref,
    q_ref,
    k_ref,
    v_ref,
    dout_ref,
    mixed_ref,
    scale_ref,
    n_ref,
    grad_ref,
    kept_ref,
    sent_ref,
    total_ref,
    *,
    heads_here,
    live
):
    length = q_ref.shape[1]
    factor = (GROUP // heads_here) ** -0.5
    rate = factor * LOG2E
    strip = pl.program_id(1)
    q, k, v, dout = q_ref[0], k_ref[0], v_ref[0], dout_ref[0]
    bias = key_bias(live(info_ref, strip), length)
    k_turned = k.T
    agree = (dout.astype(jnp.float32) * mixed_ref[0].astype(jnp.float32)).T
    dq_turned = []
    dk = jnp.zeros((length, GROUP), jnp.float32)
    dv = jnp.zeros((length, GROUP), jnp.float32)
    size = GROUP // heads_here
    for head in range(heads_here):
        mine, at_spare, _ = head_parts(head, heads_here)
        head_q = jnp.where(mine, q, low(jnp.where(at_spare, 1.0, 0.0)))
        head_dout = jnp.where(mine, dout, jnp.bfloat16(0.0))
        scores = dot(jnp.where(at_spare, bias, k), head_q, NT)
        probs = jnp.exp2(scores * rate - scale_ref[0, 0, head : head + 1, :])
        average = jnp.sum(agree[head * size : (head + 1) * size], axis=0, keepdims=True)
        dscores = low(probs * (dot(v, head_dout, NT) - average))
        dk = jnp.where(mine, dot(dscores, q, NN), dk)
        dv = jnp.where(mine, dot(low(probs), dout, NN), dv)
        dq_turned.append(dot(k_turned[head * size : (head + 1) * size], dscores, NN))
    dq = low(jnp.concatenate(dq_turned, axis=0).T * factor)
    dk, dv = low(dk * factor), low(dv)
    grad_ref[0, 0] = dq
    grad_ref[1, 0] = dk
    grad_ref[2, 0] = dv
    term = dot(n_ref[0], jnp.concatenate([dq, dk, dv], axis=1), TN)
    half = kept_ref.shape[0]
    last = pl.num_programs(1) - 1

    @pl.when(strip == 0)
    def begin():
        total_ref[...] = term

    @pl.when(strip > 0)
    def more():
        total_ref[...] += term

    @pl.when(strip == last)
    def finish():
        kept_ref[...] = low(total_ref[pl.ds(pl.multiple_of(info_ref[0] * half, 8), half), :])
        sent_ref[...] = low(total_ref[pl.ds(pl.multiple_of((1 - info_ref[0]) * half, 8), half), :])


def attend_back_call(
    packed, dmixed, mixed, scales, normed, info, heads, live, part, parts, after, name
):
    strips, length, triple = packed.shape
    width = triple // 3
    heads_here = GROUP // (width // heads)
    groups = width // GROUP
    here = groups // parts
    third = lambda j: pl.BlockSpec(
        (1, length, GROUP), lambda g, s, _: (s, 0, g + part * here + j * groups)
    )
    product = pl.BlockSpec((width // 2, 3 * GROUP), lambda g, s, _: (0, g))
    return call(
        functools.partial(attend_back_kernel, heads_here=heads_here, live=live),
        (
            sds((3, strips, length, here * GROUP)),
            sds((width // 2, here * 3 * GROUP)),
            sds((width // 2, here * 3 * GROUP)),
        ),
        (here, strips),
        [
            third(0),
            third(1),
            third(2),
            third(0),
            third(0),
            pl.BlockSpec((1, 1, 8, length), lambda g, s, _: (s, g + part * here, 0, 0)),
            pl.BlockSpec((1, length, width), lambda g, s, _: (s, 0, 0)),
        ],
        (pl.BlockSpec((3, 1, length, GROUP), lambda g, s, _: (0, s, 0, g)), product, product),
        (strips * heads * length * length * GROUP * 12 + 6 * strips * length * width * width) // parts,
        strips * length * width * 14 // parts,
        exps=strips * heads * length * length // parts,
        after=after,
        name=name,
        scratch=[pltpu.VMEM((width, 3 * GROUP), jnp.float32)],
    )(info, packed, packed, packed, dmixed, mixed, scales, normed)


def encoder_ff_kernel(info_ref, *refs, sizes):
    x_refs = refs[: sizes.strips]
    (
        mixed_ref,
        gain_ref,
        shift_ref,
        w_out_ref,
        bias_out_ref,
        w_up_ref,
        bias_up_ref,
        w_down_ref,
        w_proj_ref,
        bias_proj_ref,
        mid_ref,
        n_ref,
        act_ref,
        slope_ref,
        y_low_ref,
        encoded_ref,
        projected_ref,
        y_ref,
        bias_ref,
        pad_ref,
    ) = refs[sizes.strips :]
    places = [sizes.place(strip) for strip in range(sizes.strips)]

    @first_step
    def middle():
        bias_ref[...] = vector_of(bias_up_ref)
        for place, x_ref in zip(places, x_refs):
            x = padded_rows(x_ref, pad_ref)
            mid = x + dot(mixed_ref[place, :], w_out_ref[...], NN) + row_of(bias_out_ref, 0)
            mid_ref[place, :] = low(mid)
            normed, _, _ = norm(mid, row_of(gain_ref, 1), row_of(shift_ref, 1))
            n_ref[place, :] = low(normed)
            y_ref[place, :] = mid + row_of(bias_out_ref, 1)

    chunk = w_up_ref.shape[1]
    bias = bias_ref[:, pl.ds(pl.multiple_of(pl.program_id(0) * chunk, GROUP), chunk)]
    hidden = [dot(n_ref[place, :], w_up_ref[...], NN) + bias for place in places]
    for place, values in zip(places, hidden):
        act, slope = gelu_parts(values)
        act = low(act)
        act_ref[place, :] = act
        slope_ref[place, :] = low(slope)
        y_ref[place, :] += dot(act, w_down_ref[...], NN)

    @last_step
    def finish():
        for place in places:
            y = y_ref[place, :]
            y_low_ref[place, :] = low(y)
            encoded, _, _ = norm(y, row_of(gain_ref, 2), row_of(shift_ref, 2))
            encoded = low(encoded)
            encoded_ref[place, :] = encoded
            projected_ref[place, :] = low(
                dot(encoded, w_proj_ref[...], NN) + vector_of(bias_proj_ref)
            )


def encoder_ff_call(
    sizes, info, x, mixed, gains, shifts, w_out, bias_out, w_up, bias_up, w_down, w_proj, bias_proj
):
    rows, width = sizes.rows, x.shape[2]
    units = w_up.shape[1]
    narrow = w_proj.shape[1]
    chunk = units // 4
    return call(
        functools.partial(encoder_ff_kernel, sizes=sizes),
        (
            sds((rows, width)),
            sds((rows, width)),
            sds((rows, units)),
            sds((rows, units)),
            sds((rows, width)),
            sds((rows, width)),
            sds((rows, narrow)),
        ),
        (4,),
        sizes.raw(width)
        + [sizes.all(width)]
        + [whole(w) for w in (gains, shifts, w_out, bias_out)]
        + [
            pl.BlockSpec((width, chunk), lambda i, info: (0, i)),
            whole(bias_up),
            pl.BlockSpec((chunk, width), lambda i, info: (i, 0)),
            whole(w_proj),
            whole(bias_proj),
        ],
        (
            sizes.all(width),
            sizes.all(width),
            sizes.cols(chunk),
            sizes.cols(chunk),
            sizes.all(width),
            sizes.all(width),
            sizes.all(narrow),
        ),
        2 * rows * width * (width + 2 * units + narrow),
        rows * (width * 16 + units * 4) + 2 * width * (width + 2 * units + narrow),
        exps=rows * units,
        name="encoder_feed_forward",
        scratch=[
            pltpu.VMEM((rows, width), jnp.float32),
            pltpu.VMEM((1, units), jnp.float32),
            pltpu.VMEM((sizes.padded, width), jnp.float32),
        ],
    )(
        info,
        *[x] * sizes.strips,
        mixed,
        gains,
        shifts,
        w_out,
        bias_out,
        w_up,
        bias_up,
        w_down,
        w_proj,
        bias_proj,
    )


def decoder_ff_kernel(info_ref, *refs, sizes, folds, share, units):
    cot_refs = refs[: sizes.strips]
    (
        x_ref,
        mixed_ref,
        gain_ref,
        shift_ref,
        w_out_ref,
        bias_out_ref,
        w_up_ref,
        bias_up_ref,
        w_down_ref,
        kept_ref,
        sent_ref,
        gb_ref,
        dmixed_ref,
        sums_ref,
        up_sums_ref,
        kept_up_ref,
        sent_up_ref,
        *down_refs,
        cot_ref,
        n_ref,
        act_ref,
        dhidden_ref,
        mid_ref,
        y_ref,
        dnormed_ref,
        bias_ref,
        beside_ref,
        down_ref,
        pad_ref,
    ) = refs[sizes.strips :]
    places = [sizes.place(strip) for strip in range(sizes.strips)]
    gain, shift = row_of(gain_ref, 1), row_of(shift_ref, 1)

    @first_step
    def middle():
        bias_ref[...] = vector_of(bias_up_ref)
        dnormed_ref[...] = jnp.zeros_like(dnormed_ref)
        for place, cot_here in zip(places, cot_refs):
            mid = x_ref[place, :] + dot(mixed_ref[place, :], w_out_ref[...], NN) + row_of(bias_out_ref, 0)
            mid_ref[place, :] = mid
            normed, _, _ = norm(mid, gain, shift)
            n_ref[place, :] = low(normed)
            y_ref[place, :] = mid + row_of(bias_out_ref, 1)
            cot_ref[place, :] = low(padded_rows(cot_here, pad_ref))

    chunk = w_up_ref.shape[1]
    bias = bias_ref[:, pl.ds(pl.multiple_of(pl.program_id(0) * chunk, GROUP), chunk)]
    hidden = [dot(n_ref[place, :], w_up_ref[...], NN) + bias for place in places]
    dact = [dot(cot_ref[place, :], w_down_ref[...], NT) for place in places]
    up_sums = jnp.zeros((1, chunk), jnp.float32)
    for place, values, grads in zip(places, hidden, dact):
        act, slope = gelu_parts(values)
        act = low(act)
        act_ref[place, :] = act
        y_ref[place, :] += dot(act, w_down_ref[...], NN)
        dhidden = low(grads * slope)
        dhidden_ref[place, :] = dhidden
        up_sums = up_sums + col_sum(dhidden.astype(jnp.float32))
        dnormed_ref[place, :] += dot(dhidden, w_up_ref[...], NT)
    up_sums_ref[0:1, :] = up_sums
    step, width = pl.program_id(0), n_ref.shape[1]
    beside_ref[:, pl.ds(pl.multiple_of(step * chunk, GROUP), chunk)] = low(
        dot(n_ref[...], dhidden_ref[...], TN)
    )
    down = dot(act_ref[...], cot_ref[...], TN)
    if folds:
        down = down.reshape(-1, folds, share, width)
        here = chunk // folds
        rows = pl.ds(pl.multiple_of(step * here, share), here)
        for fold in range(folds):
            start = (folds + 1 + fold) * width
            beside_ref[rows, start : start + width] = low(down[:, fold].reshape(here, width))
    else:
        down_ref[pl.ds(pl.multiple_of(step * chunk, GROUP), chunk), :] = low(down)

    @last_step
    def finish():
        totals = []
        for place in places:
            store_halves(info_ref, kept_ref.at[place], sent_ref.at[place], y_ref[place, :])
            _, unit, inverse = norm(mid_ref[place, :], gain, shift)
            grad = cot_ref[place, :].astype(jnp.float32)
            dnormed = dnormed_ref[place, :]
            gb = low(grad + norm_back(dnormed, unit, inverse, gain))
            gb_ref[place, :] = gb
            dmixed_ref[place, :] = low(dot(gb, w_out_ref[...], NT))
            totals.append(
                (
                    col_sum(dnormed * unit),
                    col_sum(dnormed),
                    col_sum(gb.astype(jnp.float32)),
                    col_sum(grad),
                )
            )
        set_rows(sums_ref, [sum(rows) for rows in zip(*totals)])
        beside_ref[:, units : units + width] = low(dot(mixed_ref[...], gb_ref[...], TN))
        for kept, sent, whole_ref in zip(
            (kept_up_ref, *down_refs[:1]), (sent_up_ref, *down_refs[1:]), (beside_ref, down_ref)
        ):
            half = kept.shape[0]
            kept[...] = whole_ref[pl.ds(pl.multiple_of(info_ref[0] * half, 16), half), :]
            sent[...] = whole_ref[pl.ds(pl.multiple_of((1 - info_ref[0]) * half, 16), half), :]


def decoder_ff_call(
    sizes, info, x, mixed, cot, gains, shifts, w_out, bias_out, w_up, bias_up, w_down, share
):
    rows, width = x.shape
    units = w_up.shape[1]
    chunk = units // 4
    all_rows = sizes.all(width)
    half = sds((rows, width // 2))
    up_sums = pl.BlockSpec((8, chunk), lambda i, info: (0, i))
    folds = units // width if share % 8 == 0 else 0
    beside = units + width + (units if folds else 0)
    halves = [(width // 2, beside)] * 2 + ([] if folds else [(units // 2, width)] * 2)
    return call(
        functools.partial(decoder_ff_kernel, sizes=sizes, folds=folds, share=share, units=units),
        (
            half,
            half,
            sds((rows, width)),
            sds((rows, width)),
            sds((8, width), jnp.float32),
            sds((8, units), jnp.float32),
            *[sds(shape) for shape in halves],
        ),
        (4,),
        sizes.raw(width)
        + [all_rows, all_rows]
        + [whole(w) for w in (gains, shifts, w_out, bias_out)]
        + [
            pl.BlockSpec((width, chunk), lambda i, info: (0, i)),
            whole(bias_up),
            pl.BlockSpec((chunk, width), lambda i, info: (i, 0)),
        ],
        (
            sizes.all(width // 2),
            sizes.all(width // 2),
            all_rows,
            all_rows,
            sizes.sums(width),
            up_sums,
            *[pl.BlockSpec(shape, lambda i, info: (0, 0)) for shape in halves],
        ),
        2 * rows * width * (3 * width + 6 * units),
        rows * width * 16 + 4 * width * (width + 2 * units),
        exps=rows * units,
        name="decoder_feed_forward",
        scratch=[
            pltpu.VMEM((rows, width), jnp.bfloat16),
            pltpu.VMEM((rows, width), jnp.bfloat16),
            pltpu.VMEM((rows, chunk), jnp.bfloat16),
            pltpu.VMEM((rows, chunk), jnp.bfloat16),
            pltpu.VMEM((rows, width), jnp.float32),
            pltpu.VMEM((rows, width), jnp.float32),
            pltpu.VMEM((rows, width), jnp.float32),
            pltpu.VMEM((1, units), jnp.float32),
            pltpu.VMEM((width, beside), jnp.bfloat16),
            pltpu.VMEM((16 if folds else units, width), jnp.bfloat16),
            pltpu.VMEM((sizes.padded, width), jnp.float32),
        ],
    )(info, *[cot] * sizes.strips, x, mixed, gains, shifts, w_out, bias_out, w_up, bias_up, w_down)


def encoder_ff_back_kernel(
    info_ref,
    grad_ref,
    mid_ref,
    slope_ref,
    gain_ref,
    shift_ref,
    w_out_ref,
    w_up_ref,
    w_down_ref,
    dhidden_ref,
    gb_ref,
    dmixed_ref,
    sums_ref,
    up_sums_ref,
    dnormed_ref,
    *,
    sizes
):
    places = [sizes.place(strip) for strip in range(sizes.strips)]

    @first_step
    def begin():
        dnormed_ref[...] = jnp.zeros_like(dnormed_ref)

    dact = [dot(grad_ref[place, :], w_down_ref[...], NT) for place in places]
    up_sums = jnp.zeros((1, w_up_ref.shape[1]), jnp.float32)
    for place, values in zip(places, dact):
        dhidden = low(values * slope_ref[place, :].astype(jnp.float32))
        dhidden_ref[place, :] = dhidden
        up_sums = up_sums + col_sum(dhidden.astype(jnp.float32))
        dnormed_ref[place, :] += dot(dhidden, w_up_ref[...], NT)
    up_sums_ref[0:1, :] = up_sums

    @last_step
    def finish():
        gain, shift = row_of(gain_ref, 1), row_of(shift_ref, 1)
        totals = []
        for place in places:
            _, unit, inverse = norm(mid_ref[place, :].astype(jnp.float32), gain, shift)
            grad = grad_ref[place, :].astype(jnp.float32)
            dnormed = dnormed_ref[place, :]
            gb = low(grad + norm_back(dnormed, unit, inverse, gain))
            gb_ref[place, :] = gb
            dmixed_ref[place, :] = low(dot(gb, w_out_ref[...], NT))
            totals.append(
                (
                    col_sum(dnormed * unit),
                    col_sum(dnormed),
                    col_sum(gb.astype(jnp.float32)),
                    col_sum(grad),
                )
            )
        set_rows(sums_ref, [sum(rows) for rows in zip(*totals)])


def encoder_ff_back_call(sizes, info, grad, mid, slope, gains, shifts, w_out, w_up, w_down, after):
    rows, width = grad.shape
    units = w_up.shape[1]
    chunk = units // 4
    all_rows, cols = sizes.all(width), sizes.cols(chunk)
    return call(
        functools.partial(encoder_ff_back_kernel, sizes=sizes),
        (
            sds((rows, units)),
            sds((rows, width)),
            sds((rows, width)),
            sds((8, width), jnp.float32),
            sds((8, units), jnp.float32),
        ),
        (4,),
        [all_rows, all_rows, cols, whole(gains), whole(shifts), whole(w_out)]
        + [
            pl.BlockSpec((width, chunk), lambda i, info: (0, i)),
            pl.BlockSpec((chunk, width), lambda i, info: (i, 0)),
        ],
        (
            cols,
            all_rows,
            all_rows,
            sizes.sums(width),
            pl.BlockSpec((8, chunk), lambda i, info: (0, i)),
        ),
        2 * rows * width * (width + 2 * units),
        rows * (width * 16 + units * 4) + 2 * width * (width + 2 * units),
        after=after,
        name="encoder_feed_forward_back",
        scratch=[pltpu.VMEM((rows, width), jnp.float32)],
    )(info, grad, mid, slope, gains, shifts, w_out, w_up, w_down)


def packed_back(grad_ref, w_ref):
    width = w_ref.shape[0]
    return sum(dot(grad_ref[j], w_ref[:, j * width : (j + 1) * width], NT) for j in range(3))


def decoder_back_kernel(
    info_ref,
    dpacked_ref,
    gm_ref,
    x_ref,
    source_ref,
    y_ref,
    encoded_ref,
    gain_ref,
    shift_ref,
    w_ref,
    w_proj_ref,
    enc_gain_ref,
    enc_shift_ref,
    grad_ref,
    sums_ref,
    enc_sums_ref,
    kept_ref,
    sent_ref,
    total_ref,
):
    dnormed = packed_back(dpacked_ref, w_ref)
    gain = row_of(gain_ref, 0)
    _, unit, inverse = norm(x_ref[...], gain, row_of(shift_ref, 0))
    dx = gm_ref[...].astype(jnp.float32) + norm_back(dnormed, unit, inverse, gain)
    picker = picker_of(source_ref, info_ref[STRIP + pl.program_id(0)])
    taken = dot(picker, low(dx), NN)
    last = taken.shape[0] - 1
    dproj = low(jnp.where(last_row(taken.shape[0]), 0.0, taken))
    term = dot(encoded_ref[...], dproj, TN)
    half = kept_ref.shape[0]

    @pl.when(pl.program_id(0) == 0)
    def begin():
        total_ref[...] = term

    @pl.when(pl.program_id(0) > 0)
    def more():
        total_ref[...] += term

    @pl.when(pl.program_id(0) == pl.num_programs(0) - 1)
    def finish():
        kept_ref[...] = low(total_ref[pl.ds(pl.multiple_of(info_ref[0] * half, 8), half), :])
        sent_ref[...] = low(total_ref[pl.ds(pl.multiple_of((1 - info_ref[0]) * half, 8), half), :])

    dencoded = low(dot(dproj, w_proj_ref[...], NT)).astype(jnp.float32)
    enc_gain = row_of(enc_gain_ref, 2)
    _, unit_final, inverse_final = norm(
        y_ref[...].astype(jnp.float32), enc_gain, row_of(enc_shift_ref, 2)
    )
    grad_ref[...] = low(norm_back(dencoded, unit_final, inverse_final, enc_gain))
    add_rows(
        sums_ref,
        (
            col_sum(dnormed * unit),
            col_sum(dnormed),
            taken[last : last + 1],
            col_sum(dproj.astype(jnp.float32)),
        ),
    )
    add_rows(enc_sums_ref, (col_sum(dencoded * unit_final), col_sum(dencoded)))


def decoder_back_call(
    sizes,
    info,
    dpacked,
    gm,
    x,
    source,
    y,
    encoded,
    gains,
    shifts,
    w_qkv,
    w_proj,
    enc_gains,
    enc_shifts,
    after,
):
    strips, padded, rows = sizes.strips, sizes.padded, sizes.rows
    width = x.shape[2]
    wide = y.shape[2]
    weights = (gains, shifts, w_qkv, w_proj, enc_gains, enc_shifts)
    strip = sizes.strip
    return call(
        decoder_back_kernel,
        (
            sds((strips, padded, wide)),
            sds((8, width), jnp.float32),
            sds((8, wide), jnp.float32),
            sds((wide // 2, width)),
            sds((wide // 2, width)),
        ),
        (strips, 1),
        [
            pl.BlockSpec((3, None, padded, width), lambda s, i, info: (0, s, 0, 0)),
            strip(width),
            strip(width),
            whole(source),
            strip(wide),
            strip(wide),
        ]
        + [whole(w) for w in weights],
        (
            strip(wide),
            sizes.sums(width),
            sizes.sums(wide),
            pl.BlockSpec((wide // 2, width), lambda s, i, info: (0, 0)),
            pl.BlockSpec((wide // 2, width), lambda s, i, info: (0, 0)),
        ),
        2 * rows * width * (3 * width + padded + 2 * wide),
        rows * (width * 16 + wide * 8) + 2 * width * (3 * width + wide),
        after=after,
        name="decoder_packed_back",
        scratch=[pltpu.VMEM((wide, width), jnp.float32)],
    )(info, dpacked, gm, x, source, y, encoded, *weights)


def encoder_back_kernel(info_ref, *refs, parts):
    grad_refs, w_refs = refs[:parts], refs[parts : 2 * parts]
    gb_ref, x_ref, gain_ref, shift_ref, kept_ref, sent_ref, *rest = refs[2 * parts :]
    dnormed_ref, pad_ref = rest[-2:]
    term = sum(dot(grad_ref[...], w_ref[...], NT) for grad_ref, w_ref in zip(grad_refs, w_refs))

    @first_step
    def begin():
        dnormed_ref[...] = term

    @pl.when(pl.program_id(0) > 0)
    def more():
        dnormed_ref[...] += term

    @last_step
    def finish():
        dnormed = dnormed_ref[...]
        gain = row_of(gain_ref, 0)
        _, unit, inverse = norm(padded_rows(x_ref, pad_ref), gain, row_of(shift_ref, 0))
        dx = gb_ref[...].astype(jnp.float32) + norm_back(dnormed, unit, inverse, gain)
        store_halves(info_ref, kept_ref, sent_ref, dx)
        set_rows(rest[0], (col_sum(dnormed * unit), col_sum(dnormed)))


def encoder_back_call(sizes, info, dpacked, gb, x, gains, shifts, w_qkv, strip, after):
    rows, width = gb.shape
    padded = sizes.padded
    half = sds((1, sizes.length, width // 2))
    parts = len(dpacked)
    here = width // parts
    half_spec = pl.BlockSpec((None, sizes.length, width // 2), lambda j, info: (0, 0, 0))
    return call(
        functools.partial(encoder_back_kernel, parts=parts),
        (half, half, sds((8, width), jnp.float32)),
        (3,),
        [pl.BlockSpec((None, None, padded, here), lambda j, info: (j, strip, 0, 0))] * parts
        + [
            pl.BlockSpec((width, here), lambda j, info, part=part: (0, j * parts + part))
            for part in range(parts)
        ]
        + [
            pl.BlockSpec((padded, width), lambda j, info: (strip, 0)),
            sizes.raw(width)[strip],
            whole(gains),
            whole(shifts),
        ],
        (half_spec, half_spec, sizes.sums(width)),
        6 * rows * width * width // sizes.strips,
        rows * width * 12 // sizes.strips + 6 * width * width,
        after=after,
        name=f"encoder_packed_back_{strip}",
        scratch=[pltpu.VMEM((padded, width), jnp.float32)] * 2,
    )(info, *dpacked, *[w_qkv] * parts, gb, x, gains, shifts)


class Job:
    def __init__(self, left, right, row_step, col_step, offset):
        self.half = left.shape[1] // 2
        self.width = right.shape[1]
        self.rows = left.shape[0]
        self.row_step, self.col_step, self.offset = row_step, col_step, offset
        self.down = self.half // row_step
        self.across = self.width // col_step
        self.count = self.down * self.across

    def at(self, step):
        here = jnp.clip(step - self.offset, 0, self.count - 1)
        if self.across == 1:
            return here, 0
        if self.down == 1:
            return 0, here
        return here // self.across, here % self.across

    def left(self, pick):
        return pl.BlockSpec(
            (self.rows, self.row_step),
            lambda step, info: (0, pick(info[0]) * self.down + self.at(step)[0]),
        )

    def right(self):
        return pl.BlockSpec((self.rows, self.col_step), lambda step, info: (0, self.at(step)[1]))

    def out(self):
        return pl.BlockSpec((self.row_step, self.col_step), lambda step, info: self.at(step))


def product_kernel(info_ref, *refs, jobs):
    step = pl.program_id(0)
    out = 3 * len(jobs)
    for place, (offset, count) in enumerate(jobs):
        mine_ref, other_ref, right_ref = refs[3 * place : 3 * place + 3]
        kept_ref, sent_ref = refs[out + 2 * place : out + 2 * place + 2]

        @pl.when((step >= offset) & (step < offset + count))
        def product():
            right = right_ref[...]
            sent_ref[...] = low(dot(other_ref[...], right, TN))
            kept_ref[...] = low(dot(mine_ref[...], right, TN))


def product_call(info, products, name, after=()):
    jobs, operands, in_specs, out_specs, out_shape = [], [], [], [], []
    offset = flops = moved = 0
    for left, right, row_step, col_step in products:
        job = Job(left, right, row_step, col_step, offset)
        offset += job.count
        jobs.append(job)
        operands += [left, left, right]
        in_specs += [job.left(lambda own: own), job.left(lambda own: 1 - own), job.right()]
        out_specs += [job.out(), job.out()]
        out_shape += [sds((job.half, job.width))] * 2
        flops += 4 * job.rows * job.half * job.width
        moved += 2 * job.rows * (2 * job.half + job.width) + 4 * job.half * job.width
    outs = call(
        functools.partial(product_kernel, jobs=[(job.offset, job.count) for job in jobs]),
        tuple(out_shape),
        (offset,),
        in_specs,
        tuple(out_specs),
        flops,
        moved,
        after=after,
        name=name,
    )(info, *operands)
    return [outs[2 * place : 2 * place + 2] for place in range(len(jobs))]


class Chain:
    def __init__(self, pairs, order, parts):
        self.pairs = pairs
        self.bits = list(range(pairs.bit_length() - 1))
        self.order = [bit for bit in order if bit < len(self.bits)]
        self.order += [bit for bit in self.bits if bit not in self.order]
        self.parts, self.widths = [], []
        for kept, arrived in parts:
            width = kept.shape[1]
            self.widths.append(width)
            self.parts.append(tuple(array.reshape(pairs, -1, width) for array in (kept, arrived)))
        self.done = None

    def item(self):
        kept = self.parts[0][0]
        if not self.order:
            return ("last", self.parts, self.widths, None)
        bit = self.order[0]
        lower = sum(1 for other in self.bits if other < bit)
        return ("halve", self.parts, (kept.shape[0] >> (lower + 1), 1 << lower), bit)

    def take(self, outs):
        if not self.order:
            self.done = outs
            return []
        bit = self.order.pop(0)
        self.bits.remove(bit)
        kept, sent = outs
        route = [(place, place ^ (1 << bit)) for place in range(self.pairs)]
        self.parts = [(kept, lax.ppermute(sent, "dp", route))]
        return [sent]


class Total:
    def __init__(self, pairs, values):
        self.pairs = pairs
        bits = [1 << bit for bit in range((2 * pairs).bit_length() - 1)]
        self.left = [bits[-1:]] + [bits[place : place + 2] for place in range(0, len(bits) - 1, 2)]
        self.done = None
        self.launch(values)

    def launch(self, values):
        group = self.left.pop(0)
        masks = group + [sum(group)] if len(group) > 1 else group
        count = 2 * self.pairs
        arrived = [
            lax.ppermute(values, ("section", "dp"), [(place, place ^ mask) for place in range(count)])
            for mask in masks
        ]
        self.parts = [(values, *arrived)]
        self.sent = values

    def item(self):
        return ("add", self.parts, None, None)

    def take(self, outs):
        (values,) = outs
        if not self.left:
            self.done = values
            return []
        self.launch(values)
        return [values]


def in_thirds(kind, parts):
    return kind == "halve" and len(parts) == 1 and parts[0][0].shape[-1] % (3 * GROUP) == 0


def round_kernel(info_ref, *refs, items):
    place = 0
    out = sum(sum(widths) for _, widths, _, _, _, _ in items)
    for kind, widths, how, bit, count, split in items:
        pairs = []
        for width in widths:
            pairs.append(refs[place : place + width])
            place += width
        outs = refs[out : out + count]
        out += count
        run = functools.partial(round_item, info_ref, kind, pairs, how, bit, outs)
        if split:
            run()
        else:
            first_step(run)


def round_item(info_ref, kind, pairs, how, bit, outs):
    if kind == "add":
        outs[0][...] = sum(ref[...] for ref in pairs[0])
        return

    def total(pair, index):
        return pair[0][index].astype(jnp.float32) + pair[1][index].astype(jnp.float32)

    if kind == "last":
        start = 0
        values = [total(pair, 0) for pair in pairs]
        whole_row = values[0] if len(values) == 1 else jnp.concatenate(values, axis=1)
        for ref, width in zip(outs, how):
            ref[...] = whole_row[:, start : start + width]
            start += width
        return
    high, lower = how
    mine = (info_ref[BLOCK] >> bit) & 1
    for h in range(high):
        for l in range(lower):
            start = 0
            for pair in pairs:
                width = pair[0].shape[-1]
                for ref, chosen in zip(outs, (mine, 1 - mine)):
                    index = (h * 2 + chosen) * lower + l
                    ref[h * lower + l, :, start : start + width] = pair[0][index] + pair[1][index]
                start += width


def round_call(info, chains, name, after=(), through=()):
    items = [chain.item() for chain in chains]
    operands, specs, out_shape, out_specs, plain, counts, moved = [], [], [], [], [], [], 0
    for kind, parts, how, bit in items:
        split = in_thirds(kind, parts)
        for part in parts:
            operands += part
            moved += len(part) * part[0].size * part[0].dtype.itemsize
            if split:
                block = (*part[0].shape[:-1], part[0].shape[-1] // 3)
                specs += [pl.BlockSpec(block, lambda i, info: (0, 0, i))] * len(part)
            else:
                specs += [whole(array) for array in part]
        shape = parts[0][0].shape
        if kind == "add":
            shapes = [sds(shape, jnp.float32)]
        elif kind == "last":
            shapes = [sds((shape[1], width), jnp.float32) for width in how]
        else:
            width = sum(part[0].shape[-1] for part in parts)
            shapes = [sds((shape[0] // 2, shape[1], width))] * 2
        out_shape += shapes
        if split:
            out_specs += [
                pl.BlockSpec((*shape.shape[:-1], shape.shape[-1] // 3), lambda i, info: (0, 0, i))
                for shape in shapes
            ]
        else:
            out_specs += [whole(shape) for shape in shapes]
        counts.append(len(shapes))
        plain.append((kind, [len(part) for part in parts], how, bit, len(shapes), split))
    outs = call(
        functools.partial(round_kernel, items=plain),
        tuple(out_shape),
        (3 if any(item[-1] for item in plain) else 1,),
        specs,
        tuple(out_specs),
        moved,
        2 * moved,
        after=after,
        through=through,
        name=name,
    )(info, *operands)
    sent, start = [], 0
    for chain, count in zip(chains, counts):
        sent += chain.take(outs[start : start + count])
        start += count
    return sent, outs[start:]


def across(values):
    return lax.ppermute(values, "section", [(0, 1), (1, 0)])


def arrange_kernel(info_ref, *refs, strips):
    *sources, out_ref = refs
    length = out_ref.shape[1]
    holder = info_ref[STRIP + 2 * strips + pl.program_id(0)]
    slot = info_ref[STRIP + 4 * strips + pl.program_id(0)]
    values = None
    for place in range(strips):
        if len(sources) == 2:
            padded = sources[0].shape[0] // strips
            rows = slice(place * padded, (place + 1) * padded)
            kept, arrived = (ref[rows, :] for ref in sources)
        else:
            kept, arrived = sources[place][0], sources[strips + place][0]
        chosen = jnp.where(holder == info_ref[0], kept, arrived)
        values = chosen if values is None else jnp.where(slot == place, chosen, values)
    out_ref[0] = values[:length]


def arrange_call(info, kept, arrived, strips, length, name, after=()):
    half = kept[0].shape[-1]
    return call(
        functools.partial(arrange_kernel, strips=strips),
        sds((2 * strips, length, half)),
        (2 * strips,),
        [whole(array) for array in (*kept, *arrived)],
        pl.BlockSpec((1, length, half), lambda k, info: (k, 0, 0)),
        1,
        strips * length * half * 12,
        name=name,
        after=after,
    )(info, *kept, *arrived)


def gather_small_kernel(
    info_ref, up_enc, up_dec, enc, dec, dec_in, final, *rest
):
    *enc_in, out_ref = rest
    out_ref[...] = jnp.zeros_like(out_ref)
    wide, narrow = enc.shape[1], dec.shape[1]
    out_ref[0:1, : up_enc.shape[1]] = up_enc[0:1, :]
    out_ref[1:2, : up_dec.shape[1]] = up_dec[0:1, :]
    out_ref[2:6, :wide] = enc[0:4, :]
    out_ref[2:6, wide : wide + narrow] = dec[0:4, :]
    out_ref[2:6, wide + narrow : wide + 2 * narrow] = dec_in[0:4, :]
    out_ref[6:8, :wide] = final[0:2, :]
    out_ref[6:8, wide : 2 * wide] = sum(ref[0:2, :] for ref in enc_in)


def gather_small_call(info, values):
    shape = (8, values[0].shape[1])
    return call(
        gather_small_kernel,
        sds(shape, jnp.float32),
        (1,),
        [whole(value) for value in values],
        pl.BlockSpec(shape, lambda i, info: (0, 0)),
        shape[1],
        shape[1] * 64,
        name="small_rows",
    )(info, *values)


def unshuffled(parts):
    return jnp.concatenate(
        [
            part[:, (3 * group + j) * GROUP : (3 * group + j + 1) * GROUP]
            for j in range(3)
            for part in parts
            for group in range(part.shape[1] // (3 * GROUP))
        ],
        axis=1,
    )


def shares_kernel(info_ref, rows_ref, dec_qkv_ref, *refs, parts, wide, narrow, units, dec_units, count):
    block = info_ref[BLOCK]

    def share(first, last, start, width):
        values = rows_ref[first:last, start : start + width]
        part = width // count
        return pltpu.roll(values, width - block * part, 1)[:, :part]

    enc_qkv = [ref[...] for ref in refs[:parts]]
    outs = refs[parts:]
    bias_up_enc = share(0, 1, 0, units)
    bias_up_dec = share(1, 2, 0, dec_units)
    enc = share(2, 6, 0, wide)
    dec = share(2, 6, wide, narrow)
    dec_in = share(2, 6, wide + narrow, narrow)
    final = share(6, 8, 0, wide)
    enc_in = share(6, 8, wide, wide)
    for ref, value in zip(
        outs,
        (
            jnp.concatenate([enc_in[0:1], enc[0:1], final[0:1]], axis=0),
            jnp.concatenate([enc_in[1:2], enc[1:2], final[1:2]], axis=0),
            enc[2:4],
            bias_up_enc,
            dec_in[3:4],
            dec_in[2:3],
            jnp.concatenate([dec_in[0:1], dec[0:1]], axis=0),
            jnp.concatenate([dec_in[1:2], dec[1:2]], axis=0),
            dec[2:4],
            bias_up_dec,
            unshuffled([dec_qkv_ref[...]]),
            unshuffled(enc_qkv),
        ),
    ):
        ref[...] = value


def shares_call(info, rows, dec_qkv, enc_qkv, wide, narrow, units, dec_units, count):
    shapes = [
        (height, width // count)
        for height, width in (
            (3, wide),
            (3, wide),
            (2, wide),
            (1, units),
            (1, narrow),
            (1, narrow),
            (2, narrow),
            (2, narrow),
            (2, narrow),
            (1, dec_units),
        )
    ] + [dec_qkv.shape, (wide // count, 3 * wide)]
    return call(
        functools.partial(
            shares_kernel,
            parts=len(enc_qkv),
            wide=wide,
            narrow=narrow,
            units=units,
            dec_units=dec_units,
            count=count,
        ),
        tuple(sds(shape, jnp.float32) for shape in shapes),
        (1,),
        [whole(array) for array in (rows, dec_qkv, *enc_qkv)],
        tuple(pl.BlockSpec(shape, lambda i, info: (0, 0)) for shape in shapes),
        rows.size,
        rows.size * 4,
        name="shares",
    )(info, rows, dec_qkv, *enc_qkv)


def decoder_shares_kernel(info_ref, rows_ref, up_ref, out_ref, down_ref):
    width = out_ref.shape[1]
    units = up_ref.shape[1]
    share = up_ref.shape[0]
    rows = rows_ref[...]
    up_ref[...] = rows[:, :units]
    out_ref[...] = rows[:, units : units + width]
    for fold in range(units // width):
        start = units + (fold + 1) * width
        down_ref[fold * share : (fold + 1) * share, :] = rows[:, start : start + width]


def decoder_shares_call(info, rows, width, units, after):
    share = rows.shape[0]
    shapes = ((share, units), (share, width), (share * units // width, width))
    return call(
        decoder_shares_kernel,
        tuple(sds(shape, jnp.float32) for shape in shapes),
        (1,),
        [whole(rows)],
        tuple(pl.BlockSpec(shape, lambda i, info: (0, 0)) for shape in shapes),
        rows.size,
        rows.size * 6,
        name="decoder_shares",
        after=after,
    )(info, rows)


def place_table(length_rows, model_width):
    halfway = model_width // 2
    places = np.arange(length_rows, dtype=np.float64)[:, None]
    rates = np.exp(np.arange(halfway, dtype=np.float64) * (-math.log(10000.0) / halfway))[None, :]
    return np.concatenate([np.sin(places * rates), np.cos(places * rates)], axis=1).astype(
        np.float32
    )


def local(
    patches,
    visible,
    source,
    enc_gains,
    enc_shifts,
    enc_qkv,
    enc_out,
    enc_bias_out,
    enc_up,
    enc_bias_up,
    enc_down,
    enc_proj,
    proj_bias,
    mask_token,
    dec_gains,
    dec_shifts,
    dec_qkv,
    dec_out,
    dec_bias_out,
    dec_up,
    dec_bias_up,
    dec_down,
    cotangent,
):
    pairs = lax.axis_size("dp")
    count = 2 * pairs
    length = patches.shape[1]
    wide = patches.shape[2]
    narrow = dec_qkv.shape[0]
    strips = patches.shape[0] // 2
    padded = -(-(length + 1) // ROW_STEP) * ROW_STEP
    sizes = Sizes(strips, length, padded)
    rows = sizes.rows
    info = place_info(visible, strips)
    taken = jnp.pad(
        jnp.where(source < 0, padded - 1, source),
        ((0, 0), (0, padded - length)),
        constant_values=padded - 1,
    )
    places = jnp.asarray(place_table(padded, narrow))
    strip_form = lambda array: array.reshape(strips, padded, array.shape[-1])
    row_form = lambda array: array.reshape(rows, array.shape[-1])

    n1_enc, packed_enc = packed_call(sizes, info, patches, enc_gains, enc_shifts, enc_qkv)
    packed_enc = strip_form(packed_enc)
    enc_live = visible_live(strips)
    mixed_enc, scales_enc = attend_call(
        packed_enc, info, HEADS_ENC, enc_live, "encoder_attention"
    )
    mixed_enc = row_form(mixed_enc)
    mid_enc, n2_enc, act_enc, slope_enc, y_enc, encoded, projected = encoder_ff_call(
        sizes,
        info,
        patches,
        mixed_enc,
        enc_gains,
        enc_shifts,
        enc_out,
        enc_bias_out,
        enc_up,
        enc_bias_up,
        enc_down,
        enc_proj,
        proj_bias,
    )
    x_dec, n1_dec, packed_dec = decoder_in_call(
        sizes, info, projected, taken, mask_token, places, dec_gains, dec_shifts, dec_qkv
    )
    x_dec, n1_dec, packed_dec = map(strip_form, (x_dec, n1_dec, packed_dec))
    dec_live = all_live(length)
    mixed_dec, scales_dec = attend_call(
        packed_dec, info, HEADS_DEC, dec_live, "decoder_attention"
    )
    mixed_dec = row_form(mixed_dec)
    share = narrow // count
    (
        kept_dec,
        sent_dec,
        gb_dec,
        dmixed_dec,
        sums_dec,
        up_sums_dec,
        kept_beside,
        sent_beside,
        *apart,
    ) = decoder_ff_call(
        sizes,
        info,
        row_form(x_dec),
        mixed_dec,
        cotangent,
        dec_gains,
        dec_shifts,
        dec_out,
        dec_bias_out,
        dec_up,
        dec_bias_up,
        dec_down,
        share,
    )
    arrived_beside, arrived_dec = map(across, (sent_beside, sent_dec))
    enc_half = wide // 2
    dpacked_dec, kept_dqkv, sent_dqkv = attend_back_call(
        packed_dec,
        strip_form(dmixed_dec),
        strip_form(mixed_dec),
        scales_dec,
        n1_dec,
        info,
        HEADS_DEC,
        dec_live,
        0,
        1,
        (sent_beside, sent_dec),
        "decoder_attention_back",
    )
    arrived_dqkv = across(sent_dqkv)
    grad_enc, sums_dec_in, sums_final, kept_proj, sent_proj = decoder_back_call(
        sizes,
        info,
        dpacked_dec,
        strip_form(gb_dec),
        x_dec,
        taken,
        strip_form(y_enc),
        strip_form(encoded),
        dec_gains,
        dec_shifts,
        dec_qkv,
        enc_proj,
        enc_gains,
        enc_shifts,
        (sent_dqkv, arrived_dec),
    )
    grad_enc = row_form(grad_enc)
    arrived_proj = across(sent_proj)
    ((kept_edown, sent_edown),) = product_call(
        info, [(act_enc, grad_enc, enc_half, wide)], "grad_enc_down", (sent_proj,)
    )
    grads_dec = Chain(
        pairs, (0, 1, 2, 3), ((kept_beside, arrived_beside), (kept_dqkv, arrived_dqkv))
    )
    sent, (sent_edown,) = round_call(
        info, [grads_dec], "round_1", (kept_edown, arrived_proj), (sent_edown,)
    )
    arrived_edown = across(sent_edown)
    dhid_enc, gb_enc, dmixed_enc, sums_enc, up_sums_enc = encoder_ff_back_call(
        sizes,
        info,
        grad_enc,
        mid_enc,
        slope_enc,
        enc_gains,
        enc_shifts,
        enc_out,
        enc_up,
        enc_down,
        (*sent, sent_edown),
    )
    (kept_eup, sent_eup), (kept_eout, sent_eout) = product_call(
        info,
        [(n2_enc, dhid_enc, enc_half, wide), (mixed_enc, gb_enc, enc_half, wide)],
        "grad_enc_up_out",
        sent,
    )
    down_enc = Chain(pairs, (0, 2, 1, 3), ((kept_edown, arrived_edown),))
    sent, (sent_eup, sent_eout) = round_call(
        info, [down_enc, grads_dec], "round_2", (kept_eout,), (sent_eup, sent_eout)
    )
    arrived_eup, arrived_eout = map(across, (sent_eup, sent_eout))
    up_enc = Chain(pairs, (1, 0, 2, 3), ((kept_eup, arrived_eup),))
    out_enc = Chain(pairs, (0, 1, 2, 3), ((kept_eout, arrived_eout), (kept_proj, arrived_proj)))
    every = [up_enc, down_enc, grads_dec, out_enc]
    active = lambda: [chain for chain in every if chain.done is None]
    after = (*sent, sent_eup, sent_eout)
    number, dpacked_enc, qkv_enc = 3, [], []
    by_y, by_z = (1, 0, 2, 3), (2, 0, 1, 3)
    for part in range(PARTS):
        dpacked, kept, sent_here = attend_back_call(
            packed_enc,
            strip_form(dmixed_enc),
            strip_form(mixed_enc),
            scales_enc,
            strip_form(n1_enc),
            info,
            HEADS_ENC,
            enc_live,
            part,
            PARTS,
            after,
            f"encoder_attention_back_{part}",
        )
        dpacked_enc.append(dpacked)
        before = (dpacked,)
        if part == 0:
            arranged = arrange_call(
                info, [kept_dec], [arrived_dec], strips, length, "decoded_strips", before
            )
            turned = lax.optimization_barrier(jnp.swapaxes(arranged, 0, 1))
            decoded = jnp.swapaxes(turned, 0, 1)
            before = (dpacked, turned)
        sent, (sent_here,) = round_call(info, active(), f"round_{number}", before, (sent_here,))
        chain = Chain(pairs, (by_z, by_y)[part % 2], ((kept, across(sent_here)),))
        number += 1
        qkv_enc.append(chain)
        every.append(chain)
        after = (*sent, sent_here)
    kept_enc, sent_enc, sums_enc_in = [], [], []
    for strip in range(strips):
        kept, sent_here, sums = encoder_back_call(
            sizes, info, dpacked_enc, gb_enc, patches, enc_gains, enc_shifts, enc_qkv, strip, after
        )
        kept_enc.append(kept)
        sums_enc_in.append(sums)
        sent_enc.append(sent_here)
        through = ()
        if strip == strips - 1:
            through = tuple(sent_enc)
            if apart:
                down_dec = Chain(pairs, by_y, ((apart[0], across(apart[1])),))
                every.append(down_dec)
            small = gather_small_call(
                info,
                (
                    up_sums_enc,
                    up_sums_dec,
                    sums_enc,
                    sums_dec,
                    sums_dec_in,
                    sums_final,
                    *sums_enc_in,
                ),
            )
            through += (small,)
        sent, through = round_call(info, active(), f"round_{number}", (sums,), through)
        number += 1
        after = (*sent,)
    *sent_enc, small = through
    arrived_enc = [across(array) for array in sent_enc]
    small = Total(pairs, small)
    every.append(small)
    patch_grad = arrange_call(info, kept_enc, arrived_enc, strips, length, "patch_grad_strips", after)
    after = (patch_grad,)
    if not apart:
        dec_shares = decoder_shares_call(info, grads_dec.done[0], narrow, dec_up.shape[1], after)
        after += (dec_shares[1],)
    while active():
        round_call(info, active(), f"round_{number}", after)
        after = ()
        number += 1
    g_beside, g_dqkv = grads_dec.done
    shares = shares_call(
        info,
        small.done,
        g_dqkv,
        [chain.done[0] for chain in qkv_enc],
        wide,
        narrow,
        enc_up.shape[1],
        dec_up.shape[1],
        count,
    )
    if apart:
        g_dup, g_dout = g_beside[:, : dec_up.shape[1]], g_beside[:, dec_up.shape[1] :]
        (g_ddown,) = down_dec.done
    else:
        g_dup, g_dout, g_ddown = dec_shares
    (g_edown,), (g_eup,) = down_enc.done, up_enc.done
    g_eout, g_proj = out_enc.done
    return (
        decoded,
        patch_grad,
        shares[0],
        shares[1],
        shares[11],
        g_eout,
        shares[2],
        g_eup,
        shares[3].reshape(-1),
        g_edown,
        g_proj,
        shares[4].reshape(-1),
        shares[5].reshape(-1),
        shares[6],
        shares[7],
        shares[10],
        g_dout,
        shares[8],
        g_dup,
        shares[9].reshape(-1),
        g_ddown,
    )


def solution(mesh):
    return jax.shard_map(
        local,
        mesh=mesh,
        in_specs=(
            P("dp", None, None),
            P("dp"),
            P("dp", None),
            P(),
            P(),
            P(),
            P(),
            P(),
            P(),
            P(),
            P(),
            P(),
            P(),
            P(),
            P(),
            P(),
            P(),
            P(),
            P(),
            P(),
            P(),
            P(),
            P("dp", None, None),
        ),
        out_specs=(
            P("dp", None, "section"),
            P("dp", None, "section"),
            P(None, ("section", "dp")),
            P(None, ("section", "dp")),
            P(("section", "dp"), None),
            P(("section", "dp"), None),
            P(None, ("section", "dp")),
            P(("section", "dp"), None),
            P(("section", "dp")),
            P(("section", "dp"), None),
            P(("section", "dp"), None),
            P(("section", "dp")),
            P(("section", "dp")),
            P(None, ("section", "dp")),
            P(None, ("section", "dp")),
            P(("section", "dp"), None),
            P(("section", "dp"), None),
            P(None, ("section", "dp")),
            P(("section", "dp"), None),
            P(("section", "dp")),
            P(("section", "dp"), None),
        ),
        check_vma=False,
    )
```

```python
import functools
import math

import jax
import jax.numpy as jnp
import numpy as np
from jax import lax
from jax.experimental import pallas as pl
from jax.experimental.pallas import tpu as pltpu
from jax.sharding import PartitionSpec as P

HEADS_ENC = 12
HEADS_DEC = 16
ROW_STEP = 32
GROUP = 128
PARTS = 2
VMEM_BYTES = 63 * 1024 * 1024
MASKED = -1e30
LOG2E = math.log2(math.e)

epsilon = 1e-06

NN = (((1,), (0,)), ((), ()))
NT = (((1,), (1,)), ((), ()))
TN = (((0,), (0,)), ((), ()))


def dot(left_side, right_side, dims):
    return lax.dot_general(left_side, right_side, dims, preferred_element_type=jnp.float32)


def low(values):
    return values.astype(jnp.bfloat16)


def call(
    kernel, out_shape, grid, in_specs, out_specs, flops, moved, scalars=1, exps=0, after=(), name=None, scratch=(), through=()
):
    count = scalars + len(in_specs)
    ordered = [pl.BlockSpec(memory_space=pl.ANY)] * (len(after) + len(through))
    aliases = {}
    if through:
        outs = len(out_shape)
        aliases = {count + len(after) + place: outs + place for place in range(len(through))}
        out_shape = tuple(out_shape) + tuple(sds(array.shape, array.dtype) for array in through)
        out_specs = tuple(out_specs) + (pl.BlockSpec(memory_space=pl.ANY),) * len(through)

    def body(*refs):
        ins, rest = refs[:count], refs[count + len(after) + len(through) :]
        if through:
            rest = rest[:outs] + rest[outs + len(through) :]
        kernel(*ins, *rest)

    made = pl.pallas_call(
        body,
        out_shape=out_shape,
        grid_spec=pltpu.PrefetchScalarGridSpec(
            num_scalar_prefetch=scalars,
            grid=grid,
            in_specs=list(in_specs) + ordered,
            out_specs=out_specs,
            scratch_shapes=list(scratch),
        ),
        input_output_aliases=aliases,
        compiler_params=pltpu.CompilerParams(vmem_limit_bytes=VMEM_BYTES),
        cost_estimate=pl.CostEstimate(flops=flops, bytes_accessed=moved, transcendentals=exps),
        name=name,
    )
    return lambda *operands: made(*operands, *after, *through)


def whole(array):
    rank = array.ndim
    return pl.BlockSpec(array.shape, lambda *unused: (0,) * rank)


def row_of(ref, place):
    return ref[place : place + 1, :].astype(jnp.float32)


def vector_of(ref):
    return ref[...].astype(jnp.float32).reshape(1, -1)


def padded_rows(ref, pad_ref):
    length, padded = ref.shape[0], pad_ref.shape[0]
    first = length // 8 * 8
    pad_ref[first:, :] = jnp.zeros((padded - first, pad_ref.shape[1]), jnp.float32)
    pad_ref[:length, :] = ref[...].astype(jnp.float32)
    return pad_ref[...]


def sds(shape, kind=jnp.bfloat16):
    return jax.ShapeDtypeStruct(shape, kind)


def norm(values, gain_row, shift_row):
    center = values - jnp.mean(values, axis=-1, keepdims=True)
    inverse = lax.rsqrt(jnp.mean(center * center, axis=-1, keepdims=True) + epsilon)
    unit = center * inverse
    return unit * gain_row + shift_row, unit, inverse


def norm_back(grad_out, unit, inverse, gain_row):
    scaled = grad_out * gain_row
    return inverse * (
        scaled
        - jnp.mean(scaled, axis=-1, keepdims=True)
        - unit * jnp.mean(scaled * unit, axis=-1, keepdims=True)
    )


def col_sum(values):
    return jnp.sum(values, axis=0, keepdims=True)


def gelu_parts(values):
    share = 0.5 + 0.5 * lax.erf(values * math.sqrt(0.5))
    bell = jnp.exp2(values * values * (-0.5 * LOG2E)) * (1.0 / math.sqrt(2.0 * math.pi))
    return values * share, share + values * bell


def add_rows(ref, rows):
    @pl.when((pl.program_id(0) == 0) & (pl.program_id(1) == 0))
    def start():
        ref[...] = jnp.zeros_like(ref)

    for place, row in enumerate(rows):
        ref[place : place + 1, :] += row


BLOCK = 1
STRIP = 2


def place_info(visible, strips):
    section_index = lax.axis_index("section")
    block = section_index * lax.axis_size("dp") + lax.axis_index("dp")
    mine = section_index * strips + jnp.arange(strips, dtype=jnp.int32)
    every = jnp.arange(2 * strips, dtype=jnp.int32)
    return jnp.concatenate(
        [
            jnp.stack([section_index, block]),
            mine,
            lax.dynamic_slice_in_dim(visible, section_index * strips, strips, 0),
            every // strips,
            every % strips,
        ]
    ).astype(jnp.int32)


class Sizes:
    def __init__(self, strips, length, padded):
        self.strips, self.length, self.padded = strips, length, padded
        self.rows = strips * padded

    def place(self, strip):
        return slice(strip * self.padded, (strip + 1) * self.padded)

    def raw(self, width):
        return [
            pl.BlockSpec(
                (None, self.length, width), lambda *step, s=s: (step[-1][STRIP + s], 0, 0)
            )
            for s in range(self.strips)
        ]

    def all(self, width):
        return pl.BlockSpec((self.rows, width), lambda *step: (0, 0))

    def cols(self, width):
        return pl.BlockSpec((self.rows, width), lambda i, info: (0, i))

    def half(self, width):
        return pl.BlockSpec((self.strips, self.length, width), lambda *step: (0, 0, 0))

    def sums(self, width):
        return pl.BlockSpec((8, width), lambda *step: (0, 0))

    def strip(self, width):
        return pl.BlockSpec((None, self.padded, width), lambda s, i, info: (s, 0, 0))


def first_step(run):
    pl.when(pl.program_id(0) == 0)(run)


def last_step(run):
    pl.when(pl.program_id(0) == pl.num_programs(0) - 1)(run)


def store_halves(info_ref, kept_ref, sent_ref, values):
    length, half = kept_ref.shape
    first = info_ref[0] == 0
    values = values[:length]
    kept_ref[...] = low(jnp.where(first, values[:, :half], values[:, half:]))
    sent_ref[...] = low(jnp.where(first, values[:, half:], values[:, :half]))


def set_rows(ref, rows):
    for place, row in enumerate(rows):
        ref[place : place + 1, :] = row


def packed_kernel(info_ref, *refs, sizes):
    x_refs = refs[: sizes.strips]
    gain_ref, shift_ref, w_ref, n_ref, packed_ref, pad_ref = refs[sizes.strips :]

    @first_step
    def normalize():
        for strip, x_ref in enumerate(x_refs):
            x = padded_rows(x_ref, pad_ref)
            normed, _, _ = norm(x, row_of(gain_ref, 0), row_of(shift_ref, 0))
            n_ref[sizes.place(strip), :] = low(normed)

    packed_ref[...] = low(dot(n_ref[...], w_ref[...], NN))


def packed_call(sizes, info, x, gains, shifts, w_qkv):
    rows, width = sizes.rows, x.shape[2]
    return call(
        functools.partial(packed_kernel, sizes=sizes),
        (sds((rows, width)), sds((rows, 3 * width))),
        (3,),
        sizes.raw(width)
        + [whole(gains), whole(shifts), pl.BlockSpec((width, width), lambda i, info: (0, i))],
        (sizes.all(width), sizes.cols(width)),
        6 * rows * width * width,
        rows * width * 10 + 6 * width * width,
        name="encoder_packed",
        scratch=[pltpu.VMEM((sizes.padded, width), jnp.float32)],
    )(info, *[x] * sizes.strips, gains, shifts, w_qkv)


def picker_of(source_ref, strip):
    taken = source_ref[pl.ds(strip, 1), :]
    length = taken.shape[1]
    return low(jnp.where(taken == lax.broadcasted_iota(jnp.int32, (length, length), 0), 1.0, 0.0))


def last_row(length):
    return lax.broadcasted_iota(jnp.int32, (length, 1), 0) == length - 1


def decoder_in_kernel(
    info_ref,
    rows_ref,
    source_ref,
    mask_ref,
    places_ref,
    gain_ref,
    shift_ref,
    w_ref,
    x_ref,
    n_ref,
    packed_ref,
    *,
    sizes
):
    @first_step
    def gather():
        for strip in range(sizes.strips):
            place = sizes.place(strip)
            picker = picker_of(source_ref, info_ref[STRIP + strip])
            rows = jnp.where(
                last_row(sizes.padded), vector_of(mask_ref), rows_ref[place, :].astype(jnp.float32)
            )
            x = dot(picker, low(rows), TN) + places_ref[...]
            x_ref[place, :] = x
            normed, _, _ = norm(x, row_of(gain_ref, 0), row_of(shift_ref, 0))
            n_ref[place, :] = low(normed)

    packed_ref[...] = low(dot(n_ref[...], w_ref[...], NN))


def decoder_in_call(sizes, info, projected, source, mask_row, places, gains, shifts, w_qkv):
    width = projected.shape[1]
    rows = sizes.rows
    return call(
        functools.partial(decoder_in_kernel, sizes=sizes),
        (sds((rows, width), jnp.float32), sds((rows, width)), sds((rows, 3 * width))),
        (3,),
        [sizes.all(width), whole(source), whole(mask_row), whole(places), whole(gains), whole(shifts)]
        + [pl.BlockSpec((width, width), lambda i, info: (0, i))],
        (sizes.all(width), sizes.all(width), sizes.cols(width)),
        6 * rows * width * width + 2 * rows * sizes.padded * width,
        rows * width * 18 + 6 * width * width,
        name="decoder_packed",
    )(info, projected, source, mask_row, places, gains, shifts, w_qkv)


def head_parts(head, heads_here):
    lane = lax.broadcasted_iota(jnp.int32, (1, GROUP), 1)
    size = GROUP // heads_here
    mine = (lane >= head * size) & (lane < (head + 1) * size)
    spare = ((head + 1) % heads_here) * size
    return mine, lane == spare, spare


def key_bias(live, length):
    row = lax.broadcasted_iota(jnp.int32, (length, 1), 0)
    return low(jnp.where(row < live, 0.0, MASKED))


def attend_kernel(info_ref, q_ref, k_ref, v_ref, out_ref, scale_ref, *, heads_here, live):
    length = q_ref.shape[1]
    rate = (GROUP // heads_here) ** -0.5 * LOG2E
    bias = key_bias(live(info_ref, pl.program_id(0)), length)
    one = jnp.bfloat16(1.0)
    middle = length // 2
    for group in range(q_ref.shape[2] // GROUP):
        columns = slice(group * GROUP, (group + 1) * GROUP)
        k, v = k_ref[0, :, columns], v_ref[0, :, columns]
        for rows in (slice(0, middle), slice(middle, length)):
            q = q_ref[0, rows, columns]
            mixed = jnp.zeros(q.shape, jnp.float32)
            tops = jnp.zeros(q.shape, jnp.float32)
            totals = jnp.ones(q.shape, jnp.float32)
            for head in range(heads_here):
                mine, at_spare, spare = head_parts(head, heads_here)
                head_q = jnp.where(mine, q, low(jnp.where(at_spare, 1.0, 0.0)))
                scores = dot(head_q, jnp.where(at_spare, bias, k), NT)
                highest = jnp.max(scores, axis=1, keepdims=True)
                terms = low(jnp.exp2((scores - highest) * rate))
                product = dot(terms, jnp.where(at_spare, one, v), NN)
                mixed = jnp.where(mine, product * (1.0 / product[:, spare : spare + 1]), mixed)
                tops = jnp.where(at_spare, highest, tops)
                totals = jnp.where(at_spare, product, totals)
            out_ref[0, rows, columns] = low(mixed)
            scales = (tops * rate + jnp.log2(totals)).T
            for head in range(heads_here):
                spare = head_parts(head, heads_here)[2]
                scale_ref[0, group, head : head + 1, rows] = scales[spare : spare + 1]


def all_live(length):
    return lambda info_ref, strip: length


def visible_live(strips):
    return lambda info_ref, strip: info_ref[STRIP + strips + strip]


def attend_call(packed, info, heads, live, name):
    strips, length, triple = packed.shape
    width = triple // 3
    heads_here = GROUP // (width // heads)
    steps = 1 if heads_here == 2 else 2
    part = width // steps
    groups = part // GROUP
    third = lambda j: pl.BlockSpec((1, length, part), lambda s, g, _: (s, 0, g + j * steps))
    return call(
        functools.partial(attend_kernel, heads_here=heads_here, live=live),
        (sds((strips, length, width)), sds((strips, steps * groups, 8, length), jnp.float32)),
        (strips, steps),
        [third(0), third(1), third(2)],
        (third(0), pl.BlockSpec((1, groups, 8, length), lambda s, g, _: (s, g, 0, 0))),
        strips * heads * length * length * GROUP * 6,
        strips * length * width * 8,
        exps=strips * heads * length * length,
        name=name,
    )(info, packed, packed, packed)


def attend_back_kernel(
    info_ref,
    q_ref,
    k_ref,
    v_ref,
    dout_ref,
    mixed_ref,
    scale_ref,
    n_ref,
    grad_ref,
    kept_ref,
    sent_ref,
    total_ref,
    *,
    heads_here,
    live
):
    length = q_ref.shape[1]
    factor = (GROUP // heads_here) ** -0.5
    rate = factor * LOG2E
    strip = pl.program_id(1)
    q, k, v, dout = q_ref[0], k_ref[0], v_ref[0], dout_ref[0]
    bias = key_bias(live(info_ref, strip), length)
    k_turned = k.T
    agree = (dout.astype(jnp.float32) * mixed_ref[0].astype(jnp.float32)).T
    dq_turned = []
    dk = jnp.zeros((length, GROUP), jnp.float32)
    dv = jnp.zeros((length, GROUP), jnp.float32)
    size = GROUP // heads_here
    for head in range(heads_here):
        mine, at_spare, _ = head_parts(head, heads_here)
        head_q = jnp.where(mine, q, low(jnp.where(at_spare, 1.0, 0.0)))
        head_dout = jnp.where(mine, dout, jnp.bfloat16(0.0))
        scores = dot(jnp.where(at_spare, bias, k), head_q, NT)
        probs = jnp.exp2(scores * rate - scale_ref[0, 0, head : head + 1, :])
        average = jnp.sum(agree[head * size : (head + 1) * size], axis=0, keepdims=True)
        dscores = low(probs * (dot(v, head_dout, NT) - average))
        dk = jnp.where(mine, dot(dscores, q, NN), dk)
        dv = jnp.where(mine, dot(low(probs), dout, NN), dv)
        dq_turned.append(dot(k_turned[head * size : (head + 1) * size], dscores, NN))
    dq = low(jnp.concatenate(dq_turned, axis=0).T * factor)
    dk, dv = low(dk * factor), low(dv)
    grad_ref[0, 0] = dq
    grad_ref[1, 0] = dk
    grad_ref[2, 0] = dv
    term = dot(n_ref[0], jnp.concatenate([dq, dk, dv], axis=1), TN)
    half = kept_ref.shape[0]
    last = pl.num_programs(1) - 1

    @pl.when(strip == 0)
    def begin():
        total_ref[...] = term

    @pl.when(strip > 0)
    def more():
        total_ref[...] += term

    @pl.when(strip == last)
    def finish():
        kept_ref[...] = low(total_ref[pl.ds(pl.multiple_of(info_ref[0] * half, 8), half), :])
        sent_ref[...] = low(total_ref[pl.ds(pl.multiple_of((1 - info_ref[0]) * half, 8), half), :])


def attend_back_call(
    packed, dmixed, mixed, scales, normed, info, heads, live, part, parts, after, name
):
    strips, length, triple = packed.shape
    width = triple // 3
    heads_here = GROUP // (width // heads)
    groups = width // GROUP
    here = groups // parts
    third = lambda j: pl.BlockSpec(
        (1, length, GROUP), lambda g, s, _: (s, 0, g + part * here + j * groups)
    )
    product = pl.BlockSpec((width // 2, 3 * GROUP), lambda g, s, _: (0, g))
    return call(
        functools.partial(attend_back_kernel, heads_here=heads_here, live=live),
        (
            sds((3, strips, length, here * GROUP)),
            sds((width // 2, here * 3 * GROUP)),
            sds((width // 2, here * 3 * GROUP)),
        ),
        (here, strips),
        [
            third(0),
            third(1),
            third(2),
            third(0),
            third(0),
            pl.BlockSpec((1, 1, 8, length), lambda g, s, _: (s, g + part * here, 0, 0)),
            pl.BlockSpec((1, length, width), lambda g, s, _: (s, 0, 0)),
        ],
        (pl.BlockSpec((3, 1, length, GROUP), lambda g, s, _: (0, s, 0, g)), product, product),
        (strips * heads * length * length * GROUP * 12 + 6 * strips * length * width * width) // parts,
        strips * length * width * 14 // parts,
        exps=strips * heads * length * length // parts,
        after=after,
        name=name,
        scratch=[pltpu.VMEM((width, 3 * GROUP), jnp.float32)],
    )(info, packed, packed, packed, dmixed, mixed, scales, normed)


def encoder_ff_kernel(info_ref, *refs, sizes):
    x_refs = refs[: sizes.strips]
    (
        mixed_ref,
        gain_ref,
        shift_ref,
        w_out_ref,
        bias_out_ref,
        w_up_ref,
        bias_up_ref,
        w_down_ref,
        w_proj_ref,
        bias_proj_ref,
        mid_ref,
        n_ref,
        act_ref,
        slope_ref,
        y_low_ref,
        encoded_ref,
        projected_ref,
        y_ref,
        bias_ref,
        pad_ref,
    ) = refs[sizes.strips :]
    places = [sizes.place(strip) for strip in range(sizes.strips)]

    @first_step
    def middle():
        bias_ref[...] = vector_of(bias_up_ref)
        for place, x_ref in zip(places, x_refs):
            x = padded_rows(x_ref, pad_ref)
            mid = x + dot(mixed_ref[place, :], w_out_ref[...], NN) + row_of(bias_out_ref, 0)
            mid_ref[place, :] = low(mid)
            normed, _, _ = norm(mid, row_of(gain_ref, 1), row_of(shift_ref, 1))
            n_ref[place, :] = low(normed)
            y_ref[place, :] = mid + row_of(bias_out_ref, 1)

    chunk = w_up_ref.shape[1]
    bias = bias_ref[:, pl.ds(pl.multiple_of(pl.program_id(0) * chunk, GROUP), chunk)]
    hidden = [dot(n_ref[place, :], w_up_ref[...], NN) + bias for place in places]
    for place, values in zip(places, hidden):
        act, slope = gelu_parts(values)
        act = low(act)
        act_ref[place, :] = act
        slope_ref[place, :] = low(slope)
        y_ref[place, :] += dot(act, w_down_ref[...], NN)

    @last_step
    def finish():
        for place in places:
            y = y_ref[place, :]
            y_low_ref[place, :] = low(y)
            encoded, _, _ = norm(y, row_of(gain_ref, 2), row_of(shift_ref, 2))
            encoded = low(encoded)
            encoded_ref[place, :] = encoded
            projected_ref[place, :] = low(
                dot(encoded, w_proj_ref[...], NN) + vector_of(bias_proj_ref)
            )


def encoder_ff_call(
    sizes, info, x, mixed, gains, shifts, w_out, bias_out, w_up, bias_up, w_down, w_proj, bias_proj
):
    rows, width = sizes.rows, x.shape[2]
    units = w_up.shape[1]
    narrow = w_proj.shape[1]
    chunk = units // 4
    return call(
        functools.partial(encoder_ff_kernel, sizes=sizes),
        (
            sds((rows, width)),
            sds((rows, width)),
            sds((rows, units)),
            sds((rows, units)),
            sds((rows, width)),
            sds((rows, width)),
            sds((rows, narrow)),
        ),
        (4,),
        sizes.raw(width)
        + [sizes.all(width)]
        + [whole(w) for w in (gains, shifts, w_out, bias_out)]
        + [
            pl.BlockSpec((width, chunk), lambda i, info: (0, i)),
            whole(bias_up),
            pl.BlockSpec((chunk, width), lambda i, info: (i, 0)),
            whole(w_proj),
            whole(bias_proj),
        ],
        (
            sizes.all(width),
            sizes.all(width),
            sizes.cols(chunk),
            sizes.cols(chunk),
            sizes.all(width),
            sizes.all(width),
            sizes.all(narrow),
        ),
        2 * rows * width * (width + 2 * units + narrow),
        rows * (width * 16 + units * 4) + 2 * width * (width + 2 * units + narrow),
        exps=rows * units,
        name="encoder_feed_forward",
        scratch=[
            pltpu.VMEM((rows, width), jnp.float32),
            pltpu.VMEM((1, units), jnp.float32),
            pltpu.VMEM((sizes.padded, width), jnp.float32),
        ],
    )(
        info,
        *[x] * sizes.strips,
        mixed,
        gains,
        shifts,
        w_out,
        bias_out,
        w_up,
        bias_up,
        w_down,
        w_proj,
        bias_proj,
    )


def decoder_ff_kernel(info_ref, *refs, sizes, folds, share, units):
    cot_refs = refs[: sizes.strips]
    (
        x_ref,
        mixed_ref,
        gain_ref,
        shift_ref,
        w_out_ref,
        bias_out_ref,
        w_up_ref,
        bias_up_ref,
        w_down_ref,
        kept_ref,
        sent_ref,
        gb_ref,
        dmixed_ref,
        sums_ref,
        up_sums_ref,
        kept_up_ref,
        sent_up_ref,
        *down_refs,
        cot_ref,
        n_ref,
        act_ref,
        dhidden_ref,
        mid_ref,
        y_ref,
        dnormed_ref,
        bias_ref,
        beside_ref,
        down_ref,
        pad_ref,
    ) = refs[sizes.strips :]
    places = [sizes.place(strip) for strip in range(sizes.strips)]
    gain, shift = row_of(gain_ref, 1), row_of(shift_ref, 1)

    @first_step
    def middle():
        bias_ref[...] = vector_of(bias_up_ref)
        dnormed_ref[...] = jnp.zeros_like(dnormed_ref)
        for place, cot_here in zip(places, cot_refs):
            mid = x_ref[place, :] + dot(mixed_ref[place, :], w_out_ref[...], NN) + row_of(bias_out_ref, 0)
            mid_ref[place, :] = mid
            normed, _, _ = norm(mid, gain, shift)
            n_ref[place, :] = low(normed)
            y_ref[place, :] = mid + row_of(bias_out_ref, 1)
            cot_ref[place, :] = low(padded_rows(cot_here, pad_ref))

    chunk = w_up_ref.shape[1]
    bias = bias_ref[:, pl.ds(pl.multiple_of(pl.program_id(0) * chunk, GROUP), chunk)]
    hidden = [dot(n_ref[place, :], w_up_ref[...], NN) + bias for place in places]
    dact = [dot(cot_ref[place, :], w_down_ref[...], NT) for place in places]
    up_sums = jnp.zeros((1, chunk), jnp.float32)
    for place, values, grads in zip(places, hidden, dact):
        act, slope = gelu_parts(values)
        act = low(act)
        act_ref[place, :] = act
        y_ref[place, :] += dot(act, w_down_ref[...], NN)
        dhidden = low(grads * slope)
        dhidden_ref[place, :] = dhidden
        up_sums = up_sums + col_sum(dhidden.astype(jnp.float32))
        dnormed_ref[place, :] += dot(dhidden, w_up_ref[...], NT)
    up_sums_ref[0:1, :] = up_sums
    step, width = pl.program_id(0), n_ref.shape[1]
    beside_ref[:, pl.ds(pl.multiple_of(step * chunk, GROUP), chunk)] = low(
        dot(n_ref[...], dhidden_ref[...], TN)
    )
    down = dot(act_ref[...], cot_ref[...], TN)
    if folds:
        down = down.reshape(-1, folds, share, width)
        here = chunk // folds
        rows = pl.ds(pl.multiple_of(step * here, share), here)
        for fold in range(folds):
            start = (folds + 1 + fold) * width
            beside_ref[rows, start : start + width] = low(down[:, fold].reshape(here, width))
    else:
        down_ref[pl.ds(pl.multiple_of(step * chunk, GROUP), chunk), :] = low(down)

    @last_step
    def finish():
        totals = []
        for place in places:
            store_halves(info_ref, kept_ref.at[place], sent_ref.at[place], y_ref[place, :])
            _, unit, inverse = norm(mid_ref[place, :], gain, shift)
            grad = cot_ref[place, :].astype(jnp.float32)
            dnormed = dnormed_ref[place, :]
            gb = low(grad + norm_back(dnormed, unit, inverse, gain))
            gb_ref[place, :] = gb
            dmixed_ref[place, :] = low(dot(gb, w_out_ref[...], NT))
            totals.append(
                (
                    col_sum(dnormed * unit),
                    col_sum(dnormed),
                    col_sum(gb.astype(jnp.float32)),
                    col_sum(grad),
                )
            )
        set_rows(sums_ref, [sum(rows) for rows in zip(*totals)])
        beside_ref[:, units : units + width] = low(dot(mixed_ref[...], gb_ref[...], TN))
        for kept, sent, whole_ref in zip(
            (kept_up_ref, *down_refs[:1]), (sent_up_ref, *down_refs[1:]), (beside_ref, down_ref)
        ):
            half = kept.shape[0]
            kept[...] = whole_ref[pl.ds(pl.multiple_of(info_ref[0] * half, 16), half), :]
            sent[...] = whole_ref[pl.ds(pl.multiple_of((1 - info_ref[0]) * half, 16), half), :]


def decoder_ff_call(
    sizes, info, x, mixed, cot, gains, shifts, w_out, bias_out, w_up, bias_up, w_down, share
):
    rows, width = x.shape
    units = w_up.shape[1]
    chunk = units // 4
    all_rows = sizes.all(width)
    half = sds((rows, width // 2))
    up_sums = pl.BlockSpec((8, chunk), lambda i, info: (0, i))
    folds = units // width if share % 8 == 0 else 0
    beside = units + width + (units if folds else 0)
    halves = [(width // 2, beside)] * 2 + ([] if folds else [(units // 2, width)] * 2)
    return call(
        functools.partial(decoder_ff_kernel, sizes=sizes, folds=folds, share=share, units=units),
        (
            half,
            half,
            sds((rows, width)),
            sds((rows, width)),
            sds((8, width), jnp.float32),
            sds((8, units), jnp.float32),
            *[sds(shape) for shape in halves],
        ),
        (4,),
        sizes.raw(width)
        + [all_rows, all_rows]
        + [whole(w) for w in (gains, shifts, w_out, bias_out)]
        + [
            pl.BlockSpec((width, chunk), lambda i, info: (0, i)),
            whole(bias_up),
            pl.BlockSpec((chunk, width), lambda i, info: (i, 0)),
        ],
        (
            sizes.all(width // 2),
            sizes.all(width // 2),
            all_rows,
            all_rows,
            sizes.sums(width),
            up_sums,
            *[pl.BlockSpec(shape, lambda i, info: (0, 0)) for shape in halves],
        ),
        2 * rows * width * (3 * width + 6 * units),
        rows * width * 16 + 4 * width * (width + 2 * units),
        exps=rows * units,
        name="decoder_feed_forward",
        scratch=[
            pltpu.VMEM((rows, width), jnp.bfloat16),
            pltpu.VMEM((rows, width), jnp.bfloat16),
            pltpu.VMEM((rows, chunk), jnp.bfloat16),
            pltpu.VMEM((rows, chunk), jnp.bfloat16),
            pltpu.VMEM((rows, width), jnp.float32),
            pltpu.VMEM((rows, width), jnp.float32),
            pltpu.VMEM((rows, width), jnp.float32),
            pltpu.VMEM((1, units), jnp.float32),
            pltpu.VMEM((width, beside), jnp.bfloat16),
            pltpu.VMEM((16 if folds else units, width), jnp.bfloat16),
            pltpu.VMEM((sizes.padded, width), jnp.float32),
        ],
    )(info, *[cot] * sizes.strips, x, mixed, gains, shifts, w_out, bias_out, w_up, bias_up, w_down)


def encoder_ff_back_kernel(
    info_ref,
    grad_ref,
    mid_ref,
    slope_ref,
    gain_ref,
    shift_ref,
    w_out_ref,
    w_up_ref,
    w_down_ref,
    dhidden_ref,
    gb_ref,
    dmixed_ref,
    sums_ref,
    up_sums_ref,
    dnormed_ref,
    *,
    sizes
):
    places = [sizes.place(strip) for strip in range(sizes.strips)]

    @first_step
    def begin():
        dnormed_ref[...] = jnp.zeros_like(dnormed_ref)

    dact = [dot(grad_ref[place, :], w_down_ref[...], NT) for place in places]
    up_sums = jnp.zeros((1, w_up_ref.shape[1]), jnp.float32)
    for place, values in zip(places, dact):
        dhidden = low(values * slope_ref[place, :].astype(jnp.float32))
        dhidden_ref[place, :] = dhidden
        up_sums = up_sums + col_sum(dhidden.astype(jnp.float32))
        dnormed_ref[place, :] += dot(dhidden, w_up_ref[...], NT)
    up_sums_ref[0:1, :] = up_sums

    @last_step
    def finish():
        gain, shift = row_of(gain_ref, 1), row_of(shift_ref, 1)
        totals = []
        for place in places:
            _, unit, inverse = norm(mid_ref[place, :].astype(jnp.float32), gain, shift)
            grad = grad_ref[place, :].astype(jnp.float32)
            dnormed = dnormed_ref[place, :]
            gb = low(grad + norm_back(dnormed, unit, inverse, gain))
            gb_ref[place, :] = gb
            dmixed_ref[place, :] = low(dot(gb, w_out_ref[...], NT))
            totals.append(
                (
                    col_sum(dnormed * unit),
                    col_sum(dnormed),
                    col_sum(gb.astype(jnp.float32)),
                    col_sum(grad),
                )
            )
        set_rows(sums_ref, [sum(rows) for rows in zip(*totals)])


def encoder_ff_back_call(sizes, info, grad, mid, slope, gains, shifts, w_out, w_up, w_down, after):
    rows, width = grad.shape
    units = w_up.shape[1]
    chunk = units // 4
    all_rows, cols = sizes.all(width), sizes.cols(chunk)
    return call(
        functools.partial(encoder_ff_back_kernel, sizes=sizes),
        (
            sds((rows, units)),
            sds((rows, width)),
            sds((rows, width)),
            sds((8, width), jnp.float32),
            sds((8, units), jnp.float32),
        ),
        (4,),
        [all_rows, all_rows, cols, whole(gains), whole(shifts), whole(w_out)]
        + [
            pl.BlockSpec((width, chunk), lambda i, info: (0, i)),
            pl.BlockSpec((chunk, width), lambda i, info: (i, 0)),
        ],
        (
            cols,
            all_rows,
            all_rows,
            sizes.sums(width),
            pl.BlockSpec((8, chunk), lambda i, info: (0, i)),
        ),
        2 * rows * width * (width + 2 * units),
        rows * (width * 16 + units * 4) + 2 * width * (width + 2 * units),
        after=after,
        name="encoder_feed_forward_back",
        scratch=[pltpu.VMEM((rows, width), jnp.float32)],
    )(info, grad, mid, slope, gains, shifts, w_out, w_up, w_down)


def packed_back(grad_ref, w_ref):
    width = w_ref.shape[0]
    return sum(dot(grad_ref[j], w_ref[:, j * width : (j + 1) * width], NT) for j in range(3))


def decoder_back_kernel(
    info_ref,
    dpacked_ref,
    gm_ref,
    x_ref,
    source_ref,
    y_ref,
    encoded_ref,
    gain_ref,
    shift_ref,
    w_ref,
    w_proj_ref,
    enc_gain_ref,
    enc_shift_ref,
    grad_ref,
    sums_ref,
    enc_sums_ref,
    kept_ref,
    sent_ref,
    total_ref,
):
    dnormed = packed_back(dpacked_ref, w_ref)
    gain = row_of(gain_ref, 0)
    _, unit, inverse = norm(x_ref[...], gain, row_of(shift_ref, 0))
    dx = gm_ref[...].astype(jnp.float32) + norm_back(dnormed, unit, inverse, gain)
    picker = picker_of(source_ref, info_ref[STRIP + pl.program_id(0)])
    taken = dot(picker, low(dx), NN)
    last = taken.shape[0] - 1
    dproj = low(jnp.where(last_row(taken.shape[0]), 0.0, taken))
    term = dot(encoded_ref[...], dproj, TN)
    half = kept_ref.shape[0]

    @pl.when(pl.program_id(0) == 0)
    def begin():
        total_ref[...] = term

    @pl.when(pl.program_id(0) > 0)
    def more():
        total_ref[...] += term

    @pl.when(pl.program_id(0) == pl.num_programs(0) - 1)
    def finish():
        kept_ref[...] = low(total_ref[pl.ds(pl.multiple_of(info_ref[0] * half, 8), half), :])
        sent_ref[...] = low(total_ref[pl.ds(pl.multiple_of((1 - info_ref[0]) * half, 8), half), :])

    dencoded = low(dot(dproj, w_proj_ref[...], NT)).astype(jnp.float32)
    enc_gain = row_of(enc_gain_ref, 2)
    _, unit_final, inverse_final = norm(
        y_ref[...].astype(jnp.float32), enc_gain, row_of(enc_shift_ref, 2)
    )
    grad_ref[...] = low(norm_back(dencoded, unit_final, inverse_final, enc_gain))
    add_rows(
        sums_ref,
        (
            col_sum(dnormed * unit),
            col_sum(dnormed),
            taken[last : last + 1],
            col_sum(dproj.astype(jnp.float32)),
        ),
    )
    add_rows(enc_sums_ref, (col_sum(dencoded * unit_final), col_sum(dencoded)))


def decoder_back_call(
    sizes,
    info,
    dpacked,
    gm,
    x,
    source,
    y,
    encoded,
    gains,
    shifts,
    w_qkv,
    w_proj,
    enc_gains,
    enc_shifts,
    after,
):
    strips, padded, rows = sizes.strips, sizes.padded, sizes.rows
    width = x.shape[2]
    wide = y.shape[2]
    weights = (gains, shifts, w_qkv, w_proj, enc_gains, enc_shifts)
    strip = sizes.strip
    return call(
        decoder_back_kernel,
        (
            sds((strips, padded, wide)),
            sds((8, width), jnp.float32),
            sds((8, wide), jnp.float32),
            sds((wide // 2, width)),
            sds((wide // 2, width)),
        ),
        (strips, 1),
        [
            pl.BlockSpec((3, None, padded, width), lambda s, i, info: (0, s, 0, 0)),
            strip(width),
            strip(width),
            whole(source),
            strip(wide),
            strip(wide),
        ]
        + [whole(w) for w in weights],
        (
            strip(wide),
            sizes.sums(width),
            sizes.sums(wide),
            pl.BlockSpec((wide // 2, width), lambda s, i, info: (0, 0)),
            pl.BlockSpec((wide // 2, width), lambda s, i, info: (0, 0)),
        ),
        2 * rows * width * (3 * width + padded + 2 * wide),
        rows * (width * 16 + wide * 8) + 2 * width * (3 * width + wide),
        after=after,
        name="decoder_packed_back",
        scratch=[pltpu.VMEM((wide, width), jnp.float32)],
    )(info, dpacked, gm, x, source, y, encoded, *weights)


def encoder_back_kernel(info_ref, *refs, parts):
    grad_refs, w_refs = refs[:parts], refs[parts : 2 * parts]
    gb_ref, x_ref, gain_ref, shift_ref, kept_ref, sent_ref, *rest = refs[2 * parts :]
    dnormed_ref, pad_ref = rest[-2:]
    term = sum(dot(grad_ref[...], w_ref[...], NT) for grad_ref, w_ref in zip(grad_refs, w_refs))

    @first_step
    def begin():
        dnormed_ref[...] = term

    @pl.when(pl.program_id(0) > 0)
    def more():
        dnormed_ref[...] += term

    @last_step
    def finish():
        dnormed = dnormed_ref[...]
        gain = row_of(gain_ref, 0)
        _, unit, inverse = norm(padded_rows(x_ref, pad_ref), gain, row_of(shift_ref, 0))
        dx = gb_ref[...].astype(jnp.float32) + norm_back(dnormed, unit, inverse, gain)
        store_halves(info_ref, kept_ref, sent_ref, dx)
        set_rows(rest[0], (col_sum(dnormed * unit), col_sum(dnormed)))


def encoder_back_call(sizes, info, dpacked, gb, x, gains, shifts, w_qkv, strip, after):
    rows, width = gb.shape
    padded = sizes.padded
    half = sds((1, sizes.length, width // 2))
    parts = len(dpacked)
    here = width // parts
    half_spec = pl.BlockSpec((None, sizes.length, width // 2), lambda j, info: (0, 0, 0))
    return call(
        functools.partial(encoder_back_kernel, parts=parts),
        (half, half, sds((8, width), jnp.float32)),
        (3,),
        [pl.BlockSpec((None, None, padded, here), lambda j, info: (j, strip, 0, 0))] * parts
        + [
            pl.BlockSpec((width, here), lambda j, info, part=part: (0, j * parts + part))
            for part in range(parts)
        ]
        + [
            pl.BlockSpec((padded, width), lambda j, info: (strip, 0)),
            sizes.raw(width)[strip],
            whole(gains),
            whole(shifts),
        ],
        (half_spec, half_spec, sizes.sums(width)),
        6 * rows * width * width // sizes.strips,
        rows * width * 12 // sizes.strips + 6 * width * width,
        after=after,
        name=f"encoder_packed_back_{strip}",
        scratch=[pltpu.VMEM((padded, width), jnp.float32)] * 2,
    )(info, *dpacked, *[w_qkv] * parts, gb, x, gains, shifts)


class Job:
    def __init__(self, left, right, row_step, col_step, offset):
        self.half = left.shape[1] // 2
        self.width = right.shape[1]
        self.rows = left.shape[0]
        self.row_step, self.col_step, self.offset = row_step, col_step, offset
        self.down = self.half // row_step
        self.across = self.width // col_step
        self.count = self.down * self.across

    def at(self, step):
        here = jnp.clip(step - self.offset, 0, self.count - 1)
        if self.across == 1:
            return here, 0
        if self.down == 1:
            return 0, here
        return here // self.across, here % self.across

    def left(self, pick):
        return pl.BlockSpec(
            (self.rows, self.row_step),
            lambda step, info: (0, pick(info[0]) * self.down + self.at(step)[0]),
        )

    def right(self):
        return pl.BlockSpec((self.rows, self.col_step), lambda step, info: (0, self.at(step)[1]))

    def out(self):
        return pl.BlockSpec((self.row_step, self.col_step), lambda step, info: self.at(step))


def product_kernel(info_ref, *refs, jobs):
    step = pl.program_id(0)
    out = 3 * len(jobs)
    for place, (offset, count) in enumerate(jobs):
        mine_ref, other_ref, right_ref = refs[3 * place : 3 * place + 3]
        kept_ref, sent_ref = refs[out + 2 * place : out + 2 * place + 2]

        @pl.when((step >= offset) & (step < offset + count))
        def product():
            right = right_ref[...]
            sent_ref[...] = low(dot(other_ref[...], right, TN))
            kept_ref[...] = low(dot(mine_ref[...], right, TN))


def product_call(info, products, name, after=()):
    jobs, operands, in_specs, out_specs, out_shape = [], [], [], [], []
    offset = flops = moved = 0
    for left, right, row_step, col_step in products:
        job = Job(left, right, row_step, col_step, offset)
        offset += job.count
        jobs.append(job)
        operands += [left, left, right]
        in_specs += [job.left(lambda own: own), job.left(lambda own: 1 - own), job.right()]
        out_specs += [job.out(), job.out()]
        out_shape += [sds((job.half, job.width))] * 2
        flops += 4 * job.rows * job.half * job.width
        moved += 2 * job.rows * (2 * job.half + job.width) + 4 * job.half * job.width
    outs = call(
        functools.partial(product_kernel, jobs=[(job.offset, job.count) for job in jobs]),
        tuple(out_shape),
        (offset,),
        in_specs,
        tuple(out_specs),
        flops,
        moved,
        after=after,
        name=name,
    )(info, *operands)
    return [outs[2 * place : 2 * place + 2] for place in range(len(jobs))]


class Chain:
    def __init__(self, pairs, order, parts):
        self.pairs = pairs
        self.bits = list(range(pairs.bit_length() - 1))
        self.order = [bit for bit in order if bit < len(self.bits)]
        self.order += [bit for bit in self.bits if bit not in self.order]
        self.parts, self.widths = [], []
        for kept, arrived in parts:
            width = kept.shape[1]
            self.widths.append(width)
            self.parts.append(tuple(array.reshape(pairs, -1, width) for array in (kept, arrived)))
        self.done = None

    def item(self):
        kept = self.parts[0][0]
        if not self.order:
            return ("last", self.parts, self.widths, None)
        bit = self.order[0]
        lower = sum(1 for other in self.bits if other < bit)
        return ("halve", self.parts, (kept.shape[0] >> (lower + 1), 1 << lower), bit)

    def take(self, outs):
        if not self.order:
            self.done = outs
            return []
        bit = self.order.pop(0)
        self.bits.remove(bit)
        kept, sent = outs
        route = [(place, place ^ (1 << bit)) for place in range(self.pairs)]
        self.parts = [(kept, lax.ppermute(sent, "dp", route))]
        return [sent]


class Total:
    def __init__(self, pairs, values):
        self.pairs = pairs
        bits = [1 << bit for bit in range((2 * pairs).bit_length() - 1)]
        self.left = [bits[-1:]] + [bits[place : place + 2] for place in range(0, len(bits) - 1, 2)]
        self.done = None
        self.launch(values)

    def launch(self, values):
        group = self.left.pop(0)
        masks = group + [sum(group)] if len(group) > 1 else group
        count = 2 * self.pairs
        arrived = [
            lax.ppermute(values, ("section", "dp"), [(place, place ^ mask) for place in range(count)])
            for mask in masks
        ]
        self.parts = [(values, *arrived)]
        self.sent = values

    def item(self):
        return ("add", self.parts, None, None)

    def take(self, outs):
        (values,) = outs
        if not self.left:
            self.done = values
            return []
        self.launch(values)
        return [values]


def in_thirds(kind, parts):
    return kind == "halve" and len(parts) == 1 and parts[0][0].shape[-1] % (3 * GROUP) == 0


def round_kernel(info_ref, *refs, items):
    place = 0
    out = sum(sum(widths) for _, widths, _, _, _, _ in items)
    for kind, widths, how, bit, count, split in items:
        pairs = []
        for width in widths:
            pairs.append(refs[place : place + width])
            place += width
        outs = refs[out : out + count]
        out += count
        run = functools.partial(round_item, info_ref, kind, pairs, how, bit, outs)
        if split:
            run()
        else:
            first_step(run)


def round_item(info_ref, kind, pairs, how, bit, outs):
    if kind == "add":
        outs[0][...] = sum(ref[...] for ref in pairs[0])
        return

    def total(pair, index):
        return pair[0][index].astype(jnp.float32) + pair[1][index].astype(jnp.float32)

    if kind == "last":
        start = 0
        values = [total(pair, 0) for pair in pairs]
        whole_row = values[0] if len(values) == 1 else jnp.concatenate(values, axis=1)
        for ref, width in zip(outs, how):
            ref[...] = whole_row[:, start : start + width]
            start += width
        return
    high, lower = how
    mine = (info_ref[BLOCK] >> bit) & 1
    for h in range(high):
        for l in range(lower):
            start = 0
            for pair in pairs:
                width = pair[0].shape[-1]
                for ref, chosen in zip(outs, (mine, 1 - mine)):
                    index = (h * 2 + chosen) * lower + l
                    ref[h * lower + l, :, start : start + width] = pair[0][index] + pair[1][index]
                start += width


def round_call(info, chains, name, after=(), through=()):
    items = [chain.item() for chain in chains]
    operands, specs, out_shape, out_specs, plain, counts, moved = [], [], [], [], [], [], 0
    for kind, parts, how, bit in items:
        split = in_thirds(kind, parts)
        for part in parts:
            operands += part
            moved += len(part) * part[0].size * part[0].dtype.itemsize
            if split:
                block = (*part[0].shape[:-1], part[0].shape[-1] // 3)
                specs += [pl.BlockSpec(block, lambda i, info: (0, 0, i))] * len(part)
            else:
                specs += [whole(array) for array in part]
        shape = parts[0][0].shape
        if kind == "add":
            shapes = [sds(shape, jnp.float32)]
        elif kind == "last":
            shapes = [sds((shape[1], width), jnp.float32) for width in how]
        else:
            width = sum(part[0].shape[-1] for part in parts)
            shapes = [sds((shape[0] // 2, shape[1], width))] * 2
        out_shape += shapes
        if split:
            out_specs += [
                pl.BlockSpec((*shape.shape[:-1], shape.shape[-1] // 3), lambda i, info: (0, 0, i))
                for shape in shapes
            ]
        else:
            out_specs += [whole(shape) for shape in shapes]
        counts.append(len(shapes))
        plain.append((kind, [len(part) for part in parts], how, bit, len(shapes), split))
    outs = call(
        functools.partial(round_kernel, items=plain),
        tuple(out_shape),
        (3 if any(item[-1] for item in plain) else 1,),
        specs,
        tuple(out_specs),
        moved,
        2 * moved,
        after=after,
        through=through,
        name=name,
    )(info, *operands)
    sent, start = [], 0
    for chain, count in zip(chains, counts):
        sent += chain.take(outs[start : start + count])
        start += count
    return sent, outs[start:]


def across(values):
    return lax.ppermute(values, "section", [(0, 1), (1, 0)])


def arrange_kernel(info_ref, *refs, strips):
    *sources, out_ref = refs
    length = out_ref.shape[1]
    holder = info_ref[STRIP + 2 * strips + pl.program_id(0)]
    slot = info_ref[STRIP + 4 * strips + pl.program_id(0)]
    values = None
    for place in range(strips):
        if len(sources) == 2:
            padded = sources[0].shape[0] // strips
            rows = slice(place * padded, (place + 1) * padded)
            kept, arrived = (ref[rows, :] for ref in sources)
        else:
            kept, arrived = sources[place][0], sources[strips + place][0]
        chosen = jnp.where(holder == info_ref[0], kept, arrived)
        values = chosen if values is None else jnp.where(slot == place, chosen, values)
    out_ref[0] = values[:length]


def arrange_call(info, kept, arrived, strips, length, name, after=()):
    half = kept[0].shape[-1]
    return call(
        functools.partial(arrange_kernel, strips=strips),
        sds((2 * strips, length, half)),
        (2 * strips,),
        [whole(array) for array in (*kept, *arrived)],
        pl.BlockSpec((1, length, half), lambda k, info: (k, 0, 0)),
        1,
        strips * length * half * 12,
        name=name,
        after=after,
    )(info, *kept, *arrived)


def gather_small_kernel(
    info_ref, up_enc, up_dec, enc, dec, dec_in, final, *rest
):
    *enc_in, out_ref = rest
    out_ref[...] = jnp.zeros_like(out_ref)
    wide, narrow = enc.shape[1], dec.shape[1]
    out_ref[0:1, : up_enc.shape[1]] = up_enc[0:1, :]
    out_ref[1:2, : up_dec.shape[1]] = up_dec[0:1, :]
    out_ref[2:6, :wide] = enc[0:4, :]
    out_ref[2:6, wide : wide + narrow] = dec[0:4, :]
    out_ref[2:6, wide + narrow : wide + 2 * narrow] = dec_in[0:4, :]
    out_ref[6:8, :wide] = final[0:2, :]
    out_ref[6:8, wide : 2 * wide] = sum(ref[0:2, :] for ref in enc_in)


def gather_small_call(info, values):
    shape = (8, values[0].shape[1])
    return call(
        gather_small_kernel,
        sds(shape, jnp.float32),
        (1,),
        [whole(value) for value in values],
        pl.BlockSpec(shape, lambda i, info: (0, 0)),
        shape[1],
        shape[1] * 64,
        name="small_rows",
    )(info, *values)


def unshuffled(parts):
    return jnp.concatenate(
        [
            part[:, (3 * group + j) * GROUP : (3 * group + j + 1) * GROUP]
            for j in range(3)
            for part in parts
            for group in range(part.shape[1] // (3 * GROUP))
        ],
        axis=1,
    )


def shares_kernel(info_ref, rows_ref, dec_qkv_ref, *refs, parts, wide, narrow, units, dec_units, count):
    block = info_ref[BLOCK]

    def share(first, last, start, width):
        values = rows_ref[first:last, start : start + width]
        part = width // count
        return pltpu.roll(values, width - block * part, 1)[:, :part]

    enc_qkv = [ref[...] for ref in refs[:parts]]
    outs = refs[parts:]
    bias_up_enc = share(0, 1, 0, units)
    bias_up_dec = share(1, 2, 0, dec_units)
    enc = share(2, 6, 0, wide)
    dec = share(2, 6, wide, narrow)
    dec_in = share(2, 6, wide + narrow, narrow)
    final = share(6, 8, 0, wide)
    enc_in = share(6, 8, wide, wide)
    for ref, value in zip(
        outs,
        (
            jnp.concatenate([enc_in[0:1], enc[0:1], final[0:1]], axis=0),
            jnp.concatenate([enc_in[1:2], enc[1:2], final[1:2]], axis=0),
            enc[2:4],
            bias_up_enc,
            dec_in[3:4],
            dec_in[2:3],
            jnp.concatenate([dec_in[0:1], dec[0:1]], axis=0),
            jnp.concatenate([dec_in[1:2], dec[1:2]], axis=0),
            dec[2:4],
            bias_up_dec,
            unshuffled([dec_qkv_ref[...]]),
            unshuffled(enc_qkv),
        ),
    ):
        ref[...] = value


def shares_call(info, rows, dec_qkv, enc_qkv, wide, narrow, units, dec_units, count):
    shapes = [
        (height, width // count)
        for height, width in (
            (3, wide),
            (3, wide),
            (2, wide),
            (1, units),
            (1, narrow),
            (1, narrow),
            (2, narrow),
            (2, narrow),
            (2, narrow),
            (1, dec_units),
        )
    ] + [dec_qkv.shape, (wide // count, 3 * wide)]
    return call(
        functools.partial(
            shares_kernel,
            parts=len(enc_qkv),
            wide=wide,
            narrow=narrow,
            units=units,
            dec_units=dec_units,
            count=count,
        ),
        tuple(sds(shape, jnp.float32) for shape in shapes),
        (1,),
        [whole(array) for array in (rows, dec_qkv, *enc_qkv)],
        tuple(pl.BlockSpec(shape, lambda i, info: (0, 0)) for shape in shapes),
        rows.size,
        rows.size * 4,
        name="shares",
    )(info, rows, dec_qkv, *enc_qkv)


def decoder_shares_kernel(info_ref, rows_ref, up_ref, out_ref, down_ref):
    width = out_ref.shape[1]
    units = up_ref.shape[1]
    share = up_ref.shape[0]
    rows = rows_ref[...]
    up_ref[...] = rows[:, :units]
    out_ref[...] = rows[:, units : units + width]
    for fold in range(units // width):
        start = units + (fold + 1) * width
        down_ref[fold * share : (fold + 1) * share, :] = rows[:, start : start + width]


def decoder_shares_call(info, rows, width, units, after):
    share = rows.shape[0]
    shapes = ((share, units), (share, width), (share * units // width, width))
    return call(
        decoder_shares_kernel,
        tuple(sds(shape, jnp.float32) for shape in shapes),
        (1,),
        [whole(rows)],
        tuple(pl.BlockSpec(shape, lambda i, info: (0, 0)) for shape in shapes),
        rows.size,
        rows.size * 6,
        name="decoder_shares",
        after=after,
    )(info, rows)


def place_table(length_rows, model_width):
    halfway = model_width // 2
    places = np.arange(length_rows, dtype=np.float64)[:, None]
    rates = np.exp(np.arange(halfway, dtype=np.float64) * (-math.log(10000.0) / halfway))[None, :]
    return np.concatenate([np.sin(places * rates), np.cos(places * rates)], axis=1).astype(
        np.float32
    )


def local(
    patches,
    visible,
    source,
    enc_gains,
    enc_shifts,
    enc_qkv,
    enc_out,
    enc_bias_out,
    enc_up,
    enc_bias_up,
    enc_down,
    enc_proj,
    proj_bias,
    mask_token,
    dec_gains,
    dec_shifts,
    dec_qkv,
    dec_out,
    dec_bias_out,
    dec_up,
    dec_bias_up,
    dec_down,
    cotangent,
):
    pairs = lax.axis_size("dp")
    count = 2 * pairs
    length = patches.shape[1]
    wide = patches.shape[2]
    narrow = dec_qkv.shape[0]
    strips = patches.shape[0] // 2
    padded = -(-(length + 1) // ROW_STEP) * ROW_STEP
    sizes = Sizes(strips, length, padded)
    rows = sizes.rows
    info = place_info(visible, strips)
    taken = jnp.pad(source, ((0, 0), (0, padded - length)), constant_values=-1)
    taken = jnp.where(taken < 0, padded - 1, taken)
    places = jnp.asarray(place_table(padded, narrow))
    strip_form = lambda array: array.reshape(strips, padded, array.shape[-1])
    row_form = lambda array: array.reshape(rows, array.shape[-1])

    n1_enc, packed_enc = packed_call(sizes, info, patches, enc_gains, enc_shifts, enc_qkv)
    packed_enc = strip_form(packed_enc)
    enc_live = visible_live(strips)
    mixed_enc, scales_enc = attend_call(
        packed_enc, info, HEADS_ENC, enc_live, "encoder_attention"
    )
    mixed_enc = row_form(mixed_enc)
    mid_enc, n2_enc, act_enc, slope_enc, y_enc, encoded, projected = encoder_ff_call(
        sizes,
        info,
        patches,
        mixed_enc,
        enc_gains,
        enc_shifts,
        enc_out,
        enc_bias_out,
        enc_up,
        enc_bias_up,
        enc_down,
        enc_proj,
        proj_bias,
    )
    x_dec, n1_dec, packed_dec = decoder_in_call(
        sizes, info, projected, taken, mask_token, places, dec_gains, dec_shifts, dec_qkv
    )
    x_dec, n1_dec, packed_dec = map(strip_form, (x_dec, n1_dec, packed_dec))
    dec_live = all_live(length)
    mixed_dec, scales_dec = attend_call(
        packed_dec, info, HEADS_DEC, dec_live, "decoder_attention"
    )
    mixed_dec = row_form(mixed_dec)
    share = narrow // count
    (
        kept_dec,
        sent_dec,
        gb_dec,
        dmixed_dec,
        sums_dec,
        up_sums_dec,
        kept_beside,
        sent_beside,
        *apart,
    ) = decoder_ff_call(
        sizes,
        info,
        row_form(x_dec),
        mixed_dec,
        cotangent,
        dec_gains,
        dec_shifts,
        dec_out,
        dec_bias_out,
        dec_up,
        dec_bias_up,
        dec_down,
        share,
    )
    arrived_beside, arrived_dec = map(across, (sent_beside, sent_dec))
    enc_half = wide // 2
    dpacked_dec, kept_dqkv, sent_dqkv = attend_back_call(
        packed_dec,
        strip_form(dmixed_dec),
        strip_form(mixed_dec),
        scales_dec,
        n1_dec,
        info,
        HEADS_DEC,
        dec_live,
        0,
        1,
        (sent_beside, sent_dec),
        "decoder_attention_back",
    )
    arrived_dqkv = across(sent_dqkv)
    grad_enc, sums_dec_in, sums_final, kept_proj, sent_proj = decoder_back_call(
        sizes,
        info,
        dpacked_dec,
        strip_form(gb_dec),
        x_dec,
        taken,
        strip_form(y_enc),
        strip_form(encoded),
        dec_gains,
        dec_shifts,
        dec_qkv,
        enc_proj,
        enc_gains,
        enc_shifts,
        (sent_dqkv, arrived_dec),
    )
    grad_enc = row_form(grad_enc)
    arrived_proj = across(sent_proj)
    ((kept_edown, sent_edown),) = product_call(
        info, [(act_enc, grad_enc, enc_half, wide)], "grad_enc_down", (sent_proj,)
    )
    grads_dec = Chain(
        pairs, (0, 1, 2, 3), ((kept_beside, arrived_beside), (kept_dqkv, arrived_dqkv))
    )
    sent, (sent_edown,) = round_call(
        info, [grads_dec], "round_1", (kept_edown, arrived_proj), (sent_edown,)
    )
    arrived_edown = across(sent_edown)
    dhid_enc, gb_enc, dmixed_enc, sums_enc, up_sums_enc = encoder_ff_back_call(
        sizes,
        info,
        grad_enc,
        mid_enc,
        slope_enc,
        enc_gains,
        enc_shifts,
        enc_out,
        enc_up,
        enc_down,
        (*sent, sent_edown),
    )
    (kept_eup, sent_eup), (kept_eout, sent_eout) = product_call(
        info,
        [(n2_enc, dhid_enc, enc_half, wide), (mixed_enc, gb_enc, enc_half, wide)],
        "grad_enc_up_out",
        sent,
    )
    down_enc = Chain(pairs, (0, 2, 1, 3), ((kept_edown, arrived_edown),))
    sent, (sent_eup, sent_eout) = round_call(
        info, [down_enc, grads_dec], "round_2", (kept_eout,), (sent_eup, sent_eout)
    )
    arrived_eup, arrived_eout = map(across, (sent_eup, sent_eout))
    up_enc = Chain(pairs, (1, 0, 2, 3), ((kept_eup, arrived_eup),))
    out_enc = Chain(pairs, (0, 1, 2, 3), ((kept_eout, arrived_eout), (kept_proj, arrived_proj)))
    every = [up_enc, down_enc, grads_dec, out_enc]
    active = lambda: [chain for chain in every if chain.done is None]
    after = (*sent, sent_eup, sent_eout)
    number, dpacked_enc, qkv_enc = 3, [], []
    by_y, by_z = (1, 0, 2, 3), (2, 0, 1, 3)
    for part in range(PARTS):
        dpacked, kept, sent_here = attend_back_call(
            packed_enc,
            strip_form(dmixed_enc),
            strip_form(mixed_enc),
            scales_enc,
            strip_form(n1_enc),
            info,
            HEADS_ENC,
            enc_live,
            part,
            PARTS,
            after,
            f"encoder_attention_back_{part}",
        )
        dpacked_enc.append(dpacked)
        before = (dpacked,)
        if part == 0:
            arranged = arrange_call(
                info, [kept_dec], [arrived_dec], strips, length, "decoded_strips", before
            )
            turned = lax.optimization_barrier(jnp.swapaxes(arranged, 0, 1))
            decoded = jnp.swapaxes(turned, 0, 1)
            before = (dpacked, turned)
        sent, (sent_here,) = round_call(info, active(), f"round_{number}", before, (sent_here,))
        chain = Chain(pairs, (by_z, by_y)[part % 2], ((kept, across(sent_here)),))
        number += 1
        qkv_enc.append(chain)
        every.append(chain)
        after = (*sent, sent_here)
    kept_enc, sent_enc, sums_enc_in = [], [], []
    for strip in range(strips):
        kept, sent_here, sums = encoder_back_call(
            sizes, info, dpacked_enc, gb_enc, patches, enc_gains, enc_shifts, enc_qkv, strip, after
        )
        kept_enc.append(kept)
        sums_enc_in.append(sums)
        sent_enc.append(sent_here)
        through = ()
        if strip == strips - 1:
            through = tuple(sent_enc)
            if apart:
                down_dec = Chain(pairs, by_y, ((apart[0], across(apart[1])),))
                every.append(down_dec)
            small = gather_small_call(
                info,
                (
                    up_sums_enc,
                    up_sums_dec,
                    sums_enc,
                    sums_dec,
                    sums_dec_in,
                    sums_final,
                    *sums_enc_in,
                ),
            )
            through += (small,)
        sent, through = round_call(info, active(), f"round_{number}", (sums,), through)
        number += 1
        after = (*sent,)
    *sent_enc, small = through
    arrived_enc = [across(array) for array in sent_enc]
    small = Total(pairs, small)
    every.append(small)
    patch_grad = arrange_call(info, kept_enc, arrived_enc, strips, length, "patch_grad_strips", after)
    after = (patch_grad,)
    if not apart:
        dec_shares = decoder_shares_call(info, grads_dec.done[0], narrow, dec_up.shape[1], after)
        after += (dec_shares[1],)
    while active():
        round_call(info, active(), f"round_{number}", after)
        after = ()
        number += 1
    g_beside, g_dqkv = grads_dec.done
    shares = shares_call(
        info,
        small.done,
        g_dqkv,
        [chain.done[0] for chain in qkv_enc],
        wide,
        narrow,
        enc_up.shape[1],
        dec_up.shape[1],
        count,
    )
    if apart:
        g_dup, g_dout = g_beside[:, : dec_up.shape[1]], g_beside[:, dec_up.shape[1] :]
        (g_ddown,) = down_dec.done
    else:
        g_dup, g_dout, g_ddown = dec_shares
    (g_edown,), (g_eup,) = down_enc.done, up_enc.done
    g_eout, g_proj = out_enc.done
    return (
        decoded,
        patch_grad,
        shares[0],
        shares[1],
        shares[11],
        g_eout,
        shares[2],
        g_eup,
        shares[3].reshape(-1),
        g_edown,
        g_proj,
        shares[4].reshape(-1),
        shares[5].reshape(-1),
        shares[6],
        shares[7],
        shares[10],
        g_dout,
        shares[8],
        g_dup,
        shares[9].reshape(-1),
        g_ddown,
    )


def solution(mesh):
    return jax.shard_map(
        local,
        mesh=mesh,
        in_specs=(
            P("dp", None, None),
            P("dp"),
            P("dp", None),
            P(),
            P(),
            P(),
            P(),
            P(),
            P(),
            P(),
            P(),
            P(),
            P(),
            P(),
            P(),
            P(),
            P(),
            P(),
            P(),
            P(),
            P(),
            P(),
            P("dp", None, None),
        ),
        out_specs=(
            P("dp", None, "section"),
            P("dp", None, "section"),
            P(None, ("section", "dp")),
            P(None, ("section", "dp")),
            P(("section", "dp"), None),
            P(("section", "dp"), None),
            P(None, ("section", "dp")),
            P(("section", "dp"), None),
            P(("section", "dp")),
            P(("section", "dp"), None),
            P(("section", "dp"), None),
            P(("section", "dp")),
            P(("section", "dp")),
            P(None, ("section", "dp")),
            P(None, ("section", "dp")),
            P(("section", "dp"), None),
            P(("section", "dp"), None),
            P(None, ("section", "dp")),
            P(("section", "dp"), None),
            P(("section", "dp")),
            P(("section", "dp"), None),
        ),
        check_vma=False,
    )
```
